32 devices in a mesh: batch: 16 (over z, y, x), seq: 2 (over core).
Axes of the slice: x: 2, y: 2, z: 4, core: 2. Of those that a mesh axis runs over, the one named last changes fastest.
Arguments:
- frames: bfloat16 [32, 128, 1536], P('batch', 'seq'), may hold values from -6 to 6
- prompt: bfloat16 [32, 128, 768], P('batch'), may hold values from -6 to 6
- clip_frames: int32 [32, 4], P('batch'), may hold values from 0 to 128, as said below
- upstream: bfloat16 [32, 128, 1536], P('batch', 'seq'), may hold values from -6 to 6
- first_gain: float32 [1536], P(('batch', 'seq')), may hold values from 0.5 to 1.5
- first_shift: float32 [1536], P(('batch', 'seq')), may hold values from -2 to 2
- self_project: float32 [1536, 4608], P(('batch', 'seq')), may hold values from -0.15625 to 0.15625
- self_output: float32 [1536, 1536], P(('batch', 'seq')), may hold values from -1.25 to 1.25
- second_gain: float32 [1536], P(('batch', 'seq')), may hold values from 0.5 to 1.5
- second_shift: float32 [1536], P(('batch', 'seq')), may hold values from -2 to 2
- cross_query: float32 [1536, 1536], P(('batch', 'seq')), may hold values from -0.15625 to 0.15625
- cross_memory: float32 [768, 3072], P(('batch', 'seq')), may hold values from -0.21875 to 0.21875
- cross_output: float32 [1536, 1536], P(('batch', 'seq')), may hold values from -0.625 to 0.625
- third_gain: float32 [1536], P(('batch', 'seq')), may hold values from 0.5 to 1.5
- third_shift: float32 [1536], P(('batch', 'seq')), may hold values from -2 to 2
- feed_input: float32 [2, 6144, 1536], P(None, ('batch', 'seq')), may hold values from -0.15625 to 0.15625
- feed_lift: float32 [2, 6144], P(None, ('batch', 'seq')), may hold values from -2 to 2
- feed_output: float32 [6144, 1536], P(('batch', 'seq')), may hold values from -0.109375 to 0.109375
- feed_offset: float32 [1536], P(('batch', 'seq')), may hold values from -2 to 2
Outputs:
- layer_output: bfloat16 [32, 128, 1536], P('batch', 'seq')
- frame_grad: float32 [32, 128, 1536], P('batch', 'seq')
- grad_first_gain: float32 [1536], P(('batch', 'seq'))
- grad_first_shift: float32 [1536], P(('batch', 'seq'))
- grad_self_project: float32 [1536, 4608], P(('batch', 'seq'))
- grad_self_output: float32 [1536, 1536], P(('batch', 'seq'))
- grad_second_gain: float32 [1536], P(('batch', 'seq'))
- grad_second_shift: float32 [1536], P(('batch', 'seq'))
- grad_cross_query: float32 [1536, 1536], P(('batch', 'seq'))
- grad_cross_memory: float32 [768, 3072], P(('batch', 'seq'))
- grad_cross_output: float32 [1536, 1536], P(('batch', 'seq'))
- grad_third_gain: float32 [1536], P(('batch', 'seq'))
- grad_third_shift: float32 [1536], P(('batch', 'seq'))
- grad_feed_input: float32 [2, 6144, 1536], P(None, ('batch', 'seq'))
- grad_feed_lift: float32 [2, 6144], P(None, ('batch', 'seq'))
- grad_feed_output: float32 [6144, 1536], P(('batch', 'seq'))
- grad_feed_offset: float32 [1536], P(('batch', 'seq'))
The draws below stay inside these ranges and needn't reach their ends.
Inputs may be any that keep to these rules, and one draw needn't show every extreme that they name: `clip_frames`: each row's clip frame counts sum to 128. Among the 2 rows of one batch device, one row, drawn from the seed, is a single clip of 128 frames followed by empty slots; every other row is cut at 3 frames drawn at random.
All inputs are finite; a program needn't handle non-finite values.
Results may differ from the reference program's by a relative error of at most 0.02.
Values may be sent and summed in bfloat16 or wider, within the bound.
No kernel may reach another device: no remote copies, remote signals or barrier semaphores. Data moves between devices by JAX's collectives and lax.ppermute only.
A program may use at most 384 MiB of HBM per device.

```python
import jax
import jax.numpy as jnp
from jax import lax

D = 1536
HEADS = 24
HEAD_DIM = 64
FF = 6144
CTX_D = 768
CTXLEN = 128
ROWS_DEV = 2
CLIPS = 4
ROW = 128
ROWS = 32


def draw_clip_frames(key, part):
    key = jax.random.fold_in(key, 11)
    cut_key = jax.random.fold_in(key, 1)
    pick_key = jax.random.fold_in(key, 2)
    cuts = jnp.sort(jax.random.randint(cut_key, (ROWS, CLIPS - 1), 1, ROW), axis=1)
    bounds = jnp.concatenate([jnp.zeros((ROWS, 1), jnp.int32), cuts.astype(jnp.int32), jnp.full((ROWS, 1), ROW, jnp.int32)], 1)
    pieces = bounds[:, 1:] - bounds[:, :-1]
    chosen = jax.random.randint(pick_key, (ROWS // ROWS_DEV,), 0, ROWS_DEV)
    row_ids = jnp.arange(ROWS, dtype=jnp.int32)
    single_row = row_ids % ROWS_DEV == jnp.repeat(chosen, ROWS_DEV, total_repeat_length=ROWS)
    single = jnp.concatenate([jnp.full((ROWS, 1), ROW, jnp.int32), jnp.zeros((ROWS, CLIPS - 1), jnp.int32)], 1)
    return jnp.where(single_row[:, None], single, pieces).astype(jnp.int32)


def level_of(stream_key, shape, cuts, least, high):
    def one(axis_at, shards_of):
        heights = jax.random.uniform(jax.random.fold_in(jax.random.fold_in(stream_key, 6), axis_at), (shards_of,), jnp.float32, least / len(cuts), high / len(cuts))
        return jnp.repeat(jnp.exp(heights), shape[axis_at] // shards_of).reshape((-1,) + (1,) * (len(shape) - axis_at - 1))

    factor_of = one(*cuts[0])
    for cut in cuts[1:]:
        factor_of = factor_of * one(*cut)
    return factor_of


def centred(own_key, extent, scale, most, cuts=(), kind=jnp.bfloat16):
    array = jax.random.normal(own_key, extent, jnp.float32) * scale
    if len(cuts) > 0:
        array = level_of(own_key, extent, cuts, -0.22, 0.18) * array
    return jnp.clip(array, min=-most, max=most).astype(kind)


def setup_inputs(seed: int = 0) -> dict:
    arg_keys = jax.random.split(jax.random.key(seed), 20)
    return {
        "frames": centred(arg_keys[0], (ROWS, ROW, D), 1.0, 6.0, ((0, 16), (1, 2))),
        "prompt": centred(arg_keys[1], (ROWS, CTXLEN, CTX_D), 1.0, 6.0, ((0, 16),)),
        "clip_frames": draw_clip_frames(jax.random.fold_in(arg_keys[19], 71), 0),
        "upstream": centred(arg_keys[3], (ROWS, ROW, D), 1.0, 6.0, ((0, 16), (1, 2))),
        "first_gain": jnp.clip(1.0 + 0.1 * jax.random.normal(arg_keys[4], (D,), jnp.float32), 0.5, 1.5),
        "first_shift": centred(arg_keys[5], (D,), 0.3, 2.0, ((0, 32),), jnp.float32),
        "self_project": centred(arg_keys[6], (D, 3 * D), D ** -0.5, 0.15625, ((0, 32),), jnp.float32),
        "self_output": centred(arg_keys[7], (D, D), (D // 64) ** -0.5, 1.25, ((0, 32),), jnp.float32),
        "second_gain": jnp.clip(1.0 + 0.1 * jax.random.normal(arg_keys[8], (D,), jnp.float32), 0.5, 1.5),
        "second_shift": centred(arg_keys[9], (D,), 0.3, 2.0, ((0, 32),), jnp.float32),
        "cross_query": centred(arg_keys[10], (D, D), D ** -0.5, 0.15625, ((0, 32),), jnp.float32),
        "cross_memory": centred(arg_keys[11], (CTX_D, 2 * D), CTX_D ** -0.5, 0.21875, ((0, 32),), jnp.float32),
        "cross_output": centred(arg_keys[12], (D, D), (D // 16) ** -0.5, 0.625, ((0, 32),), jnp.float32),
        "third_gain": jnp.clip(1.0 + 0.1 * jax.random.normal(arg_keys[13], (D,), jnp.float32), 0.5, 1.5),
        "third_shift": centred(arg_keys[14], (D,), 0.3, 2.0, ((0, 32),), jnp.float32),
        "feed_input": centred(arg_keys[15], (2, FF, D), D ** -0.5, 0.15625, ((1, 32),), jnp.float32),
        "feed_lift": centred(arg_keys[16], (2, FF), 0.3, 2.0, ((1, 32),), jnp.float32),
        "feed_output": centred(arg_keys[17], (FF, D), (FF // 2) ** -0.5, 0.109375, ((0, 32),), jnp.float32),
        "feed_offset": centred(arg_keys[18], (D,), 0.3, 2.0, ((0, 32),), jnp.float32),
    }


EPS = 1e-05
NEG = -1e+30
HIGH = lax.Precision.HIGHEST

@jax.custom_vjp
def low(v):
    return lax.optimization_barrier(v.astype(jnp.bfloat16)).astype(jnp.float32)

@jax.custom_vjp
def low_back(v):
    return v

def low_keep(v):
    return (low(v), None)

def low_pass(kept, grad):
    return (grad,)

def back_keep(v):
    return (v, None)

def back_low(kept, grad):
    return (low(grad),)
low.defvjp(low_keep, low_pass)
low_back.defvjp(back_keep, back_low)

def matmul(left, right):
    return jnp.dot(left, right, precision=HIGH)

def normalize(values, gain, shift):
    center = values - lax.optimization_barrier(jnp.mean(values, -1, keepdims=True))
    spread = lax.optimization_barrier(jnp.mean(center * center, -1, keepdims=True))
    return center * lax.rsqrt(spread + EPS) * gain + shift

def clip_tables(lengths, places):
    ends = jnp.cumsum(lengths)
    later = places[:, None] >= ends[None, :]
    ident = lax.optimization_barrier(jnp.sum(later.astype(jnp.int32), 1))
    starts = lax.optimization_barrier(jnp.max(jnp.where(later, ends[None, :], 0), 1))
    return (ident, places - starts)

def turn(values, offsets, sign):
    half = values.shape[-1] // 2
    freq = 10000.0 ** (-jnp.arange(half, dtype=jnp.float32) / half)
    angle = offsets.astype(jnp.float32)[..., None, None] * freq
    cosine = jnp.cos(angle)
    sine = sign * jnp.sin(angle)
    first = values[..., :half]
    second = values[..., half:]
    return jnp.concatenate([first * cosine - second * sine, second * cosine + first * sine], -1)

def row_pass(params, item):
    first_gain, first_shift, self_project, self_output, second_gain, second_shift, cross_query, cross_memory, cross_output, third_gain, third_shift, feed_input, feed_lift, feed_output, feed_offset = params
    inputs, prompt, lengths = item
    scale = HEAD_DIM ** (-0.5)
    ident, offsets = clip_tables(lengths, jnp.arange(ROW, dtype=jnp.int32))
    visible = ident[:, None] == ident[None, :]
    hidden = low(normalize(inputs, first_gain, first_shift))
    triple = low_back(matmul(hidden, self_project)).reshape(ROW, 3, HEADS, HEAD_DIM)
    query = low(turn(triple[:, 0], offsets, 1.0) * scale)
    keys = low(turn(triple[:, 1], offsets, 1.0))
    values = low(triple[:, 2])
    scores = low_back(jnp.einsum('qhd,khd->hqk', query, keys, precision=HIGH))
    weights = low(jax.nn.softmax(jnp.where(visible[None], scores, NEG), -1))
    mixed = jnp.einsum('hqk,khd->qhd', weights, values, precision=HIGH).reshape(ROW, D)
    mixed = low(low_back(mixed))
    after_self = inputs + low_back(matmul(mixed, self_output))
    hidden = low(normalize(after_self, second_gain, second_shift))
    asking = low(low_back(matmul(hidden, cross_query)).reshape(ROW, HEADS, HEAD_DIM) * scale)
    memory = low(low_back(matmul(prompt, cross_memory))).reshape(CTXLEN, 2, HEADS, HEAD_DIM)
    cross_scores = low_back(jnp.einsum('qhd,khd->hqk', asking, memory[:, 0], precision=HIGH))
    cross_weights = low(jax.nn.softmax(cross_scores, -1))
    cross_mixed = jnp.einsum('hqk,khd->qhd', cross_weights, memory[:, 1], precision=HIGH).reshape(ROW, D)
    cross_mixed = low(low_back(cross_mixed))
    after_cross = after_self + low_back(matmul(cross_mixed, cross_output))
    hidden = low(normalize(after_cross, third_gain, third_shift))
    lifted = low_back(jnp.einsum('fd,ghd->fgh', hidden, feed_input, precision=HIGH) + feed_lift)
    middle = low(low_back(lifted[:, 0] * jax.nn.silu(lifted[:, 1])))
    return after_cross + low_back(matmul(middle, feed_output) + feed_offset)

def reference(frames, prompt, clip_frames, upstream, first_gain, first_shift, self_project, self_output, second_gain, second_shift, cross_query, cross_memory, cross_output, third_gain, third_shift, feed_input, feed_lift, feed_output, feed_offset):
    masters = (first_gain, first_shift, self_project, self_output, second_gain, second_shift, cross_query, cross_memory, cross_output, third_gain, third_shift, feed_input, feed_lift, feed_output, feed_offset)
    prompt_wide = prompt.astype(jnp.float32)
    stepper = jax.checkpoint(row_pass)

    def whole(params, inputs):
        rounded = tuple((low(param) for param in params))
        return lax.map(lambda item: stepper(rounded, item), (inputs, prompt_wide, clip_frames))
    result, pull = jax.vjp(whole, masters, frames.astype(jnp.float32))
    grads, frame_grad = pull(upstream.astype(jnp.float32))
    return (result.astype(jnp.bfloat16), frame_grad, grads[0], grads[1], grads[2], grads[3], grads[4], grads[5], grads[6], grads[7], grads[8], grads[9], grads[10], grads[11], grads[12], grads[13], grads[14])
```

```python
import jax
import jax.numpy as jnp
import numpy as np
from jax import lax
from jax.experimental import pallas as pl
from jax.experimental.pallas import tpu as pltpu
from jax.sharding import PartitionSpec as P

HEAD_DIM = 64
EPS = 1e-05
NEG = -1e30
B = "batch"
S = "seq"
AX = (B, S)


def narrow(value):
    return value.astype(jnp.bfloat16)


def widen(value):
    return value.astype(jnp.float32)


def mult(left, right, form):
    return jnp.einsum(form, left, right, preferred_element_type=jnp.float32)


def dot(left, right):
    return lax.dot_general(left, right, (((1,), (0,)), ((), ())), preferred_element_type=jnp.float32)


def dot_t(left, right):
    return lax.dot_general(left, right, (((1,), (1,)), ((), ())), preferred_element_type=jnp.float32)


def tdot(left, right):
    return lax.dot_general(left, right, (((0,), (0,)), ((), ())), preferred_element_type=jnp.float32)


def standardize(values):
    center = values - jnp.mean(values, -1, keepdims=True)
    inverse = lax.rsqrt(jnp.mean(center * center, -1, keepdims=True) + EPS)
    return (center * inverse, inverse)


def norm_back(incoming, normed, inverse, gain):
    scaled = incoming * gain
    inner = (
        scaled
        - jnp.mean(scaled, -1, keepdims=True)
        - normed * jnp.mean(scaled * normed, -1, keepdims=True)
    )
    return (inner * inverse, jnp.sum(incoming * normed, 0), jnp.sum(incoming, 0))


def clip_tables(lengths, places):
    ends = jnp.cumsum(lengths, 1)
    later = places[None, :, None] >= ends[:, None, :]
    ident = jnp.sum(later.astype(jnp.int32), 2)
    starts = jnp.max(jnp.where(later, ends[:, None, :], 0), 2)
    return (ident, places[None, :] - starts)


def turn(values, offsets, sign):
    half = values.shape[-1] // 2
    freq = 10000.0 ** (-jnp.arange(half, dtype=jnp.float32) / half)
    angle = offsets.astype(jnp.float32)[..., None, None] * freq
    cosine = jnp.cos(angle)
    sine = sign * jnp.sin(angle)
    first = values[..., :half]
    second = values[..., half:]
    return jnp.concatenate([first * cosine - second * sine, second * cosine + first * sine], -1)


def softmax_back(probs, prob_grad):
    return probs * (prob_grad - jnp.sum(probs * prob_grad, -1, keepdims=True))


def hop(value, mask):
    count = lax.axis_size(B) * lax.axis_size(S)
    return lax.ppermute(value, AX, [(i, i ^ mask) for i in range(count)])


def masks_of(order):
    masks = [0]
    for mask in order:
        masks = masks + [old ^ mask for old in masks]
    return masks


def gather(value, order):
    for mask in order:
        value = jnp.concatenate([value, hop(value, mask)], 0)
    return value


def scatter_rest(value, order):
    for mask in reversed(order):
        half = value.shape[0] // 2
        sent = value[half:]
        value = widen(value[:half]) + widen(hop(narrow(sent), mask))
    return value


def scatter_made(make, count, order):
    half = count // 2
    got = hop(narrow(make(half, half)), order[-1])
    kept = make(0, half) + widen(got)
    return scatter_rest(kept, order[:-1])


def gather_halves(value, split, masks, seq_masks):
    known = [0]
    for mask in reversed(masks[2:]):
        value = jnp.concatenate([value, hop(value, mask)], 0)
        known = known + [old ^ mask for old in known]
    halves = []
    for columns, (first, last) in (
        (value[:, :split], (masks[0], masks[1])),
        (value[:, split:], (masks[1], masks[0])),
    ):
        columns = jnp.concatenate([columns, hop(columns, first)], 0)
        have = known + [old ^ first for old in known]
        pieces = [(columns, have), (hop(columns, last), [old ^ last for old in have])]
        for mask in seq_masks:
            pieces = pieces + [(hop(piece, mask), [m ^ mask for m in have]) for piece, have in pieces]
        halves.append(pieces)
    return halves


def settle(halves, targets, widths, me):
    pieces = [(h, piece, have) for h in range(2) for piece, have in halves[h]]
    total = sum(len(have) for h, piece, have in pieces if h == 0)
    rows = pieces[0][1].shape[0] // len(pieces[0][2])
    if rows % 16:
        outs = [[] for _ in widths]
        for h in range(2):
            have = sum([have for _, have in halves[h]], [])
            table = np.zeros(total, np.int32)
            table[np.array(have)] = np.arange(total)
            place = jnp.asarray(table)[me ^ jnp.arange(total, dtype=jnp.int32)]
            blocks = jnp.concatenate([piece for piece, _ in halves[h]], 0).reshape(total, rows, -1)
            blocks = jnp.take(blocks, place, axis=0).reshape(total * rows, -1)
            for source, out, _, count in targets[h]:
                outs[out].append(blocks[:, source : source + count])
        return [jnp.concatenate(out, 1) for out in outs]

    def body(me_ref, *refs):
        ins = refs[: len(pieces)]
        outs = refs[len(pieces) : len(pieces) + len(widths)]
        held = refs[len(pieces) + len(widths) : -2]
        in_sems, out_sems = refs[-2:]
        loads = []
        for i in range(len(pieces)):
            load = pltpu.make_async_copy(ins[i], held[i], in_sems.at[i])
            load.start()
            loads.append(load)
        stores = []
        for i, (h, _, have) in enumerate(pieces):
            loads[i].wait()
            for j, mask in enumerate(have):
                start = pl.multiple_of((me_ref[0] ^ mask) * rows, rows)
                for source, out, column, count in targets[h]:
                    store = pltpu.make_async_copy(
                        held[i].at[pl.ds(j * rows, rows), pl.ds(source, count)],
                        outs[out].at[pl.ds(start, rows), pl.ds(column, count)],
                        out_sems.at[len(stores)],
                    )
                    store.start()
                    stores.append(store)
        for store in stores:
            store.wait()

    count = sum(len(have) * len(targets[h]) for h, _, have in pieces)
    size = 2 * sum(piece.size for _, piece, _ in pieces)
    return pl.pallas_call(
        body,
        out_shape=[jax.ShapeDtypeStruct((total * rows, width), jnp.bfloat16) for width in widths],
        in_specs=[pl.BlockSpec(memory_space=pltpu.SMEM)]
        + [pl.BlockSpec(memory_space=pl.ANY)] * len(pieces),
        out_specs=[pl.BlockSpec(memory_space=pl.ANY)] * len(widths),
        scratch_shapes=[pltpu.VMEM(piece.shape, jnp.bfloat16) for _, piece, _ in pieces]
        + [pltpu.SemaphoreType.DMA((len(pieces),)), pltpu.SemaphoreType.DMA((count,))],
        compiler_params=pltpu.CompilerParams(vmem_limit_bytes=size + (4 << 20)),
        cost_estimate=pl.CostEstimate(flops=0, bytes_accessed=2 * size, transcendentals=0),
    )(me.reshape(1), *[piece for _, piece, _ in pieces])


def scatter_weight(turned, grads, masks, seq_masks):
    size = turned.shape[1]
    value = None
    for mask in reversed(seq_masks):
        half = size // 2
        if value is None:
            sent = narrow(tdot(turned[:, half:], grads))
            kept = narrow(tdot(turned[:, :half], grads))
        else:
            sent, kept = value[half:], value[:half]
        value = narrow(widen(kept) + widen(hop(sent, mask)))
        size = half
    width = value.shape[1]
    value = value.reshape(2, 2, -1, width)
    split = width // 2
    left, right = value[..., :split], value[..., split:]
    left = narrow(widen(left[0]) + widen(hop(left[1], masks[1])))
    right = narrow(widen(right[:, 0]) + widen(hop(right[:, 1], masks[0])))
    left = widen(left[0]) + widen(hop(left[1], masks[0]))
    right = widen(right[0]) + widen(hop(right[1], masks[1]))
    value = narrow(jnp.concatenate([left, right], 1))
    for mask in masks[2:]:
        half = value.shape[0] // 2
        value = widen(value[:half]) + widen(hop(narrow(value[half:]), mask))
    return value


def order_matrix(size, order, me):
    masks = jnp.asarray(np.array(masks_of(order), np.int32))
    rows = size // masks.shape[0]
    source = ((me ^ masks)[:, None] * rows + jnp.arange(rows, dtype=jnp.int32)[None, :]).reshape(-1)
    return (jnp.arange(size, dtype=jnp.int32)[:, None] == source[None, :]).astype(jnp.bfloat16)


def local(
    frames,
    prompt,
    clip_frames,
    upstream,
    first_gain,
    first_shift,
    self_project,
    self_output,
    second_gain,
    second_shift,
    cross_query,
    cross_memory,
    cross_output,
    third_gain,
    third_shift,
    feed_input,
    feed_lift,
    feed_output,
    feed_offset,
):
    row_count, frame_count, width = frames.shape
    heads = width // HEAD_DIM
    token_count = row_count * frame_count
    scale = HEAD_DIM ** (-0.5)
    batch_count = lax.axis_size(B)
    seq_count = lax.axis_size(S)
    device_count = batch_count * seq_count
    seq_place = lax.axis_index(S)
    me = lax.axis_index(B) * seq_count + seq_place
    row_length = frame_count * seq_count
    memory_count = prompt.shape[1]
    memory_share = memory_count // seq_count
    share = first_gain.shape[0]

    seq_masks = [1 << i for i in range(seq_count.bit_length() - 1)]
    batch_masks = [seq_count << i for i in range(batch_count.bit_length() - 1)]
    order = batch_masks[:1:-1] + batch_masks[:2] + seq_masks
    near = batch_masks[:3]
    far = batch_masks[3:]
    token_orders = [near[j:] + near[:j] + seq_masks for j in range(3)]
    third = (token_count * 3 // 8) // 16 * 16
    cuts = [0, third, 2 * third, token_count]

    vectors = [first_gain, first_shift, second_gain, second_shift, third_gain, third_shift, feed_offset]
    vectors = jnp.pad(jnp.stack(vectors, 1), ((0, 0), (0, 128 - len(vectors))))
    split = 3 * width // 2
    halves = gather_halves(
        narrow(jnp.concatenate([vectors, self_project], 1)), 128 + split, batch_masks, seq_masks
    )
    packed, triple_low = settle(
        halves, [[(0, 0, 0, 128), (128, 1, 0, split)], [(0, 1, split, split)]], [128, 3 * width], me
    )
    gain_one, shift_one, gain_two, shift_two, gain_three, shift_three, drop_bias = widen(
        jnp.transpose(packed[:, :7])
    )
    memory_rows = jnp.concatenate([cross_memory[:, :width], cross_memory[:, width:]], 0)
    memory_rows = jnp.pad(memory_rows, ((0, share - memory_rows.shape[0]), (0, 0)))
    halves = gather_halves(
        narrow(jnp.concatenate([self_output, cross_query, cross_output, memory_rows], 1)),
        2 * width,
        batch_masks,
        seq_masks,
    )
    self_low, ask_low, cross_low, memory_low = settle(
        halves,
        [[(0, 0, 0, width), (width, 1, 0, width)], [(0, 2, 0, width), (width, 3, 0, width)]],
        [width] * 4,
        me,
    )
    memory_low = memory_low.reshape(device_count, share, width)[:, : 2 * cross_memory.shape[0]]
    memory_low = memory_low.reshape(device_count, 2, cross_memory.shape[0], width)
    memory_low = jnp.concatenate(
        [memory_low[:, p].reshape(-1, width) for p in range(2)], 1
    )
    lift_low = narrow(feed_input)
    drop_low = narrow(feed_output)
    lift_bias = feed_lift
    for mask in far:
        lift_low = jnp.concatenate([lift_low, hop(lift_low, mask)], 1)
        drop_low = jnp.concatenate([drop_low, hop(drop_low, mask)], 0)
        lift_bias = jnp.concatenate([lift_bias, hop(lift_bias, mask)], 1)
    unit_count = drop_low.shape[0]
    lift_low = lift_low.reshape(2 * unit_count, width)
    lift_bias = widen(narrow(lift_bias.reshape(2 * unit_count)))

    def gather_tokens(value):
        parts = [gather(value[cuts[p] : cuts[p + 1]], token_orders[p]) for p in range(3)]
        return jnp.concatenate(parts, 0)

    upstream_tokens = upstream.reshape(token_count, width)
    feed_cotangent = gather_tokens(upstream_tokens)

    own_places = seq_place * frame_count + jnp.arange(frame_count, dtype=jnp.int32)
    key_order = masks_of(seq_masks)
    key_places = jnp.concatenate(
        [(seq_place ^ k) * frame_count + jnp.arange(frame_count, dtype=jnp.int32) for k in key_order]
    )
    own_clip, own_offset = clip_tables(clip_frames, own_places)
    key_clip = clip_tables(clip_frames, key_places)[0]
    visible = own_clip[:, None, :, None] == key_clip[:, None, None, :]
    prompt_turned = jnp.concatenate(
        [
            lax.dynamic_slice_in_dim(prompt, (seq_place ^ k) * memory_share, memory_share, 1)
            for k in key_order
        ],
        1,
    )
    prompt_flat = prompt_turned.reshape(-1, prompt.shape[2])

    def split_heads(value):
        return value.reshape(row_count, -1, heads, HEAD_DIM)

    inputs = widen(frames).reshape(token_count, width)
    normed_one, inverse_one = standardize(inputs)
    hidden_one = narrow(normed_one * gain_one + shift_one)
    triple = dot(hidden_one, triple_low)
    query = narrow(turn(split_heads(triple[:, :width]), own_offset, 1.0) * scale)
    own_keys = narrow(turn(split_heads(triple[:, width : 2 * width]), own_offset, 1.0))
    own_values = narrow(triple[:, 2 * width :])
    pairs = jnp.concatenate([own_keys.reshape(token_count, width), own_values], 1)
    pairs = pairs.reshape(1, row_count, frame_count, 2 * width)
    pairs = gather(pairs, seq_masks)
    pairs = jnp.transpose(pairs, (1, 0, 2, 3)).reshape(row_count, row_length, 2, heads, HEAD_DIM)
    all_keys = pairs[:, :, 0]
    all_values = pairs[:, :, 1]
    scores = jnp.where(visible, mult(query, all_keys, "rqhd,rkhd->rhqk"), NEG)
    probs = jax.nn.softmax(scores, -1)
    self_mixed = narrow(mult(narrow(probs), all_values, "rhqk,rkhd->rqhd"))
    self_mixed = self_mixed.reshape(token_count, width)
    after_self = inputs + dot(self_mixed, self_low)
    normed_two, inverse_two = standardize(after_self)
    hidden_two = narrow(normed_two * gain_two + shift_two)
    asking = split_heads(narrow(dot(hidden_two, ask_low) * scale))
    memory = narrow(dot(prompt_flat, memory_low)).reshape(
        row_count, memory_count, 2, heads, HEAD_DIM
    )
    memory_keys = memory[:, :, 0]
    memory_values = memory[:, :, 1]
    cross_probs = jax.nn.softmax(mult(asking, memory_keys, "rqhd,rkhd->rhqk"), -1)
    cross_mixed = narrow(mult(narrow(cross_probs), memory_values, "rhqk,rkhd->rqhd"))
    cross_mixed = cross_mixed.reshape(token_count, width)
    after_cross = after_self + dot(cross_mixed, cross_low)
    normed_three, inverse_three = standardize(after_cross)
    hidden_three = narrow(normed_three * gain_three + shift_three)

    feed_rows = gather_tokens(hidden_three)
    group_count = len(masks_of(token_orders[0]))
    starts = [group_count * cut for cut in cuts]
    middle_grad = widen(narrow(dot_t(feed_cotangent, drop_low)))
    lifted = dot_t(feed_rows, lift_low) + lift_bias
    value_part = lifted[:, :unit_count]
    gate_part = lifted[:, unit_count:]
    sigma = jax.nn.sigmoid(gate_part)
    middle = narrow(value_part * gate_part * sigma)
    lift_grad = narrow(
        jnp.concatenate(
            [
                middle_grad * gate_part * sigma,
                middle_grad * value_part * sigma * (1.0 + gate_part * (1.0 - sigma)),
            ],
            1,
        )
    )

    def scatter_tokens(rows, weight):
        sums = []
        for p in range(3):
            part = rows[starts[p] : starts[p + 1]]
            make = lambda start, size, part=part: dot(part[start : start + size], weight)
            sums.append(scatter_made(make, part.shape[0], token_orders[p]))
        return jnp.concatenate(sums, 0)

    feed_back = scatter_tokens(lift_grad, lift_low)
    feed_term = scatter_tokens(middle, drop_low)
    layer_output = after_cross + feed_term + drop_bias

    def shed_units(make, lift):
        spans = [make(k) for k in range(1 << len(far))]
        for mask in reversed(far):
            half = len(spans) // 2
            got = [hop(span if lift else narrow(span), mask) for span in spans[half:]]
            spans = [a + widen(b) for a, b in zip(spans[:half], got)]
        return spans[0]

    units = feed_output.shape[0]
    wide_grad = lift_grad.reshape(-1, 2, unit_count)

    def lift_rows(k):
        rows = wide_grad[:, :, k * units : (k + 1) * units]
        return tdot(rows.reshape(-1, 2 * units), feed_rows)

    def drop_rows(k):
        return tdot(middle[:, k * units : (k + 1) * units], feed_cotangent)

    def bias_rows(k):
        return jnp.sum(widen(wide_grad[:, :, k * units : (k + 1) * units]), 0)

    grad_lift = shed_units(lift_rows, False).reshape(2, units, width)
    grad_drop = shed_units(drop_rows, False)
    grad_lift_bias = shed_units(bias_rows, True)

    matrix = order_matrix(width, order, me)

    def weight_grad(rows, grads):
        return scatter_weight(narrow(dot(rows, matrix)), grads, batch_masks, seq_masks)

    outer_grad = widen(upstream_tokens)
    grad_drop_bias = jnp.sum(outer_grad, 0)
    back_three, grad_gain_three, grad_shift_three = norm_back(
        feed_back, normed_three, inverse_three, gain_three
    )
    cross_out_grad = outer_grad + back_three
    cross_branch = narrow(cross_out_grad)
    cross_mixed_grad = split_heads(narrow(dot_t(cross_branch, cross_low)))
    grad_cross = weight_grad(cross_mixed, cross_branch)
    cross_score_grad = narrow(
        softmax_back(cross_probs, mult(cross_mixed_grad, memory_values, "rqhd,rkhd->rhqk"))
    )
    asking_grad = narrow(
        (mult(cross_score_grad, memory_keys, "rhqk,rkhd->rqhd") * scale).reshape(token_count, width)
    )
    memory_key_grad = mult(cross_score_grad, asking, "rhqk,rqhd->rkhd")
    memory_value_grad = mult(narrow(cross_probs), cross_mixed_grad, "rhqk,rqhd->rkhd")
    memory_grad = narrow(
        jnp.stack([memory_key_grad, memory_value_grad], 2).reshape(row_count, memory_count, 2 * width)
    )
    back_two, grad_gain_two, grad_shift_two = norm_back(
        dot_t(asking_grad, ask_low), normed_two, inverse_two, gain_two
    )
    grad_ask = weight_grad(hidden_two, asking_grad)

    def shed_frames(value):
        value = value.reshape(row_count, seq_count, -1, value.shape[-1])
        for mask in reversed(seq_masks):
            half = value.shape[1] // 2
            value = widen(value[:, :half]) + widen(hop(narrow(value[:, half:]), mask))
        return value.reshape(-1, value.shape[-1])

    memory_own = narrow(shed_frames(memory_grad))
    prompt_own = prompt_flat.reshape(row_count, memory_count, -1)[:, :memory_share]
    prompt_own = prompt_own.reshape(-1, prompt.shape[2])
    prompt_own = narrow(dot(prompt_own, order_matrix(prompt.shape[2], order, me)))
    grad_memory = scatter_weight(prompt_own, memory_own, batch_masks, seq_masks)
    self_out_grad = cross_out_grad + back_two
    self_branch = narrow(self_out_grad)
    self_mixed_grad = split_heads(narrow(dot_t(self_branch, self_low)))
    grad_self = weight_grad(self_mixed, self_branch)
    score_grad = narrow(softmax_back(probs, mult(self_mixed_grad, all_values, "rqhd,rkhd->rhqk")))
    query_grad = mult(score_grad, all_keys, "rhqk,rkhd->rqhd") * scale
    key_grad = mult(score_grad, query, "rhqk,rqhd->rkhd")
    value_grad = mult(narrow(probs), self_mixed_grad, "rhqk,rqhd->rkhd")
    pair_grad = narrow(
        jnp.stack([key_grad, value_grad], 2).reshape(row_count, row_length, 2 * width)
    )
    own_pair_grad = shed_frames(pair_grad)
    query_back = narrow(turn(query_grad, own_offset, -1.0)).reshape(token_count, width)
    key_back = narrow(turn(split_heads(own_pair_grad[:, :width]), own_offset, -1.0))
    key_back = key_back.reshape(token_count, width)
    value_back = narrow(own_pair_grad[:, width:])
    triple_back = jnp.concatenate([query_back, key_back, value_back], 1)
    back_hidden = dot_t(triple_back, triple_low)
    back_one, grad_gain_one, grad_shift_one = norm_back(
        back_hidden, normed_one, inverse_one, gain_one
    )
    grad_triple = weight_grad(hidden_one, triple_back)
    frame_grad = self_out_grad + back_one

    sums = jnp.stack(
        [
            grad_gain_one,
            grad_shift_one,
            grad_gain_two,
            grad_shift_two,
            grad_gain_three,
            grad_shift_three,
            grad_drop_bias,
        ],
        0,
    ).reshape(7, device_count, share)
    sums = jnp.transpose(sums, (1, 0, 2)).reshape(device_count, 7 * share)
    sums = jnp.pad(sums, ((0, 0), (0, 1024 - 7 * share)))
    sums = jnp.take(sums, me ^ jnp.asarray(np.array(masks_of(order), np.int32)), axis=0)
    sums = sums.reshape(device_count, 8, 128)
    for mask in reversed(order):
        half = sums.shape[0] // 2
        sums = sums[:half] + hop(sums[half:], mask)
    sums = sums.reshape(1024)[: 7 * share].reshape(7, share)

    shape = frames.shape
    return (
        narrow(layer_output).reshape(shape),
        frame_grad.reshape(shape),
        sums[0],
        sums[1],
        grad_triple,
        grad_self,
        sums[2],
        sums[3],
        grad_ask,
        grad_memory,
        grad_cross,
        sums[4],
        sums[5],
        grad_lift,
        grad_lift_bias,
        grad_drop,
        sums[6],
    )


def solution(mesh):
    both = P(AX)
    wide = P(AX, None)
    rows = P(B, S, None)
    units = P(None, AX, None)
    in_specs = (
        rows,
        P(B, None, None),
        P(B, None),
        rows,
        both,
        both,
        wide,
        wide,
        both,
        both,
        wide,
        wide,
        wide,
        both,
        both,
        units,
        P(None, AX),
        wide,
        both,
    )
    out_specs = (
        rows,
        rows,
        both,
        both,
        wide,
        wide,
        both,
        both,
        wide,
        wide,
        wide,
        both,
        both,
        units,
        P(None, AX),
        wide,
        both,
    )
    return jax.shard_map(local, mesh=mesh, in_specs=in_specs, out_specs=out_specs, check_vma=False)
```

```python
import jax
import jax.numpy as jnp
import numpy as np
from jax import lax
from jax.experimental import pallas as pl
from jax.experimental.pallas import tpu as pltpu
from jax.sharding import PartitionSpec as P

HEAD_DIM = 64
LANES = 512
UNITS = ["unit0", "unit1", "unit2", "unit3", "unit4", "unit5"]
EPS = 1e-05
NEG = -1e30
B = "batch"
S = "seq"
AX = (B, S)


def narrow(value):
    return value.astype(jnp.bfloat16)


def widen(value):
    return value.astype(jnp.float32)


def mult(left, right, form):
    return jnp.einsum(form, left, right, preferred_element_type=jnp.float32)


def dot(left, right):
    return lax.dot_general(left, right, (((1,), (0,)), ((), ())), preferred_element_type=jnp.float32)


def dot_t(left, right):
    return lax.dot_general(left, right, (((1,), (1,)), ((), ())), preferred_element_type=jnp.float32)


def tdot(left, right):
    return lax.dot_general(left, right, (((0,), (0,)), ((), ())), preferred_element_type=jnp.float32)


def standardize(values):
    center = values - jnp.mean(values, -1, keepdims=True)
    inverse = lax.rsqrt(jnp.mean(center * center, -1, keepdims=True) + EPS)
    return (center * inverse, inverse)


def norm_back(incoming, normed, inverse, gain):
    scaled = incoming * gain
    inner = (
        scaled
        - jnp.mean(scaled, -1, keepdims=True)
        - normed * jnp.mean(scaled * normed, -1, keepdims=True)
    )
    return (
        inner * inverse,
        jnp.sum(incoming * normed, 0, keepdims=True),
        jnp.sum(incoming, 0, keepdims=True),
    )


def clip_tables(lengths, places):
    ends = jnp.cumsum(lengths, 1)
    later = places[None, :, None] >= ends[:, None, :]
    ident = jnp.sum(later.astype(jnp.int32), 2)
    starts = jnp.max(jnp.where(later, ends[:, None, :], 0), 2)
    return (ident, places[None, :] - starts)


def softmax_back(probs, prob_grad):
    return probs * (prob_grad - jnp.sum(probs * prob_grad, -1, keepdims=True))


def hop(value, mask):
    count = lax.axis_size(B) * lax.axis_size(S)
    return lax.ppermute(value, AX, [(i, i ^ mask) for i in range(count)])


def volley(values, masks):
    values = lax.optimization_barrier(tuple(values))
    return lax.optimization_barrier(tuple(hop(value, mask) for value, mask in zip(values, masks)))


def masks_of(order):
    masks = [0]
    for mask in order:
        masks = masks + [old ^ mask for old in masks]
    return masks


def gather(value, order):
    for mask in order:
        value = jnp.concatenate([value, hop(value, mask)], 0)
    return value


def settle(halves, targets, widths, me):
    pieces = [(h, piece, have) for h in range(2) for piece, have in halves[h]]
    total = sum(len(have) for h, piece, have in pieces if h == 0)
    rows = pieces[0][1].shape[0] // len(pieces[0][2])
    if rows % 16:
        outs = [[] for _ in widths]
        for h in range(2):
            have = sum([have for _, have in halves[h]], [])
            table = np.zeros(total, np.int32)
            table[np.array(have)] = np.arange(total)
            place = jnp.asarray(table)[me ^ jnp.arange(total, dtype=jnp.int32)]
            blocks = jnp.concatenate([piece for piece, _ in halves[h]], 0).reshape(total, rows, -1)
            blocks = jnp.take(blocks, place, axis=0).reshape(total * rows, -1)
            for source, out, _, count in targets[h]:
                outs[out].append(blocks[:, source : source + count])
        return [jnp.concatenate(out, 1) for out in outs]

    def body(me_ref, *refs):
        ins = refs[: len(pieces)]
        outs = refs[len(pieces) : len(pieces) + len(widths)]
        held = refs[len(pieces) + len(widths) : -2]
        in_sems, out_sems = refs[-2:]
        loads = []
        for i in range(len(pieces)):
            load = pltpu.make_async_copy(ins[i], held[i], in_sems.at[i])
            load.start()
            loads.append(load)
        stores = []
        for i, (h, _, have) in enumerate(pieces):
            loads[i].wait()
            for j, mask in enumerate(have):
                start = pl.multiple_of((me_ref[0] ^ mask) * rows, rows)
                for source, out, column, count in targets[h]:
                    store = pltpu.make_async_copy(
                        held[i].at[pl.ds(j * rows, rows), pl.ds(source, count)],
                        outs[out].at[pl.ds(start, rows), pl.ds(column, count)],
                        out_sems.at[len(stores)],
                    )
                    store.start()
                    stores.append(store)
        for store in stores:
            store.wait()

    count = sum(len(have) * len(targets[h]) for h, _, have in pieces)
    size = 2 * sum(piece.size for _, piece, _ in pieces)
    return pl.pallas_call(
        body,
        out_shape=[jax.ShapeDtypeStruct((total * rows, width), jnp.bfloat16) for width in widths],
        in_specs=[pl.BlockSpec(memory_space=pltpu.SMEM)]
        + [pl.BlockSpec(memory_space=pl.ANY)] * len(pieces),
        out_specs=[pl.BlockSpec(memory_space=pl.ANY)] * len(widths),
        scratch_shapes=[pltpu.VMEM(piece.shape, jnp.bfloat16) for _, piece, _ in pieces]
        + [pltpu.SemaphoreType.DMA((len(pieces),)), pltpu.SemaphoreType.DMA((count,))],
        compiler_params=pltpu.CompilerParams(vmem_limit_bytes=size + (4 << 20)),
        cost_estimate=pl.CostEstimate(flops=0, bytes_accessed=size // 16, transcendentals=0),
    )(me.reshape(1), *[piece for _, piece, _ in pieces])


class Traffic:
    def __init__(self):
        self.flows = {}
        self.done = {}

    def turn(self, outs, new=None, step=None):
        names = list(self.flows) if step is None else [n for n in step if n in self.flows]
        gots = sum([self.flows[name][1] for name in names], ())
        tied = lax.optimization_barrier(gots + tuple(outs))
        outs = tied[len(gots) :]
        started = []
        for name in names:
            flow, got = self.flows.pop(name)
            got, tied = tied[: len(got)], tied[len(got) :]
            try:
                started.append((name, flow, flow.send(got)))
            except StopIteration as end:
                self.done[name] = end.value
        if new is not None:
            flows = new(self.done)
            for name, flow in ((name, flow) for name, flow in flows.items() if flow is not None):
                started.append((name, flow, next(flow)))
        sents = sum([sent for _, _, sent in started], ())
        tied = lax.optimization_barrier(sents + outs)
        for name, flow, sent in started:
            self.flows[name] = (flow, flow.send(tied[: len(sent)]))
            tied = tied[len(sent) :]
        return tied


def hops(values, masks):
    return tuple(hop(value, mask) for value, mask in zip(values, masks))


def once(values, masks):
    values = yield tuple(values)
    return (yield hops(values, masks))


def halve_pairs(pairs, orders):
    for step in list(zip(*orders))[::-1]:
        sent = yield tuple(sent for _, sent in pairs)
        got = yield hops(sent, step)
        sums = [(kept, part) for (kept, _), part in zip(pairs, got)]
        pairs = []
        for kept, part in sums:
            half = kept.shape[0] // 2
            pair = [widen(kept[cut]) + widen(part[cut]) for cut in (slice(half), slice(half, None))]
            pairs.append(pair if kept.ndim == 3 else [narrow(item) for item in pair])
    return [widen(kept) + widen(part) for kept, part in sums]


def halve_list_rows(value, masks):
    for mask in reversed(masks):
        half = value.shape[0] // 2
        sent = yield (value[half:],)
        (got,) = yield hops(sent, (mask,))
        value = value[:half] + got
    return value


def halve_list(blocks, masks):
    for mask in reversed(masks):
        half = len(blocks) // 2
        sent = yield tuple(narrow(block) for block in blocks[half:])
        got = yield hops(sent, (mask,) * half)
        blocks = [widen(a) + widen(b) for a, b in zip(blocks[:half], got)]
    return blocks[0]


def halve_rows(blocks, first, last, masks):
    for mask in reversed(masks):
        half = len(blocks) // 2
        sent = yield tuple(narrow(block[first:last]) for block in blocks[half:])
        got = yield hops(sent, (mask,) * half)
        blocks = [widen(a[first:last]) + widen(b) for a, b in zip(blocks[:half], got)]
        first, last = 0, last - first
    return blocks[0]


def double_each(parts, orders):
    for step in zip(*orders):
        parts = yield tuple(parts)
        got = yield hops(parts, step)
        parts = [jnp.concatenate(pair, 0) for pair in zip(parts, got)]
    return jnp.concatenate(parts, 0)


def double_list(value, masks):
    blocks = (value,)
    for mask in masks:
        blocks = yield blocks
        got = yield hops(blocks, (mask,) * len(blocks))
        blocks = tuple(blocks) + tuple(got)
    return blocks


def spin(value, cosine, sine):
    lane = lax.broadcasted_iota(jnp.int32, value.shape, 1)
    other = jnp.where(lane % 64 < 32, pltpu.roll(value, 96, 1), pltpu.roll(value, 32, 1))
    return value * cosine + other * sine


def spin_tables(offsets, sign):
    half = HEAD_DIM // 2
    freq = 10000.0 ** (-jnp.arange(half, dtype=jnp.float32) / half)
    angle = offsets.astype(jnp.float32).reshape(-1, 1) * freq
    cosine = jnp.cos(angle)
    sine = sign * jnp.sin(angle)
    return (jnp.concatenate([cosine] * 4, 1), jnp.concatenate([-sine, sine, -sine, sine], 1))


def hint():
    return pl.CostEstimate(flops=1 << 20, bytes_accessed=1 << 20, transcendentals=0)


def whole(array):
    return pl.BlockSpec(array.shape, lambda i: (0,) * array.ndim)


def like(shape, dtype=jnp.float32):
    return jax.ShapeDtypeStruct(shape, dtype)


BIG = pltpu.CompilerParams(vmem_limit_bytes=44 << 20)


def project(inputs, gain, shift, weight, tables, scale):
    rows, width = inputs.shape
    block = width // 2

    def body(in_ref, gain_ref, shift_ref, cos_ref, sin_ref, weight_ref, *outs):
        query_ref, pair_ref, normed_ref, inverse_ref, hidden_ref = outs
        step = pl.program_id(0)

        @pl.when(step == 0)
        def _():
            normed, inverse = standardize(widen(in_ref[...]))
            normed_ref[...] = normed
            inverse_ref[...] = inverse
            hidden_ref[...] = narrow(normed * gain_ref[...] + shift_ref[...])

        value = dot(hidden_ref[...], weight_ref[...])

        def turned(factor):
            parts = [
                spin(value[:, j : j + 128], cos_ref[...], sin_ref[...]) for j in range(0, block, 128)
            ]
            return [narrow(part * factor) for part in parts]

        @pl.when(step < 2)
        def _():
            for j, part in enumerate(turned(scale)):
                query_ref[:, 128 * j : 128 * j + 128] = part

        @pl.when((step >= 2) & (step < 4))
        def _():
            for j, part in enumerate(turned(1.0)):
                pair_ref[:, 128 * j : 128 * j + 128] = part

        @pl.when(step >= 4)
        def _():
            pair_ref[...] = narrow(value)

    def pair_place(i):
        return (jnp.maximum(i // 2 - 1, 0), jnp.where(i < 2, 0, i % 2))

    return pl.pallas_call(
        body,
        grid=(6,),
        out_shape=[
            like((rows, width), jnp.bfloat16),
            like((2 * rows, width), jnp.bfloat16),
            like((rows, width)),
            like((rows, 1)),
            like((rows, width), jnp.bfloat16),
        ],
        in_specs=[
            whole(inputs),
            whole(gain),
            whole(shift),
            whole(tables[0]),
            whole(tables[1]),
            pl.BlockSpec((width, block), lambda i: (0, i)),
        ],
        out_specs=[
            pl.BlockSpec((rows, block), lambda i: (0, jnp.minimum(i, 1))),
            pl.BlockSpec((rows, block), pair_place),
            pl.BlockSpec((rows, width), lambda i: (0, 0)),
            pl.BlockSpec((rows, 1), lambda i: (0, 0)),
            pl.BlockSpec((rows, width), lambda i: (0, 0)),
        ],
        compiler_params=BIG,
        cost_estimate=hint(),
    )(inputs, gain, shift, *tables, weight)


def ahead(mixed, low, before, gain, shift, ask=None, scale=1.0):
    rows, width = before.shape
    steps = width // LANES

    def body(mixed_ref, before_ref, gain_ref, shift_ref, *refs):
        low_ref, refs = refs[0], refs[1:]
        if ask is not None:
            ask_ref, refs = refs[0], refs[1:]
        sum_ref, normed_ref, inverse_ref, hidden_ref = refs[:4]
        step = pl.program_id(0)

        @pl.when(step < steps)
        def _():
            lanes = pl.ds(pl.multiple_of(step * LANES, LANES), LANES)
            sum_ref[:, lanes] = widen(before_ref[:, lanes]) + dot(mixed_ref[...], low_ref[...])

        @pl.when(step == steps - 1)
        def _():
            normed, inverse = standardize(sum_ref[...])
            normed_ref[...] = normed
            inverse_ref[...] = inverse
            hidden_ref[...] = narrow(normed * gain_ref[...] + shift_ref[...])

        if ask is not None:

            @pl.when(step >= steps)
            def _():
                refs[4][...] = narrow(dot(hidden_ref[...], ask_ref[...]) * scale)

    full = pl.BlockSpec((rows, width), lambda i: (0, 0))
    args = (mixed, before, gain, shift, low)
    specs = [whole(mixed), whole(before), whole(gain), whole(shift)]
    specs.append(pl.BlockSpec((width, LANES), lambda i: (0, jnp.minimum(i, steps - 1))))
    shapes = [
        like((rows, width)),
        like((rows, width)),
        like((rows, 1)),
        like((rows, width), jnp.bfloat16),
    ]
    outs = [full, full, pl.BlockSpec((rows, 1), lambda i: (0, 0)), full]
    if ask is not None:
        args = args + (ask,)
        specs.append(pl.BlockSpec((width, LANES), lambda i: (0, jnp.maximum(i - steps, 0))))
        shapes.append(like((rows, width), jnp.bfloat16))
        outs.append(pl.BlockSpec((rows, LANES), lambda i: (0, jnp.maximum(i - steps, 0))))
    return pl.pallas_call(
        body,
        grid=(steps if ask is None else 2 * steps,),
        out_shape=shapes,
        in_specs=specs,
        out_specs=outs,
        compiler_params=BIG,
        cost_estimate=hint(),
    )(*args)


def back(incoming, low, grads, normed, inverse, gain, out=None):
    rows, width = grads.shape
    block = LANES if low is None or low.shape[1] == width else LANES // 2
    first = 0 if low is None else width // block
    last = 0 if out is None else width // LANES
    norm_step = max(first - 1, 0)

    def body(in_ref, grad_ref, normed_ref, inverse_ref, gain_ref, *refs):
        if low is not None:
            low_ref, refs = refs[0], refs[1:]
        if out is not None:
            out_ref, refs = refs[0], refs[1:]
        sum_ref, gain_grad_ref, shift_grad_ref = refs[:3]
        held_ref = refs[-1]
        step = pl.program_id(0)
        if low is not None:

            @pl.when(step < first)
            def _():
                lanes = pl.ds(pl.multiple_of(step * block, block), block)
                held_ref[:, lanes] = dot_t(in_ref[...], low_ref[...])

        @pl.when(step == norm_step)
        def _():
            value = in_ref[...] if low is None else held_ref[...]
            inner, gain_grad, shift_grad = norm_back(
                value, normed_ref[...], inverse_ref[...], gain_ref[...]
            )
            total = widen(grad_ref[...]) + inner
            sum_ref[...] = total
            gain_grad_ref[...] = gain_grad
            shift_grad_ref[...] = shift_grad
            if out is not None:
                refs[3][...] = narrow(total)

        if out is not None:

            @pl.when(step >= first)
            def _():
                refs[4][...] = narrow(dot_t(refs[3][...], out_ref[...]))

    full = pl.BlockSpec((rows, width), lambda i: (0, 0))
    line = pl.BlockSpec((1, width), lambda i: (0, 0))
    args = (incoming, grads, normed, inverse, gain)
    specs = [whole(array) for array in args]
    if low is not None:
        args = args + (low,)
        specs.append(pl.BlockSpec((block, low.shape[1]), lambda i: (jnp.minimum(i, first - 1), 0)))
    shapes = [like((rows, width)), like((1, width)), like((1, width))]
    outs = [full, line, line]
    if out is not None:
        args = args + (out,)
        specs.append(pl.BlockSpec((LANES, width), lambda i: (jnp.maximum(i - first, 0), 0)))
        shapes = shapes + [like((rows, width), jnp.bfloat16)] * 2
        outs = outs + [full, pl.BlockSpec((rows, LANES), lambda i: (0, jnp.maximum(i - first, 0)))]
    return pl.pallas_call(
        body,
        grid=(first + last,),
        out_shape=shapes,
        in_specs=specs,
        out_specs=outs,
        scratch_shapes=[pltpu.VMEM((rows, width), jnp.float32)],
        compiler_params=BIG,
        cost_estimate=hint(),
    )(*args)


def feed_block(rows, ups, value_low, gate_low, drop_low, value_bias, gate_bias):
    count, width = rows.shape
    units = drop_low.shape[0]
    block = min(count, 256)

    def body(row_ref, up_ref, value_ref, gate_ref, drop_ref, value_bias_ref, gate_bias_ref, *outs):
        middle_ref, value_out, gate_out, back_ref, term_ref = outs
        middle_grad = widen(narrow(dot_t(up_ref[...], drop_ref[...])))
        value = dot_t(row_ref[...], value_ref[...]) + value_bias_ref[...]
        gate = dot_t(row_ref[...], gate_ref[...]) + gate_bias_ref[...]
        sigma = jax.nn.sigmoid(gate)
        middle = narrow(value * gate * sigma)
        value_grad = narrow(middle_grad * gate * sigma)
        gate_grad = narrow(middle_grad * value * sigma * (1.0 + gate * (1.0 - sigma)))
        middle_ref[...] = middle
        value_out[...] = value_grad
        gate_out[...] = gate_grad
        back_ref[...] = narrow(dot(value_grad, value_ref[...]) + dot(gate_grad, gate_ref[...]))
        term_ref[...] = narrow(dot(middle, drop_ref[...]))

    wide = pl.BlockSpec((block, width), lambda i: (i, 0))
    thin = pl.BlockSpec((block, units), lambda i: (i, 0))
    args = (rows, ups, value_low, gate_low, drop_low, value_bias, gate_bias)
    return pl.pallas_call(
        body,
        grid=(count // block,),
        out_shape=[like((count, units), jnp.bfloat16)] * 3 + [like((count, width), jnp.bfloat16)] * 2,
        in_specs=[wide, wide] + [whole(array) for array in args[2:]],
        out_specs=[thin] * 3 + [wide] * 2,
        compiler_params=BIG,
        cost_estimate=hint(),
    )(*args)


def unit_grad(lefts, rights, sums):
    units = lefts[0].shape[1]
    width = rights[0].shape[1]
    count = len(lefts)
    block = 128 if units % 128 == 0 else units

    def body(*refs):
        total = 0.0
        for left, right in zip(refs[:count], refs[count : 2 * count]):
            total = total + tdot(left[...], right[...])
        refs[2 * count][...] = narrow(total)
        if sums:
            refs[2 * count + 1][...] = sum(
                jnp.sum(widen(left[...]), 0, keepdims=True) for left in refs[:count]
            )

    specs = [pl.BlockSpec((left.shape[0], block), lambda i: (0, i)) for left in lefts]
    outs = [pl.BlockSpec((block, width), lambda i: (i, 0))]
    shapes = [like((units, width), jnp.bfloat16)]
    if sums:
        outs.append(pl.BlockSpec((1, block), lambda i: (0, i)))
        shapes.append(like((1, units)))
    return pl.pallas_call(
        body,
        grid=(units // block,),
        out_shape=shapes,
        in_specs=specs + [whole(right) for right in rights],
        out_specs=outs,
        compiler_params=BIG,
        cost_estimate=hint(),
    )(*lefts, *rights)


def spin_backward(query, pairs, got, cosine, sine):
    rows, width = query.shape

    def body(cos_ref, sin_ref, query_ref, own_ref, got_ref, out_ref):
        step = pl.program_id(0)

        @pl.when(step == 0)
        def _():
            out_ref[...] = query_ref[...]

        @pl.when(step == 1)
        def _():
            for j in range(0, width, 128):
                value = widen(own_ref[:, j : j + 128]) + widen(got_ref[:, j : j + 128])
                out_ref[:, j : j + 128] = narrow(spin(value, cos_ref[...], sin_ref[...]))

        @pl.when(step == 2)
        def _():
            out_ref[...] = narrow(widen(own_ref[...]) + widen(got_ref[...]))

    table = pl.BlockSpec((rows, 128), lambda i: (0, 0))
    part = pl.BlockSpec((rows, width), lambda i: (jnp.maximum(i - 1, 0), 0))
    return pl.pallas_call(
        body,
        grid=(3,),
        out_shape=jax.ShapeDtypeStruct((rows, 3 * width), jnp.bfloat16),
        in_specs=[table, table, pl.BlockSpec((rows, width), lambda i: (0, 0)), part, part],
        out_specs=pl.BlockSpec((rows, width), lambda i: (0, i)),
        cost_estimate=pl.CostEstimate(
            flops=24 * query.size, bytes_accessed=16 * query.size, transcendentals=0
        ),
    )(cosine, sine, query, pairs, got)


def two_heads(value):
    lane = lax.broadcasted_iota(jnp.int32, value.shape, 1)
    zero = jnp.zeros_like(value)
    first = jnp.where(lane < HEAD_DIM, value, zero)
    second = jnp.where(lane < HEAD_DIM, zero, value)
    return jnp.concatenate([first, second], 0)


def one_row(value):
    half = value.shape[0] // 2
    lane = lax.broadcasted_iota(jnp.int32, (half, value.shape[1]), 1)
    return jnp.where(lane < HEAD_DIM, value[:half], value[half:])


def row_probs(asked, keys, seen):
    scores = dot_t(asked, keys)
    if seen is not None:
        scores = jnp.where(jnp.concatenate([seen, seen], 0) > 0.5, scores, NEG)
    expo = jnp.exp(scores - jnp.max(scores, -1, keepdims=True))
    return expo / jnp.sum(expo, -1, keepdims=True)


def pair_rows(ref, part, r, lanes, row_count, block_count):
    keys = ref.shape[0] // (2 * row_count * block_count)
    starts = [((2 * b + part) * row_count + r) * keys for b in range(block_count)]
    return jnp.concatenate([ref[start : start + keys, lanes] for start in starts], 0)


def attend(query, pairs, seen, row_count, block_count):
    tokens, width = query.shape
    frames = tokens // row_count
    keys = pairs.shape[0] // (2 * row_count)

    def body(*refs):
        query_ref, pair_ref = refs[:2]
        out_ref = refs[-1]
        for r in range(row_count):
            span = slice(r * frames, (r + 1) * frames)
            for j in range(0, LANES, 128):
                lanes = slice(j, j + 128)
                asked = two_heads(query_ref[span, lanes])
                key = pair_rows(pair_ref, 0, r, lanes, row_count, block_count)
                value = pair_rows(pair_ref, 1, r, lanes, row_count, block_count)
                probs = row_probs(asked, key, refs[2][r] if seen is not None else None)
                out_ref[span, lanes] = narrow(one_row(dot(narrow(probs), value)))

    token_spec = pl.BlockSpec((tokens, LANES), lambda i: (0, i))
    args = (query, pairs)
    specs = [token_spec, pl.BlockSpec((pairs.shape[0], LANES), lambda i: (0, i))]
    if seen is not None:
        args = args + (seen,)
        specs.append(pl.BlockSpec(seen.shape, lambda i: (0, 0, 0)))
    return pl.pallas_call(
        body,
        grid=(width // LANES,),
        out_shape=jax.ShapeDtypeStruct((tokens, width), jnp.bfloat16),
        in_specs=specs,
        out_specs=token_spec,
        cost_estimate=pl.CostEstimate(
            flops=8 * tokens * width * keys,
            bytes_accessed=4 * query.size + 2 * pairs.size,
            transcendentals=0,
        ),
    )(*args)


def attend_back(query, pairs, seen, grads, tables, row_count, block_count, scale):
    tokens, width = query.shape
    frames = tokens // row_count
    keys = pairs.shape[0] // (2 * row_count)

    def body(*refs):
        query_ref, pair_ref, grad_ref = refs[:3]
        out_query, out_pair = refs[-2:]

        def put(part, r, lanes, value):
            count = keys // block_count
            for b in range(block_count):
                start = ((2 * b + part) * row_count + r) * count
                out_pair[start : start + count, lanes] = narrow(value[b * count : (b + 1) * count])

        for r in range(row_count):
            span = slice(r * frames, (r + 1) * frames)
            for j in range(0, LANES, 128):
                lanes = slice(j, j + 128)
                asked = two_heads(query_ref[span, lanes])
                grad = two_heads(grad_ref[span, lanes])
                key = pair_rows(pair_ref, 0, r, lanes, row_count, block_count)
                value = pair_rows(pair_ref, 1, r, lanes, row_count, block_count)
                probs = row_probs(asked, key, refs[5][r] if seen is not None else None)
                score_grad = narrow(softmax_back(probs, dot_t(grad, value)))
                back = one_row(dot(score_grad, key))
                if tables is not None:
                    back = spin(back, refs[3][span, :], refs[4][span, :])
                out_query[span, lanes] = narrow(back * scale)
                put(0, r, lanes, tdot(score_grad, asked))
                put(1, r, lanes, tdot(narrow(probs), grad))

    token_spec = pl.BlockSpec((tokens, LANES), lambda i: (0, i))
    pair_spec = pl.BlockSpec((pairs.shape[0], LANES), lambda i: (0, i))
    specs = [token_spec, pair_spec, token_spec]
    args = (query, pairs, grads)
    if tables is not None:
        specs = specs + [pl.BlockSpec((tokens, 128), lambda i: (0, 0))] * 2
        args = args + tuple(tables)
    if seen is not None:
        specs.append(pl.BlockSpec(seen.shape, lambda i: (0, 0, 0)))
        args = args + (seen,)
    return pl.pallas_call(
        body,
        grid=(width // LANES,),
        out_shape=[
            jax.ShapeDtypeStruct((tokens, width), jnp.bfloat16),
            jax.ShapeDtypeStruct(pairs.shape, jnp.bfloat16),
        ],
        in_specs=specs,
        out_specs=[token_spec, pair_spec],
        cost_estimate=pl.CostEstimate(
            flops=20 * tokens * width * keys,
            bytes_accessed=6 * query.size + 4 * pairs.size,
            transcendentals=0,
        ),
    )(*args)


def order_matrix(size, rows, order, me):
    masks = jnp.asarray(np.array(masks_of(order), np.int32))
    source = ((me ^ masks)[:, None] * rows + jnp.arange(rows, dtype=jnp.int32)[None, :]).reshape(-1)
    return (jnp.arange(size, dtype=jnp.int32)[:, None] == source[None, :]).astype(jnp.bfloat16)


def local(
    frames,
    prompt,
    clip_frames,
    upstream,
    first_gain,
    first_shift,
    self_project,
    self_output,
    second_gain,
    second_shift,
    cross_query,
    cross_memory,
    cross_output,
    third_gain,
    third_shift,
    feed_input,
    feed_lift,
    feed_output,
    feed_offset,
):
    row_count, frame_count, width = frames.shape
    heads = width // HEAD_DIM
    token_count = row_count * frame_count
    scale = HEAD_DIM ** (-0.5)
    batch_count = lax.axis_size(B)
    seq_count = lax.axis_size(S)
    device_count = batch_count * seq_count
    seq_place = lax.axis_index(S)
    me = lax.axis_index(B) * seq_count + seq_place
    share = first_gain.shape[0]

    seq_masks = [1 << i for i in range(seq_count.bit_length() - 1)]
    batch_masks = [seq_count << i for i in range(batch_count.bit_length() - 1)]
    near = batch_masks[:3]
    far = batch_masks[3:]
    x_mask, y_mask = batch_masks[:2]
    places = [(0, 3, 1, 2), (3, 1, 2, 0), (3, 2, 0, 1)]
    if len(batch_masks) != 4:
        places = [[(i + j) % len(batch_masks) for i in range(len(batch_masks))] for j in range(3)]
    tail_orders = [[batch_masks[i] for i in place] for place in places]
    near_orders = [near[j:] + near[:j] for j in range(3)]
    near_count = len(masks_of(near))
    third = (token_count * 3 // 8) // 16 * 16
    cuts = [0, third, 2 * third, token_count]
    units = feed_output.shape[0]

    vectors = [first_gain, first_shift, second_gain, second_shift, third_gain, third_shift, feed_offset]
    vectors = jnp.pad(jnp.stack(vectors, 1), ((0, 0), (0, 128 - len(vectors))))
    split = 3 * width // 2
    group_one = narrow(jnp.concatenate([vectors, self_project], 1))
    memory_rows = ((0, share // 2 - cross_memory.shape[0]), (0, 0))
    memory_rows = jnp.concatenate(
        [
            jnp.pad(cross_memory[:, :width], memory_rows),
            jnp.pad(cross_memory[:, width:], memory_rows),
        ],
        0,
    )
    group_two = narrow(jnp.concatenate([self_output, cross_query, cross_output, memory_rows], 1))
    lift_rows = jnp.pad(feed_lift, ((0, 14), (0, width - units)))
    feed_sent = narrow(
        jnp.concatenate([feed_input.reshape(2 * units, width), feed_output, lift_rows], 0)
    )
    known = [0]
    for mask in batch_masks[:1:-1]:
        group_one = jnp.concatenate([group_one, hop(group_one, mask)], 0)
        if len(known) == 1:
            group_one, group_two = lax.optimization_barrier((group_one, group_two))
        group_two = jnp.concatenate([group_two, hop(group_two, mask)], 0)
        known = known + [old ^ mask for old in known]
    known = [known + [old ^ mask for old in known] for mask in (x_mask, y_mask)]

    def pieces_of(columns, others):
        halves = []
        for h in range(2):
            have = known[h]
            pieces = [(columns[h], have), (others[h], [old ^ (y_mask, x_mask)[h] for old in have])]
            halves.append(pieces)
        return halves

    def add_core(halves, got):
        for h in range(2):
            halves[h] = halves[h] + [
                (piece, [old ^ seq_masks[0] for old in have])
                for piece, (_, have) in zip(got[h], halves[h])
            ]
            for mask in seq_masks[1:]:
                halves[h] = halves[h] + [
                    (hop(piece, mask), [old ^ mask for old in have]) for piece, have in halves[h]
                ]
        return halves

    core = seq_masks[0]
    traffic = Traffic()
    feed_cuts = [0, 3 * units // 4, 2 * units + units // 6, feed_sent.shape[0]]
    if units % 192:
        feed_cuts = [0, units, 2 * units, feed_sent.shape[0]]
    feed_parts = [feed_sent[feed_cuts[p] : feed_cuts[p + 1]] for p in range(3)]
    ones = (group_one[:, : 128 + split], group_one[:, 128 + split :])
    got = volley(ones + (feed_parts[0],), [x_mask, y_mask, far[0]])
    feed_got = [got[2]]
    ones = tuple(jnp.concatenate(pair, 0) for pair in zip(ones, got))
    got_one = volley(ones + ones + (feed_parts[1],), [y_mask, x_mask, core, core, far[0]])
    feed_got.append(got_one[4])
    twos = (group_two[:, : 2 * width], group_two[:, 2 * width :])
    got = volley(
        twos + got_one[:2] + (feed_parts[2],), [x_mask, y_mask, core, core, far[0]]
    )
    feed_got.append(got[4])
    twos = tuple(jnp.concatenate(pair, 0) for pair in zip(twos, got))
    halves = pieces_of(ones, got_one[:2])
    halves = add_core(halves, ((got_one[2], got[2]), (got_one[3], got[3])))
    new = {"two": once(twos + twos, [y_mask, x_mask, core, core])}
    pieces = traffic.turn([piece for have in halves for piece, _ in have], lambda done: new)
    count = len(pieces) // 2
    halves = [
        [(piece, have) for piece, (_, have) in zip(pieces[h * count : (h + 1) * count], halves[h])]
        for h in range(2)
    ]
    packed, triple_low = settle(
        halves, [[(0, 0, 0, 128), (128, 1, 0, split)], [(0, 1, split, split)]], [128, 3 * width], me
    )
    packed = dot_t(jnp.eye(8, 128, dtype=jnp.bfloat16), packed)
    gain_one, shift_one, gain_two, shift_two, gain_three, shift_three, drop_bias = [
        packed[j : j + 1] for j in range(7)
    ]

    def cut_tokens(value):
        return [value[cuts[p] : cuts[p + 1]] for p in range(3)]

    def token_pairs(value):
        pairs = []
        for p in range(3):
            first, last = near_count * cuts[p], near_count * cuts[p + 1]
            middle = (first + last) // 2
            pairs.append((narrow(value[first:middle]), narrow(value[middle:last])))
        return pairs

    upstream_tokens = upstream.reshape(token_count, width)

    own_places = seq_place * frame_count + jnp.arange(frame_count, dtype=jnp.int32)
    key_order = masks_of(seq_masks)
    key_places = jnp.concatenate(
        [(seq_place ^ k) * frame_count + jnp.arange(frame_count, dtype=jnp.int32) for k in key_order]
    )
    own_clip, own_offset = clip_tables(clip_frames, own_places)
    key_clip = clip_tables(clip_frames, key_places)[0]
    seen = widen(own_clip[:, :, None] == key_clip[:, None, :])
    prompt_flat = prompt.reshape(-1, prompt.shape[2])
    rows = cross_memory.shape[0]
    place = jnp.arange(prompt.shape[2], dtype=jnp.int32)
    place = place // rows * share + place % rows
    places = jnp.arange(width, dtype=jnp.int32)[None, :]
    prompt_spread = [
        narrow(dot(prompt_flat, (place[:, None] + j * (share // 2) == places).astype(jnp.bfloat16)))
        for j in range(2)
    ]
    prompt_spread = jnp.concatenate(prompt_spread, 0)
    turn_tables = spin_tables(own_offset, 1.0)
    back_tables = spin_tables(own_offset, -1.0)

    inputs = frames.reshape(token_count, width)
    query, pairs, normed_one, inverse_one, hidden_one = project(
        inputs, gain_one, shift_one, triple_low, turn_tables, scale
    )
    query, prompt_spread = traffic.turn(
        (query, prompt_spread), lambda done: {"pairs": double_list(pairs, seq_masks)}, step=[]
    )
    for _ in seq_masks:
        (query,) = traffic.turn((query,), step=["pairs"])
    pairs = jnp.concatenate(traffic.done["pairs"], 0)

    def turn_rows(rows, order):
        return narrow(dot(rows, order_matrix(rows.shape[1], rows.shape[1] // device_count, order, me)))

    self_mixed = attend(query, pairs, seen, row_count, seq_count)

    def started(done):
        return {
            "last": once(done["two"][:2], [core, core]),
            "up": double_each(cut_tokens(upstream_tokens), near_orders),
        }

    self_mixed, feed_sent, *feed_got = traffic.turn([self_mixed, feed_sent] + feed_got, started)
    got_two = traffic.done["two"]
    feed_all = jnp.concatenate([feed_sent] + feed_got, 0)
    for mask in far[1:]:
        feed_all = jnp.concatenate([feed_all, hop(feed_all, mask)], 0)
    feed_all = feed_all.reshape(-1, feed_sent.shape[0], width)
    value_low, gate_low, drop_low = [
        feed_all[:, j * units : (j + 1) * units].reshape(-1, width) for j in range(3)
    ]
    unit_count = drop_low.shape[0]
    value_bias, gate_bias = [
        widen(feed_all[:, 3 * units + j, :units].reshape(1, unit_count)) for j in range(2)
    ]
    self_mixed, value_low, gate_low, drop_low, value_bias, gate_bias = traffic.turn(
        (self_mixed, value_low, gate_low, drop_low, value_bias, gate_bias),
        lambda done: {"mixed": double_list(self_mixed, seq_masks)},
    )
    got = traffic.done["last"]
    halves = add_core(
        pieces_of(twos, got_two[:2]), ((got_two[2], got[0]), (got_two[3], got[1]))
    )
    lows = settle(
        halves,
        [[(0, 0, 0, width), (width, 1, 0, width)], [(0, 2, 0, width), (width, 3, 0, width)]],
        [width] * 4,
        me,
    )
    self_low, ask_low, cross_low, memory_low, self_mixed = traffic.turn(
        (*lows, self_mixed), lambda done: {"hidden": double_list(hidden_one, seq_masks)}
    )
    memory = narrow(dot(prompt_spread, memory_low))
    after_self, normed_two, inverse_two, hidden_two, asking = ahead(
        self_mixed, self_low, inputs, gain_two, shift_two, ask_low, scale
    )
    cross_mixed = attend(asking, memory, None, row_count, 1)
    (cross_mixed,) = traffic.turn(
        (cross_mixed,),
        lambda done: {
            "ups": double_list(done["up"], seq_masks),
            "hidden_two": double_list(hidden_two, seq_masks),
        },
    )
    after_cross, normed_three, inverse_three, hidden_three = ahead(
        cross_mixed, cross_low, after_self, gain_three, shift_three
    )

    hidden_three, cross_mixed = traffic.turn(
        (hidden_three, cross_mixed),
        lambda done: {
            "rows": double_each(cut_tokens(hidden_three), near_orders),
            "cross_mixed": double_list(cross_mixed, seq_masks),
        },
    )
    for _ in seq_masks[1:]:
        traffic.turn((), step=["ups", "cross_mixed", "hidden_two", "hidden", "mixed"])
    ups = traffic.done["ups"]
    hidden_all, mixed_all, asked_all = [
        jnp.concatenate(traffic.done[name], 0) for name in ("hidden", "mixed", "hidden_two")
    ]
    turned_triple = [turn_rows(hidden_all, order) for order in tail_orders]
    turned_triple = traffic.turn(turned_triple)
    cross_all = jnp.concatenate(traffic.done["cross_mixed"], 0)
    turned_memory = turn_rows(prompt_flat, tail_orders[2])
    turned_memory = jnp.concatenate([turned_memory] * seq_count, 0)
    turned_cross = turn_rows(cross_all, tail_orders[0])
    turned_ask = turn_rows(asked_all, tail_orders[1])
    turned_self = [turn_rows(mixed_all, order) for order in tail_orders]
    turned_cross, turned_ask, turned_memory, *turned_self = traffic.turn(
        [turned_cross, turned_ask, turned_memory] + turned_self,
        lambda done: {"all": double_list(done["rows"], seq_masks)} if "rows" in done else {},
    )
    while "rows" in traffic.flows:
        traffic.turn((), lambda done: {"all": double_list(done["rows"], seq_masks)} if "rows" in done else {})
    lows = (value_low, gate_low, drop_low, value_bias, gate_bias)
    results = [feed_block(traffic.done["rows"], ups[0], *lows)]
    results[0] = traffic.turn(results[0])
    for _ in seq_masks[1:]:
        traffic.turn((), step=["all"])
    feed_rows = traffic.done["all"]
    for rows, up in zip(feed_rows[1:], ups[1:]):
        results.append(feed_block(rows, up, *lows))
    middles, value_grads, gate_grads, back_sums, term_sums = [list(item) for item in zip(*results)]

    def back_flow():
        value = yield from halve_list(back_sums, seq_masks)
        return (yield from halve_pairs(token_pairs(value), near_orders))

    blocks = len(feed_rows)
    far_count = len(masks_of(far))
    tied = traffic.turn(middles + value_grads + gate_grads, lambda done: {"back": back_flow()})
    middles, value_grads, gate_grads = tied[:blocks], tied[blocks : 2 * blocks], tied[2 * blocks :]
    drop_grad = unit_grad(middles, ups, False)[0]
    tied = traffic.turn((drop_grad, *value_grads, *gate_grads))
    for _ in seq_masks[1:]:
        tied = traffic.turn(tied)
    drop_grad, value_grads, gate_grads = tied[0], tied[1 : 1 + blocks], tied[1 + blocks :]
    value_grad, value_bias_grad = unit_grad(value_grads, feed_rows, True)
    gate_grad, gate_bias_grad = unit_grad(gate_grads, feed_rows, True)
    value_grad, gate_grad, drop_grad = traffic.turn(
        (value_grad, gate_grad, drop_grad),
        lambda done: {"term": halve_list(term_sums, seq_masks)},
    )

    def unit_rows(k):
        rows = slice(k * units, (k + 1) * units)
        bias = jnp.concatenate([value_bias_grad[:, rows], gate_bias_grad[:, rows]], 0)
        bias = narrow(jnp.pad(bias, ((0, 14), (0, width - units))))
        return jnp.concatenate([value_grad[rows], gate_grad[rows], drop_grad[rows], bias], 0)

    unit_sums = [unit_rows(k) for k in range(far_count)]
    unit_sums = list(traffic.turn(unit_sums))
    for _ in seq_masks[1:]:
        traffic.turn((), step=["term"])
    unit_cuts = [0] + [units // 2 * j for j in range(1, 6)] + [3 * units + 16]
    if units % 32:
        unit_cuts = [0] + [3 * units + 16] * 6

    def unit_flow(p):
        if unit_cuts[p] < unit_cuts[p + 1]:
            return halve_rows(unit_sums, unit_cuts[p], unit_cuts[p + 1], far)

    while "back" in traffic.flows:
        unit_sums = list(traffic.turn(unit_sums))
    feed_back = jnp.concatenate(traffic.done["back"], 0)
    (feed_back,) = traffic.turn(
        (feed_back,),
        lambda done: {"term_near": halve_pairs(token_pairs(done["term"]), near_orders)},
    )
    cross_out_grad, grad_gain_three, grad_shift_three, cross_branch, cross_mixed_grad = back(
        feed_back, None, upstream_tokens, normed_three, inverse_three, gain_three, cross_low
    )

    def weight_pair(turned, *grads):
        half = turned.shape[1] // 2
        pair = []
        for columns in (turned[:, :half], turned[:, half:]):
            sums = [narrow(tdot(columns, grad)) for grad in grads]
            if len(grads) > 1:
                rows = cross_memory.shape[0]
                sums = [
                    jnp.pad(part.reshape(-1, rows, width), ((0, 0), (0, share // 2 - rows), (0, 0)))
                    for part in sums
                ]
                sums = [jnp.concatenate(sums, 1).reshape(-1, width)]
            pair.append(sums[0])
        return tuple(pair)

    (cross_mixed_grad,) = traffic.turn(
        (cross_mixed_grad,),
        lambda done: {"dc": double_list(cross_branch, seq_masks), "unit0": unit_flow(0)},
    )
    asking_grad, memory_grad = attend_back(
        asking, memory, None, cross_mixed_grad, None, row_count, 1, scale
    )
    asking_grad, memory_grad = traffic.turn(
        (asking_grad, memory_grad),
        lambda done: {
            "dq": double_list(asking_grad, seq_masks),
            "dm": double_list(memory_grad, seq_masks),
        },
    )
    for _ in seq_masks[1:]:
        traffic.turn((), step=["dc"])
    self_out_grad, grad_gain_two, grad_shift_two, self_branch, self_mixed_grad = back(
        asking_grad, ask_low, cross_out_grad, normed_two, inverse_two, gain_two, self_low
    )
    (self_mixed_grad,) = traffic.turn(
        (self_mixed_grad,),
        lambda done: {"da": double_list(self_branch, seq_masks)},
    )
    for _ in seq_masks[1:]:
        traffic.turn((), step=["dq", "dm", "da"])
    cross_pair = weight_pair(turned_cross, jnp.concatenate(traffic.done["dc"], 0))
    layer_output = narrow(
        after_cross + jnp.concatenate(traffic.done["term_near"], 0) + drop_bias
    )
    ask_pair = weight_pair(turned_ask, jnp.concatenate(traffic.done["dq"], 0))
    memory_all = traffic.done["dm"]
    half = memory_grad.shape[0] // 2
    memory_pair = weight_pair(
        turned_memory,
        jnp.concatenate([part[:half] for part in memory_all], 0),
        jnp.concatenate([part[half:] for part in memory_all], 0),
    )
    self_mixed_grad, layer_output = traffic.turn(
        (self_mixed_grad, layer_output),
        lambda done: {
            "first": halve_pairs([cross_pair, ask_pair, memory_pair], tail_orders),
            "unit1": unit_flow(1),
        },
    )
    query_back, pair_grad = attend_back(
        query, pairs, seen, self_mixed_grad, back_tables, row_count, seq_count, scale
    )

    def shed_frames(value):
        for mask in reversed(seq_masks):
            half = value.shape[0] // 2
            (sent,) = yield (value[half:],)
            (got,) = yield hops((sent,), (mask,))
            if mask > seq_masks[0]:
                value = narrow(widen(value[:half]) + widen(got))
        return value, got

    (query_back,) = traffic.turn((query_back,), lambda done: {"pair": shed_frames(pair_grad)}, step=[])
    for _ in seq_masks:
        (query_back,) = traffic.turn((query_back,), step=["pair"])
    triple_back = spin_backward(query_back, *traffic.done["pair"], *back_tables)
    (triple_back,) = traffic.turn(
        (triple_back,), lambda done: {"dt": double_list(triple_back, seq_masks)}
    )
    frame_grad, grad_gain_one, grad_shift_one = back(
        triple_back, triple_low, self_out_grad, normed_one, inverse_one, gain_one
    )
    branch_all = jnp.concatenate(traffic.done["da"], 0)
    third = width // 3
    self_pairs = [
        weight_pair(turned, branch_all[:, p * third : (p + 1) * third])
        for p, turned in enumerate(turned_self)
    ]

    frame_grad, *sums = traffic.turn(
        (
            frame_grad,
            grad_gain_one,
            grad_shift_one,
            grad_gain_two,
            grad_shift_two,
            grad_gain_three,
            grad_shift_three,
        ),
        lambda done: {"unit2": unit_flow(2)},
    )
    grad_drop_bias = jnp.sum(widen(upstream_tokens), 0, keepdims=True)
    sums = jnp.concatenate(sums + [grad_drop_bias], 0).reshape(7, device_count, share)
    sums = jnp.transpose(sums, (1, 0, 2)).reshape(device_count, 7 * share)
    sums = jnp.pad(sums, ((0, 0), (0, 1024 - 7 * share)))
    tail_masks = masks_of(tail_orders[0] + seq_masks)
    sums = jnp.take(sums, me ^ jnp.asarray(np.array(tail_masks, np.int32)), axis=0)
    sums = sums.reshape(device_count, 8, 128)
    for _ in seq_masks[1:]:
        traffic.turn((), step=["dt"])
    triple_all = jnp.concatenate(traffic.done["dt"], 0)
    triple_pairs = [
        weight_pair(turned, triple_all[:, p * width : (p + 1) * width])
        for p, turned in enumerate(turned_triple)
    ]
    triple_pairs = [
        tuple(jnp.concatenate(item, 1) for item in zip(*pair))
        for pair in zip(triple_pairs, self_pairs)
    ]
    tied = traffic.turn(
        sum(triple_pairs, ()), lambda done: {"sums": halve_list_rows(sums, seq_masks)}
    )
    triple_pairs = [tied[2 * p : 2 * p + 2] for p in range(3)]
    while "first" in traffic.flows or "sums" in traffic.flows:
        traffic.turn(())
    sums = traffic.done["sums"]
    half = sums.shape[0] // 2
    traffic.turn(
        (),
        lambda done: {
            "tail": halve_pairs(
                triple_pairs + [(sums[:half], sums[half:])], tail_orders + [tail_orders[0]]
            ),
            "unit3": unit_flow(3),
        },
    )
    traffic.turn((), lambda done: {"unit4": unit_flow(4)})
    traffic.turn((), lambda done: {"unit5": unit_flow(5)})
    while traffic.flows:
        traffic.turn(())
    parts = traffic.done["tail"]
    grad_cross, grad_ask, grad_memory = traffic.done["first"]
    grad_self = jnp.concatenate([part[:, width:] for part in parts[:3]], 1)
    unit_sums = jnp.concatenate([traffic.done[name] for name in UNITS if name in traffic.done], 0)
    grad_triple = jnp.concatenate([part[:, :width] for part in parts[:3]], 1)
    sums = parts[3].reshape(1024)[: 7 * share].reshape(7, share)
    grad_memory = grad_memory.reshape(2, share // 2, width)[:, : cross_memory.shape[0]]
    grad_memory = jnp.concatenate([grad_memory[0], grad_memory[1]], 1)
    grad_lift = unit_sums[: 2 * units].reshape(2, units, width)
    grad_drop = unit_sums[2 * units : 3 * units]
    grad_lift_bias = unit_sums[3 * units : 3 * units + 2, :units]

    shape = frames.shape
    return (
        layer_output.reshape(shape),
        frame_grad.reshape(shape),
        sums[0],
        sums[1],
        grad_triple,
        grad_self,
        sums[2],
        sums[3],
        grad_ask,
        grad_memory,
        grad_cross,
        sums[4],
        sums[5],
        grad_lift,
        grad_lift_bias,
        grad_drop,
        sums[6],
    )


def solution(mesh):
    both = P(AX)
    wide = P(AX, None)
    rows = P(B, S, None)
    units = P(None, AX, None)
    in_specs = (
        rows,
        P(B, None, None),
        P(B, None),
        rows,
        both,
        both,
        wide,
        wide,
        both,
        both,
        wide,
        wide,
        wide,
        both,
        both,
        units,
        P(None, AX),
        wide,
        both,
    )
    out_specs = (
        rows,
        rows,
        both,
        both,
        wide,
        wide,
        both,
        both,
        wide,
        wide,
        wide,
        both,
        both,
        units,
        P(None, AX),
        wide,
        both,
    )
    return jax.shard_map(local, mesh=mesh, in_specs=in_specs, out_specs=out_specs, check_vma=False)
```

```python
import jax
import jax.numpy as jnp
import numpy as np
from jax import lax
from jax.experimental import pallas as pl
from jax.experimental.pallas import tpu as pltpu
from jax.sharding import PartitionSpec as P

HEAD_DIM = 64
LANES = 512
UNITS = ["unit0", "unit1", "unit2", "unit3", "unit4"]
EPS = 1e-05
NEG = -1e30
B = "batch"
S = "seq"
AX = (B, S)


def narrow(value):
    return value.astype(jnp.bfloat16)


def widen(value):
    return value.astype(jnp.float32)


def mult(left, right, form):
    return jnp.einsum(form, left, right, preferred_element_type=jnp.float32)


def dot(left, right):
    return lax.dot_general(left, right, (((1,), (0,)), ((), ())), preferred_element_type=jnp.float32)


def dot_t(left, right):
    return lax.dot_general(left, right, (((1,), (1,)), ((), ())), preferred_element_type=jnp.float32)


def tdot(left, right):
    return lax.dot_general(left, right, (((0,), (0,)), ((), ())), preferred_element_type=jnp.float32)


def standardize(values):
    center = values - jnp.mean(values, -1, keepdims=True)
    inverse = lax.rsqrt(jnp.mean(center * center, -1, keepdims=True) + EPS)
    return (center * inverse, inverse)


def norm_back(incoming, normed, inverse, gain):
    scaled = incoming * gain
    inner = (
        scaled
        - jnp.mean(scaled, -1, keepdims=True)
        - normed * jnp.mean(scaled * normed, -1, keepdims=True)
    )
    return (
        inner * inverse,
        jnp.sum(incoming * normed, 0, keepdims=True),
        jnp.sum(incoming, 0, keepdims=True),
    )


def clip_tables(lengths, places):
    ends = jnp.cumsum(lengths, 1)
    later = places[None, :, None] >= ends[:, None, :]
    ident = jnp.sum(later.astype(jnp.int32), 2)
    starts = jnp.max(jnp.where(later, ends[:, None, :], 0), 2)
    return (ident, places[None, :] - starts)


def softmax_back(probs, prob_grad):
    return probs * (prob_grad - jnp.sum(probs * prob_grad, 0, keepdims=True))


def hop(value, mask):
    count = lax.axis_size(B) * lax.axis_size(S)
    return lax.ppermute(value, AX, [(i, i ^ mask) for i in range(count)])


def volley(values, masks):
    values = lax.optimization_barrier(tuple(values))
    return lax.optimization_barrier(tuple(hop(value, mask) for value, mask in zip(values, masks)))


def masks_of(order):
    masks = [0]
    for mask in order:
        masks = masks + [old ^ mask for old in masks]
    return masks


def gather(value, order):
    for mask in order:
        value = jnp.concatenate([value, hop(value, mask)], 0)
    return value


def settle(halves, targets, widths, me):
    pieces = [(h, piece, have) for h in range(2) for piece, have in halves[h]]
    total = sum(len(have) for h, piece, have in pieces if h == 0)
    rows = pieces[0][1].shape[0] // len(pieces[0][2])
    if rows % 16:
        outs = [[] for _ in widths]
        for h in range(2):
            have = sum([have for _, have in halves[h]], [])
            table = np.zeros(total, np.int32)
            table[np.array(have)] = np.arange(total)
            place = jnp.asarray(table)[me ^ jnp.arange(total, dtype=jnp.int32)]
            blocks = jnp.concatenate([piece for piece, _ in halves[h]], 0).reshape(total, rows, -1)
            blocks = jnp.take(blocks, place, axis=0).reshape(total * rows, -1)
            for source, out, _, count in targets[h]:
                outs[out].append(blocks[:, source : source + count])
        return [jnp.concatenate(out, 1) for out in outs]

    def body(me_ref, *refs):
        ins = refs[: len(pieces)]
        outs = refs[len(pieces) : len(pieces) + len(widths)]
        held = refs[len(pieces) + len(widths) : -2]
        in_sems, out_sems = refs[-2:]
        loads = []
        for i in range(len(pieces)):
            load = pltpu.make_async_copy(ins[i], held[i], in_sems.at[i])
            load.start()
            loads.append(load)
        stores = []
        for i, (h, _, have) in enumerate(pieces):
            loads[i].wait()
            for j, mask in enumerate(have):
                start = pl.multiple_of((me_ref[0] ^ mask) * rows, rows)
                for source, out, column, count in targets[h]:
                    store = pltpu.make_async_copy(
                        held[i].at[pl.ds(j * rows, rows), pl.ds(source, count)],
                        outs[out].at[pl.ds(start, rows), pl.ds(column, count)],
                        out_sems.at[len(stores)],
                    )
                    store.start()
                    stores.append(store)
        for store in stores:
            store.wait()

    count = sum(len(have) * len(targets[h]) for h, _, have in pieces)
    size = 2 * sum(piece.size for _, piece, _ in pieces)
    return pl.pallas_call(
        body,
        out_shape=[jax.ShapeDtypeStruct((total * rows, width), jnp.bfloat16) for width in widths],
        in_specs=[pl.BlockSpec(memory_space=pltpu.SMEM)]
        + [pl.BlockSpec(memory_space=pl.ANY)] * len(pieces),
        out_specs=[pl.BlockSpec(memory_space=pltpu.HBM)] * len(widths),
        scratch_shapes=[pltpu.VMEM(piece.shape, jnp.bfloat16) for _, piece, _ in pieces]
        + [pltpu.SemaphoreType.DMA((len(pieces),)), pltpu.SemaphoreType.DMA((count,))],
        compiler_params=pltpu.CompilerParams(vmem_limit_bytes=size + (2 << 20)),
        cost_estimate=pl.CostEstimate(flops=0, bytes_accessed=size // 16, transcendentals=0),
    )(me.reshape(1), *[piece for _, piece, _ in pieces])


class Traffic:
    def __init__(self):
        self.flows = {}
        self.done = {}

    def turn(self, outs, new=None, step=None):
        names = list(self.flows) if step is None else [n for n in step if n in self.flows]
        gots = sum([self.flows[name][1] for name in names], ())
        tied = lax.optimization_barrier(gots + tuple(outs))
        outs = tied[len(gots) :]
        started = []
        for name in names:
            flow, got = self.flows.pop(name)
            got, tied = tied[: len(got)], tied[len(got) :]
            try:
                started.append((name, flow, flow.send(got)))
            except StopIteration as end:
                self.done[name] = end.value
        if new is not None:
            flows = new(self.done)
            for name, flow in ((name, flow) for name, flow in flows.items() if flow is not None):
                started.append((name, flow, next(flow)))
        sents = sum([sent for _, _, sent in started], ())
        tied = lax.optimization_barrier(sents + outs)
        for name, flow, sent in started:
            self.flows[name] = (flow, flow.send(tied[: len(sent)]))
            tied = tied[len(sent) :]
        return tied


def hops(values, masks):
    return tuple(hop(value, mask) for value, mask in zip(values, masks))


def once(values, masks):
    values = yield tuple(values)
    return (yield hops(values, masks))


def halve_pairs(pairs, orders):
    for step in list(zip(*orders))[::-1]:
        sent = yield tuple(sent for _, sent in pairs)
        got = yield hops(sent, step)
        sums = [(kept, part) for (kept, _), part in zip(pairs, got)]
        pairs = []
        for kept, part in sums:
            half = kept.shape[0] // 2
            pair = [widen(kept[cut]) + widen(part[cut]) for cut in (slice(half), slice(half, None))]
            pairs.append(pair if kept.ndim == 3 else [narrow(item) for item in pair])
    return [widen(kept) + widen(part) for kept, part in sums]


def halve_list_rows(value, masks):
    for mask in reversed(masks):
        half = value.shape[0] // 2
        sent = yield (value[half:],)
        (got,) = yield hops(sent, (mask,))
        value = value[:half] + got
    return value


def halve_list(blocks, masks):
    for mask in reversed(masks):
        half = len(blocks) // 2
        sent = yield tuple(narrow(block) for block in blocks[half:])
        got = yield hops(sent, (mask,) * half)
        blocks = [widen(a) + widen(b) for a, b in zip(blocks[:half], got)]
    return blocks[0]


def halve_rows(blocks, first, last, masks):
    for mask in reversed(masks):
        half = len(blocks) // 2
        sent = yield tuple(narrow(block[first:last]) for block in blocks[half:])
        got = yield hops(sent, (mask,) * half)
        blocks = [widen(a[first:last]) + widen(b) for a, b in zip(blocks[:half], got)]
        first, last = 0, last - first
    return blocks[0]


def double_each(parts, orders):
    for step in zip(*orders):
        parts = yield tuple(parts)
        got = yield hops(parts, step)
        pairs = list(zip(parts, got))
        parts = [jnp.concatenate(pair, 0) for pair in pairs]
    return sum(pairs, ())


def double_list(value, masks):
    blocks = (value,)
    for mask in masks:
        blocks = yield blocks
        got = yield hops(blocks, (mask,) * len(blocks))
        blocks = tuple(blocks) + tuple(got)
    return blocks


def spin(value, cosine, sine):
    lane = lax.broadcasted_iota(jnp.int32, value.shape, 1)
    other = jnp.where(lane % 64 < 32, pltpu.roll(value, 96, 1), pltpu.roll(value, 32, 1))
    return value * cosine + other * sine


def spin_tables(offsets, sign):
    half = HEAD_DIM // 2
    freq = 10000.0 ** (-jnp.arange(half, dtype=jnp.float32) / half)
    angle = offsets.astype(jnp.float32).reshape(-1, 1) * freq
    cosine = jnp.cos(angle)
    sine = sign * jnp.sin(angle)
    return (jnp.concatenate([cosine] * 4, 1), jnp.concatenate([-sine, sine, -sine, sine], 1))


def hint():
    return pl.CostEstimate(flops=1 << 20, bytes_accessed=1 << 20, transcendentals=0)


def whole(array):
    return pl.BlockSpec(array.shape, lambda i: (0,) * array.ndim)


def like(shape, dtype=jnp.float32):
    return jax.ShapeDtypeStruct(shape, dtype)


def room(mebibytes):
    return pltpu.CompilerParams(vmem_limit_bytes=mebibytes << 20)


def project(inputs, gain, shift, weight, tables, scale):
    rows, width = inputs.shape
    block = width

    def body(in_ref, gain_ref, shift_ref, cos_ref, sin_ref, weight_ref, *outs):
        query_ref, pair_ref, normed_ref, inverse_ref, hidden_ref = outs
        step = pl.program_id(0)

        @pl.when(step == 0)
        def _():
            normed, inverse = standardize(widen(in_ref[...]))
            normed_ref[...] = normed
            inverse_ref[...] = inverse
            hidden_ref[...] = narrow(normed * gain_ref[...] + shift_ref[...])

        value = dot(hidden_ref[...], weight_ref[...])

        def turned(factor):
            parts = [
                spin(value[:, j : j + 128], cos_ref[...], sin_ref[...]) for j in range(0, block, 128)
            ]
            return [narrow(part * factor) for part in parts]

        @pl.when(step == 0)
        def _():
            for j, part in enumerate(turned(scale)):
                query_ref[:, 128 * j : 128 * j + 128] = part

        @pl.when(step == 1)
        def _():
            for j, part in enumerate(turned(1.0)):
                pair_ref[:, 128 * j : 128 * j + 128] = part

        @pl.when(step == 2)
        def _():
            pair_ref[...] = narrow(value)

    return pl.pallas_call(
        body,
        grid=(3,),
        out_shape=[
            like((rows, width), jnp.bfloat16),
            like((2 * rows, width), jnp.bfloat16),
            like((rows, width)),
            like((rows, 1)),
            like((rows, width), jnp.bfloat16),
        ],
        in_specs=[
            whole(inputs),
            whole(gain),
            whole(shift),
            whole(tables[0]),
            whole(tables[1]),
            pl.BlockSpec((width, block), lambda i: (0, i)),
        ],
        out_specs=[
            pl.BlockSpec((rows, block), lambda i: (0, 0)),
            pl.BlockSpec((rows, block), lambda i: (jnp.maximum(i - 1, 0), 0)),
            pl.BlockSpec((rows, width), lambda i: (0, 0)),
            pl.BlockSpec((rows, 1), lambda i: (0, 0)),
            pl.BlockSpec((rows, width), lambda i: (0, 0)),
        ],
        compiler_params=room(22),
        cost_estimate=hint(),
    )(inputs, gain, shift, *tables, weight)


def ahead(mixed, low, before, gain, shift, ask=None, scale=1.0):
    rows, width = before.shape
    steps = width // LANES

    def body(mixed_ref, before_ref, gain_ref, shift_ref, *refs):
        low_ref, refs = refs[0], refs[1:]
        if ask is not None:
            ask_ref, refs = refs[0], refs[1:]
        sum_ref, normed_ref, inverse_ref, hidden_ref = refs[:4]
        step = pl.program_id(0)

        @pl.when(step < steps)
        def _():
            lanes = pl.ds(pl.multiple_of(step * LANES, LANES), LANES)
            sum_ref[:, lanes] = widen(before_ref[:, lanes]) + dot(mixed_ref[...], low_ref[...])

        @pl.when(step == steps - 1)
        def _():
            normed, inverse = standardize(sum_ref[...])
            normed_ref[...] = normed
            inverse_ref[...] = inverse
            hidden_ref[...] = narrow(normed * gain_ref[...] + shift_ref[...])

        if ask is not None:

            @pl.when(step >= steps)
            def _():
                refs[4][...] = narrow(dot(hidden_ref[...], ask_ref[...]) * scale)

    full = pl.BlockSpec((rows, width), lambda i: (0, 0))
    args = (mixed, before, gain, shift, low)
    specs = [whole(mixed), whole(before), whole(gain), whole(shift)]
    specs.append(pl.BlockSpec((width, LANES), lambda i: (0, jnp.minimum(i, steps - 1))))
    shapes = [
        like((rows, width)),
        like((rows, width)),
        like((rows, 1)),
        like((rows, width), jnp.bfloat16),
    ]
    outs = [full, full, pl.BlockSpec((rows, 1), lambda i: (0, 0)), full]
    if ask is not None:
        args = args + (ask,)
        specs.append(pl.BlockSpec((width, LANES), lambda i: (0, jnp.maximum(i - steps, 0))))
        shapes.append(like((rows, width), jnp.bfloat16))
        outs.append(pl.BlockSpec((rows, LANES), lambda i: (0, jnp.maximum(i - steps, 0))))
    return pl.pallas_call(
        body,
        grid=(steps if ask is None else 2 * steps,),
        out_shape=shapes,
        in_specs=specs,
        out_specs=outs,
        compiler_params=room(16),
        cost_estimate=hint(),
    )(*args)


def back(incoming, low, grads, normed, inverse, gain, out=None):
    rows, width = grads.shape
    block = LANES
    first = 0 if low is None else width // block
    last = 0 if out is None else width // LANES
    norm_step = max(first - 1, 0)

    def body(in_ref, grad_ref, normed_ref, inverse_ref, gain_ref, *refs):
        if low is not None:
            low_ref, refs = refs[0], refs[1:]
        if out is not None:
            out_ref, refs = refs[0], refs[1:]
        sum_ref, gain_grad_ref, shift_grad_ref = refs[:3]
        held_ref = refs[-1]
        step = pl.program_id(0)
        if low is not None:

            @pl.when(step < first)
            def _():
                lanes = pl.ds(pl.multiple_of(step * block, block), block)
                held_ref[:, lanes] = dot_t(in_ref[...], low_ref[...])

        @pl.when(step == norm_step)
        def _():
            value = in_ref[...] if low is None else held_ref[...]
            inner, gain_grad, shift_grad = norm_back(
                value, normed_ref[...], inverse_ref[...], gain_ref[...]
            )
            total = widen(grad_ref[...]) + inner
            sum_ref[...] = total
            gain_grad_ref[...] = gain_grad
            shift_grad_ref[...] = shift_grad
            if out is not None:
                refs[3][...] = narrow(total)

        if out is not None:

            @pl.when(step >= first)
            def _():
                refs[4][...] = narrow(dot_t(refs[3][...], out_ref[...]))

    full = pl.BlockSpec((rows, width), lambda i: (0, 0))
    line = pl.BlockSpec((1, width), lambda i: (0, 0))
    args = (incoming, grads, normed, inverse, gain)
    specs = [whole(array) for array in args]
    if low is not None:
        args = args + (low,)
        specs.append(pl.BlockSpec((block, low.shape[1]), lambda i: (jnp.minimum(i, first - 1), 0)))
    shapes = [like((rows, width)), like((1, width)), like((1, width))]
    outs = [full, line, line]
    if out is not None:
        args = args + (out,)
        specs.append(pl.BlockSpec((LANES, width), lambda i: (jnp.maximum(i - first, 0), 0)))
        shapes = shapes + [like((rows, width), jnp.bfloat16)] * 2
        outs = outs + [full, pl.BlockSpec((rows, LANES), lambda i: (0, jnp.maximum(i - first, 0)))]
    return pl.pallas_call(
        body,
        grid=(first + last,),
        out_shape=shapes,
        in_specs=specs,
        out_specs=outs,
        scratch_shapes=[pltpu.VMEM((rows, width), jnp.float32)],
        compiler_params=room(24),
        cost_estimate=hint(),
    )(*args)


def feed_block(rows, ups, value_low, gate_low, drop_low, value_bias, gate_bias):
    count, width = rows.shape
    units = drop_low.shape[0]
    block = min(count, 256)

    def body(row_ref, up_ref, value_ref, gate_ref, drop_ref, value_bias_ref, gate_bias_ref, *outs):
        middle_ref, value_out, gate_out, back_ref, term_ref = outs
        middle_grad = widen(narrow(dot_t(up_ref[...], drop_ref[...])))
        value = dot_t(row_ref[...], value_ref[...]) + value_bias_ref[...]
        gate = dot_t(row_ref[...], gate_ref[...]) + gate_bias_ref[...]
        sigma = jax.nn.sigmoid(gate)
        middle = narrow(value * gate * sigma)
        value_grad = narrow(middle_grad * gate * sigma)
        gate_grad = narrow(middle_grad * value * sigma * (1.0 + gate * (1.0 - sigma)))
        middle_ref[...] = middle
        value_out[...] = value_grad
        gate_out[...] = gate_grad
        back_ref[...] = narrow(dot(value_grad, value_ref[...]) + dot(gate_grad, gate_ref[...]))
        term_ref[...] = narrow(dot(middle, drop_ref[...]))

    wide = pl.BlockSpec((block, width), lambda i: (i, 0))
    thin = pl.BlockSpec((block, units), lambda i: (i, 0))
    args = (rows, ups, value_low, gate_low, drop_low, value_bias, gate_bias)
    return pl.pallas_call(
        body,
        grid=(count // block,),
        out_shape=[like((count, units), jnp.bfloat16)] * 3 + [like((count, width), jnp.bfloat16)] * 2,
        in_specs=[wide, wide] + [whole(array) for array in args[2:]],
        out_specs=[thin] * 3 + [wide] * 2,
        compiler_params=room(24),
        cost_estimate=hint(),
    )(*args)


def unit_grad(lefts, rights, sums):
    units = lefts[0].shape[1]
    width = rights[0].shape[1]
    count = len(lefts)
    block = 128 if units % 128 == 0 else units

    def body(*refs):
        total = 0.0
        for left, right in zip(refs[:count], refs[count : 2 * count]):
            total = total + tdot(left[...], right[...])
        refs[2 * count][...] = narrow(total)
        if sums:
            refs[2 * count + 1][...] = sum(
                jnp.sum(widen(left[...]), 0, keepdims=True) for left in refs[:count]
            )

    specs = [pl.BlockSpec((left.shape[0], block), lambda i: (0, i)) for left in lefts]
    outs = [pl.BlockSpec((block, width), lambda i: (i, 0))]
    shapes = [like((units, width), jnp.bfloat16)]
    if sums:
        outs.append(pl.BlockSpec((1, block), lambda i: (0, i)))
        shapes.append(like((1, units)))
    return pl.pallas_call(
        body,
        grid=(units // block,),
        out_shape=shapes,
        in_specs=specs + [whole(right) for right in rights],
        out_specs=outs,
        compiler_params=room(24),
        cost_estimate=hint(),
    )(*lefts, *rights)


def spin_backward(query, pairs, got, cosine, sine):
    rows, width = query.shape

    def body(cos_ref, sin_ref, query_ref, own_ref, got_ref, out_ref):
        step = pl.program_id(0)

        @pl.when(step == 0)
        def _():
            out_ref[...] = query_ref[...]

        @pl.when(step == 1)
        def _():
            for j in range(0, width, 128):
                value = widen(own_ref[:, j : j + 128]) + widen(got_ref[:, j : j + 128])
                out_ref[:, j : j + 128] = narrow(spin(value, cos_ref[...], sin_ref[...]))

        @pl.when(step == 2)
        def _():
            out_ref[...] = narrow(widen(own_ref[...]) + widen(got_ref[...]))

    table = pl.BlockSpec((rows, 128), lambda i: (0, 0))
    part = pl.BlockSpec((rows, width), lambda i: (jnp.maximum(i - 1, 0), 0))
    return pl.pallas_call(
        body,
        grid=(3,),
        out_shape=jax.ShapeDtypeStruct((rows, 3 * width), jnp.bfloat16),
        in_specs=[table, table, pl.BlockSpec((rows, width), lambda i: (0, 0)), part, part],
        out_specs=pl.BlockSpec((rows, width), lambda i: (0, i)),
        compiler_params=room(8),
        cost_estimate=pl.CostEstimate(
            flops=24 * query.size, bytes_accessed=16 * query.size, transcendentals=0
        ),
    )(cosine, sine, query, pairs, got)


def two_heads(value):
    lane = lax.broadcasted_iota(jnp.int32, value.shape, 1)
    zero = jnp.zeros_like(value)
    first = jnp.where(lane < HEAD_DIM, value, zero)
    second = jnp.where(lane < HEAD_DIM, zero, value)
    return jnp.concatenate([first, second], 0)


def one_row(value):
    half = value.shape[0] // 2
    lane = lax.broadcasted_iota(jnp.int32, (half, value.shape[1]), 1)
    return jnp.where(lane < HEAD_DIM, value[:half], value[half:])


def row_probs(asked, keys, seen):
    scores = dot_t(keys, asked)
    if seen is not None:
        scores = jnp.where(jnp.concatenate([seen, seen], 1) > 0.5, scores, NEG)
    expo = jnp.exp(scores - jnp.max(scores, 0, keepdims=True))
    return expo * (1.0 / jnp.sum(expo, 0, keepdims=True))


def pair_rows(refs, part, r, lanes, row_count):
    keys = refs[0].shape[0] // (2 * row_count)
    start = (part * row_count + r) * keys
    return jnp.concatenate([ref[start : start + keys, lanes] for ref in refs], 0)


def attend(query, pairs, seen, row_count):
    tokens, width = query.shape
    frames = tokens // row_count
    count = len(pairs)

    def body(*refs):
        query_ref, pair_refs, out_ref = refs[0], refs[1 : 1 + count], refs[-1]
        for r in range(row_count):
            span = slice(r * frames, (r + 1) * frames)
            for j in range(0, LANES, 128):
                lanes = slice(j, j + 128)
                asked = two_heads(query_ref[span, lanes])
                key, value = [pair_rows(pair_refs, p, r, lanes, row_count) for p in range(2)]
                probs = row_probs(asked, key, refs[1 + count][r] if seen is not None else None)
                out_ref[span, lanes] = narrow(one_row(tdot(narrow(probs), value)))

    token_spec = pl.BlockSpec((tokens, LANES), lambda i: (0, i))
    args = (query, *pairs)
    specs = [token_spec] + [pl.BlockSpec((pairs[0].shape[0], LANES), lambda i: (0, i))] * count
    if seen is not None:
        args = args + (seen,)
        specs.append(whole(seen))
    return pl.pallas_call(
        body,
        grid=(width // LANES,),
        out_shape=like((tokens, width), jnp.bfloat16),
        in_specs=specs,
        out_specs=token_spec,
        compiler_params=room(8),
        cost_estimate=hint(),
    )(*args)


def attend_back(query, pairs, seen, grads, tables, row_count, scale):
    tokens, width = query.shape
    frames = tokens // row_count
    count = len(pairs)
    block = pairs[0].shape[0]
    keys = block // (2 * row_count)

    def body(*refs):
        query_ref, grad_ref, pair_refs = refs[0], refs[1], refs[2 : 2 + count]
        rest = refs[2 + count :]
        out_query, out_pair = refs[-2:]

        def put(part, r, lanes, value):
            for b in range(count):
                start = b * block + (part * row_count + r) * keys
                out_pair[start : start + keys, lanes] = narrow(value[b * keys : (b + 1) * keys])

        for r in range(row_count):
            span = slice(r * frames, (r + 1) * frames)
            for j in range(0, LANES, 128):
                lanes = slice(j, j + 128)
                asked = two_heads(query_ref[span, lanes])
                grad = two_heads(grad_ref[span, lanes])
                key, value = [pair_rows(pair_refs, p, r, lanes, row_count) for p in range(2)]
                probs = row_probs(asked, key, rest[2][r] if seen is not None else None)
                score_grad = narrow(softmax_back(probs, dot_t(value, grad)))
                result = one_row(tdot(score_grad, key))
                if tables is not None:
                    result = spin(result, rest[0][span, :], rest[1][span, :])
                out_query[span, lanes] = narrow(result * scale)
                put(0, r, lanes, dot(score_grad, asked))
                put(1, r, lanes, dot(narrow(probs), grad))

    token_spec = pl.BlockSpec((tokens, LANES), lambda i: (0, i))
    specs = [token_spec] * 2 + [pl.BlockSpec((block, LANES), lambda i: (0, i))] * count
    args = (query, grads, *pairs)
    if tables is not None:
        specs = specs + [whole(table) for table in tables]
        args = args + tuple(tables)
    if seen is not None:
        specs.append(whole(seen))
        args = args + (seen,)
    return pl.pallas_call(
        body,
        grid=(width // LANES,),
        out_shape=[like((tokens, width), jnp.bfloat16), like((count * block, width), jnp.bfloat16)],
        in_specs=specs,
        out_specs=[token_spec, pl.BlockSpec((count * block, LANES), lambda i: (0, i))],
        compiler_params=room(12),
        cost_estimate=hint(),
    )(*args)


def multiply(left, right):
    rows, depth = left.shape
    width = right.shape[1]

    def body(left_ref, right_ref, out_ref):
        out_ref[...] = narrow(dot(left_ref[...], right_ref[...]))

    return pl.pallas_call(
        body,
        grid=(width // LANES,),
        out_shape=like((rows, width), jnp.bfloat16),
        in_specs=[whole(left), pl.BlockSpec((depth, LANES), lambda i: (0, i))],
        out_specs=pl.BlockSpec((rows, LANES), lambda i: (0, i)),
        compiler_params=room(12),
        cost_estimate=hint(),
    )(left, right)


def weight_sums(lefts, rights):
    rows = lefts[0].shape[1] // 2
    widths = [right.shape[1] for right in rights]
    count = len(lefts)
    if rows % 128:
        sums = [narrow(tdot(left, right)) for left, right in zip(lefts, rights)]
        sums = jnp.concatenate(sums, 1)
        return sums[:rows], sums[rows:]

    def body(*refs):
        for half in range(2):

            @pl.when(pl.program_id(0) == half)
            def _():
                start = 0
                for left, right, width in zip(refs[:count], refs[count : 2 * count], widths):
                    lanes = slice(start, start + width)
                    refs[2 * count + half][:, lanes] = narrow(tdot(left[...], right[...]))
                    start = start + width

    specs = [pl.BlockSpec((left.shape[0], rows), lambda i: (0, i)) for left in lefts]
    out = pl.BlockSpec((rows, sum(widths)), lambda i: (0, 0))
    return pl.pallas_call(
        body,
        grid=(2,),
        out_shape=[like((rows, sum(widths)), jnp.bfloat16)] * 2,
        in_specs=specs + [whole(right) for right in rights],
        out_specs=[out, out],
        compiler_params=room(14),
        cost_estimate=hint(),
    )(*lefts, *rights)


def order_matrix(size, rows, order, me):
    masks = jnp.asarray(np.array(masks_of(order), np.int32))
    source = ((me ^ masks)[:, None] * rows + jnp.arange(rows, dtype=jnp.int32)[None, :]).reshape(-1)
    return (jnp.arange(size, dtype=jnp.int32)[:, None] == source[None, :]).astype(jnp.bfloat16)


def local(
    frames,
    prompt,
    clip_frames,
    upstream,
    first_gain,
    first_shift,
    self_project,
    self_output,
    second_gain,
    second_shift,
    cross_query,
    cross_memory,
    cross_output,
    third_gain,
    third_shift,
    feed_input,
    feed_lift,
    feed_output,
    feed_offset,
):
    row_count, frame_count, width = frames.shape
    heads = width // HEAD_DIM
    token_count = row_count * frame_count
    scale = HEAD_DIM ** (-0.5)
    batch_count = lax.axis_size(B)
    seq_count = lax.axis_size(S)
    device_count = batch_count * seq_count
    seq_place = lax.axis_index(S)
    me = lax.axis_index(B) * seq_count + seq_place
    share = first_gain.shape[0]

    seq_masks = [1 << i for i in range(seq_count.bit_length() - 1)]
    batch_masks = [seq_count << i for i in range(batch_count.bit_length() - 1)]
    near = batch_masks[:3]
    far = batch_masks[3:]
    x_mask, y_mask = batch_masks[:2]
    places = [(0, 3, 1, 2), (3, 1, 2, 0), (3, 2, 0, 1)]
    if len(batch_masks) != 4:
        places = [[(i + j) % len(batch_masks) for i in range(len(batch_masks))] for j in range(3)]
    tail_orders = [[batch_masks[i] for i in place] for place in places]
    near_orders = [near[j:] + near[:j] for j in range(3)]
    near_count = len(masks_of(near))
    third = (token_count * 3 // 8) // 16 * 16
    cuts = [0, third, 2 * third, token_count]
    units = feed_output.shape[0]

    vectors = [first_gain, first_shift, second_gain, second_shift, third_gain, third_shift, feed_offset]
    vectors = jnp.pad(jnp.stack(vectors, 1), ((0, 0), (0, 128 - len(vectors))))
    split = 3 * width // 2
    group_one = narrow(jnp.concatenate([vectors, self_project], 1))
    memory_rows = ((0, share // 2 - cross_memory.shape[0]), (0, 0))
    memory_rows = jnp.concatenate(
        [
            jnp.pad(cross_memory[:, :width], memory_rows),
            jnp.pad(cross_memory[:, width:], memory_rows),
        ],
        0,
    )
    group_two = narrow(jnp.concatenate([self_output, cross_query, cross_output, memory_rows], 1))
    lift_rows = jnp.pad(feed_lift, ((0, 14), (0, width - units)))
    feed_sent = narrow(
        jnp.concatenate([feed_input.reshape(2 * units, width), feed_output, lift_rows], 0)
    )
    own_places = seq_place * frame_count + jnp.arange(frame_count, dtype=jnp.int32)
    key_order = masks_of(seq_masks)
    key_places = jnp.concatenate(
        [(seq_place ^ k) * frame_count + jnp.arange(frame_count, dtype=jnp.int32) for k in key_order]
    )
    own_clip, own_offset = clip_tables(clip_frames, own_places)
    key_clip = clip_tables(clip_frames, key_places)[0]
    seen = widen(own_clip[:, None, :] == key_clip[:, :, None])
    prompt_flat = prompt.reshape(-1, prompt.shape[2])
    rows = cross_memory.shape[0]
    place = jnp.arange(prompt.shape[2], dtype=jnp.int32)
    place = place // rows * share + place % rows
    places = jnp.arange(width, dtype=jnp.int32)[None, :]
    prompt_spread = [
        narrow(dot(prompt_flat, (place[:, None] + j * (share // 2) == places).astype(jnp.bfloat16)))
        for j in range(2)
    ]
    prompt_spread = jnp.concatenate(prompt_spread, 0)
    turn_tables = spin_tables(own_offset, 1.0)
    back_tables = spin_tables(own_offset, -1.0)

    def turn_rows(rows, matrix):
        return narrow(dot(rows, matrix))

    turned_memory = turn_rows(
        prompt_flat, order_matrix(prompt.shape[2], cross_memory.shape[0], tail_orders[2], me)
    )
    turned_memory = jnp.concatenate([turned_memory] * seq_count, 0)
    matrices = [order_matrix(width, share, order, me) for order in tail_orders]
    upstream_tokens = upstream.reshape(token_count, width)
    grad_drop_bias = jnp.sum(widen(upstream_tokens), 0, keepdims=True)
    early = [prompt_spread, turned_memory, seen, grad_drop_bias]
    early = early + matrices + list(turn_tables) + list(back_tables)

    known = [0]
    for mask in batch_masks[:1:-1]:
        group_one = jnp.concatenate([group_one, hop(group_one, mask)], 0)
        known = known + [old ^ mask for old in known]
    known = [known + [old ^ mask for old in known] for mask in (x_mask, y_mask)]
    group_one, group_two, *early = lax.optimization_barrier((group_one, group_two, *early))
    prompt_spread, turned_memory, seen, grad_drop_bias = early[:4]
    matrices, turn_tables, back_tables = early[4:7], early[7:9], early[9:]

    def pieces_of(columns, others):
        halves = []
        for h in range(2):
            have = known[h]
            pieces = [(columns[h], have), (others[h], [old ^ (y_mask, x_mask)[h] for old in have])]
            halves.append(pieces)
        return halves

    def add_core(halves, got):
        for h in range(2):
            halves[h] = halves[h] + [
                (piece, [old ^ seq_masks[0] for old in have])
                for piece, (_, have) in zip(got[h], halves[h])
            ]
            for mask in seq_masks[1:]:
                halves[h] = halves[h] + [
                    (hop(piece, mask), [old ^ mask for old in have]) for piece, have in halves[h]
                ]
        return halves

    core = seq_masks[0]
    traffic = Traffic()
    feed_parts = [feed_sent[2 * units :], feed_sent[: 2 * units]]
    ones = (group_one[:, : 128 + split], group_one[:, 128 + split :])
    group_two = gather(group_two, batch_masks[:2:-1])
    got = volley(ones, [x_mask, y_mask])
    ones = tuple(jnp.concatenate(pair, 0) for pair in zip(ones, got))
    got = volley(
        ones + (feed_parts[0], group_two, ones[0]),
        [y_mask, x_mask, far[0], batch_masks[2], core],
    )
    feed_got = [got[2]]
    group_two = jnp.concatenate([group_two, got[3]], 0)
    twos = (group_two[:, : 2 * width], group_two[:, 2 * width :])
    got_one = got[:2] + got[4:]
    got = volley(
        twos + (ones[1],) + got_one[:2], [x_mask, y_mask, core, core, core]
    )
    got_one = got_one + got[2:]
    twos = tuple(jnp.concatenate(pair, 0) for pair in zip(twos, got))
    halves = pieces_of(ones, got_one[:2])
    halves = add_core(halves, ((got_one[2], got_one[4]), (got_one[3], got_one[5])))
    new = {
        "two": once(twos + twos[:1], [y_mask, x_mask, core]),
        "feed": once(feed_parts[1:], far[:1]),
    }
    pieces = traffic.turn([piece for have in halves for piece, _ in have], lambda done: new)
    count = len(pieces) // 2
    halves = [
        [(piece, have) for piece, (_, have) in zip(pieces[h * count : (h + 1) * count], halves[h])]
        for h in range(2)
    ]
    packed, triple_low = settle(
        halves, [[(0, 0, 0, 128), (128, 1, 0, split)], [(0, 1, split, split)]], [128, 3 * width], me
    )
    packed = dot_t(jnp.eye(8, 128, dtype=jnp.bfloat16), packed)
    gain_one, shift_one, gain_two, shift_two, gain_three, shift_three, drop_bias = [
        packed[j : j + 1] for j in range(7)
    ]

    def cut_tokens(value):
        return [value[cuts[p] : cuts[p + 1]] for p in range(3)]

    def token_pairs(value):
        pairs = []
        for p in range(3):
            first, last = near_count * cuts[p], near_count * cuts[p + 1]
            middle = (first + last) // 2
            pairs.append((narrow(value[first:middle]), narrow(value[middle:last])))
        return pairs

    inputs = frames.reshape(token_count, width)
    query, pairs, normed_one, inverse_one, hidden_one = project(
        inputs, gain_one, shift_one, triple_low, turn_tables, scale
    )
    query, normed_one = traffic.turn(
        (query, normed_one),
        lambda done: {"pairs": double_list(pairs, seq_masks)},
        step=[],
    )
    for _ in seq_masks:
        (query,) = traffic.turn((query,), step=["pairs"])
    pairs = traffic.done["pairs"]
    self_mixed = attend(query, pairs, seen, row_count)

    def started(done):
        return {
            "last": once((twos[1],) + done["two"][:2], [core] * 3),
            "up": double_each(cut_tokens(upstream_tokens), near_orders),
        }

    self_mixed, *feed_all = traffic.turn([self_mixed] + feed_parts + feed_got, started)
    got_two = traffic.done["two"]
    feed_all.append(traffic.done["feed"][0])
    far_count = len(masks_of(far))
    unit_count = far_count * units
    drop_low, value_low, gate_low = [
        jnp.concatenate([part[rows : rows + units] for part in feed_all[p::2]], 0)
        for p, rows in ((0, 0), (1, 0), (1, units))
    ]
    biases = [part[units : units + 2, :units] for part in feed_all[::2]]
    biases = jnp.concatenate(biases, 1)
    for mask in far[1:]:
        drop_low, value_low, gate_low = [
            jnp.concatenate([low, hop(low, mask)], 0) for low in (drop_low, value_low, gate_low)
        ]
        biases = jnp.concatenate([biases, hop(biases, mask)], 1)
    value_bias, gate_bias = widen(biases[:1]), widen(biases[1:])
    self_mixed, value_low, gate_low, drop_low, value_bias, gate_bias = traffic.turn(
        (self_mixed, value_low, gate_low, drop_low, value_bias, gate_bias),
        lambda done: {"mixed": double_list(self_mixed, seq_masks)},
    )
    got = traffic.done["last"]
    halves = add_core(
        pieces_of(twos, got_two[:2]), ((got_two[2], got[1]), (got[0], got[2]))
    )
    lows = settle(
        halves,
        [[(0, 0, 0, width), (width, 1, 0, width)], [(0, 2, 0, width), (width, 3, 0, width)]],
        [width] * 4,
        me,
    )
    self_low, ask_low, cross_low, memory_low, self_mixed = traffic.turn(
        (*lows, self_mixed), lambda done: {"hidden": double_list(hidden_one, seq_masks)}
    )
    after_self, normed_two, inverse_two, hidden_two, asking = ahead(
        self_mixed, self_low, inputs, gain_two, shift_two, ask_low, scale
    )
    asking, prompt_spread = lax.optimization_barrier((asking, prompt_spread))
    memory = multiply(prompt_spread, memory_low)
    cross_mixed = attend(asking, [memory], None, row_count)
    (cross_mixed,) = traffic.turn(
        (cross_mixed,), lambda done: {"asked": double_list(hidden_two, seq_masks)}
    )
    after_cross, normed_three, inverse_three, hidden_three = ahead(
        cross_mixed, cross_low, after_self, gain_three, shift_three
    )

    hidden_three, cross_mixed = traffic.turn(
        (hidden_three, cross_mixed),
        lambda done: {
            "rows": double_each(cut_tokens(hidden_three), near_orders),
            "crossed": double_list(cross_mixed, seq_masks),
        },
        step=["asked"],
    )
    traffic.turn((), step=["rows", "crossed"])
    up = jnp.concatenate(traffic.done["up"], 0)
    traffic.turn((), lambda done: {"ups": double_list(up, seq_masks)}, step=["rows"])
    for _ in seq_masks[1:]:
        traffic.turn((), step=["asked", "crossed", "hidden", "mixed", "ups"])
    hidden_all, mixed_all, asked_all, cross_all = [
        jnp.concatenate(traffic.done[name], 0) for name in ("hidden", "mixed", "asked", "crossed")
    ]
    turned_triple = [turn_rows(hidden_all, matrix) for matrix in matrices]
    turned_cross = turn_rows(cross_all, matrices[0])
    turned_ask = turn_rows(asked_all, matrices[1])

    def rows_there(done):
        if "rows" not in done:
            return {}
        done["rows"] = jnp.concatenate(done["rows"], 0)
        return {"all": double_list(done["rows"], seq_masks)}

    turned_cross, turned_ask, mixed_all, *turned_triple = traffic.turn(
        [turned_cross, turned_ask, mixed_all] + turned_triple, rows_there
    )
    while "rows" in traffic.flows:
        traffic.turn((), rows_there)
    ups = traffic.done["ups"]
    lows = (value_low, gate_low, drop_low, value_bias, gate_bias)
    results = [feed_block(traffic.done["rows"], ups[0], *lows)]
    results[0] = traffic.turn(results[0])
    for _ in seq_masks[1:]:
        traffic.turn((), step=["all"])
    feed_rows = traffic.done["all"]
    for rows, up in zip(feed_rows[1:], ups[1:]):
        results.append(feed_block(rows, up, *lows))
    middles, value_grads, gate_grads, back_sums, term_sums = [list(item) for item in zip(*results)]

    def back_flow():
        value = yield from halve_list(back_sums, seq_masks)
        return (yield from halve_pairs(token_pairs(value), near_orders))

    blocks = len(feed_rows)
    tied = traffic.turn(middles + value_grads + gate_grads, lambda done: {"back": back_flow()})
    middles, value_grads, gate_grads = tied[:blocks], tied[blocks : 2 * blocks], tied[2 * blocks :]
    drop_grad = unit_grad(middles, ups, False)[0]
    tied = traffic.turn((drop_grad, *value_grads, *gate_grads))
    for _ in seq_masks[1:]:
        tied = traffic.turn(tied)
    drop_grad, value_grads, gate_grads = tied[0], tied[1 : 1 + blocks], tied[1 + blocks :]
    value_grad, value_bias_grad = unit_grad(value_grads, feed_rows, True)
    gate_grad, gate_bias_grad = unit_grad(gate_grads, feed_rows, True)

    def unit_blocks(grad):
        return [grad[k * units : (k + 1) * units] for k in range(far_count)]

    bias_grads = [
        narrow(
            jnp.pad(
                jnp.concatenate(
                    [bias[:, k * units : (k + 1) * units] for bias in (value_bias_grad, gate_bias_grad)], 0
                ),
                ((0, 14), (0, width - units)),
            )
        )
        for k in range(far_count)
    ]

    def unit_flow(p):
        blocks = unit_blocks((drop_grad, drop_grad, value_grad, value_grad, gate_grad)[p])
        if p == 4:
            blocks = [jnp.concatenate(pair, 0) for pair in zip(blocks, bias_grads)]
            return halve_rows(blocks, 0, units + 16, far)
        half = units // 2
        return halve_rows(blocks, p % 2 * half, (p % 2 + 1) * half, far)

    value_grad, gate_grad, drop_grad, mixed_all = traffic.turn(
        (value_grad, gate_grad, drop_grad, mixed_all),
        lambda done: {"term": halve_list(term_sums, seq_masks), "unit0": unit_flow(0)},
    )
    turned_self = [turn_rows(mixed_all, matrix) for matrix in matrices]

    (*turned_self,) = traffic.turn(turned_self)
    for _ in seq_masks[1:]:
        traffic.turn((), step=["term"])
    while "back" in traffic.flows:
        traffic.turn((), step=["back", "term"])

    while "back" in traffic.flows:
        unit_sums = list(traffic.turn(unit_sums, step=["back", "term"]))
    feed_back = jnp.concatenate(traffic.done["back"], 0)
    (feed_back,) = traffic.turn(
        (feed_back,),
        lambda done: {
            "term_near": halve_pairs(token_pairs(done["term"]), near_orders),
        },
    )
    cross_out_grad, grad_gain_three, grad_shift_three, cross_branch, cross_mixed_grad = back(
        feed_back, None, upstream_tokens, normed_three, inverse_three, gain_three, cross_low
    )

    def weight_pair(turned, *grads):
        half = turned.shape[1] // 2
        pair = []
        for columns in (turned[:, :half], turned[:, half:]):
            sums = [narrow(tdot(columns, grad)) for grad in grads]
            if len(grads) > 1:
                rows = cross_memory.shape[0]
                sums = [
                    jnp.pad(part.reshape(-1, rows, width), ((0, 0), (0, share // 2 - rows), (0, 0)))
                    for part in sums
                ]
                sums = [jnp.concatenate(sums, 1).reshape(-1, width)]
            pair.append(sums[0])
        return tuple(pair)

    (cross_mixed_grad,) = traffic.turn(
        (cross_mixed_grad,),
        lambda done: {"dc": double_list(cross_branch, seq_masks), "unit1": unit_flow(1)},
    )
    asking_grad, memory_grad = attend_back(
        asking, [memory], None, cross_mixed_grad, None, row_count, scale
    )
    asking_grad, memory_grad = traffic.turn(
        (asking_grad, memory_grad),
        lambda done: {
            "dq": double_list(asking_grad, seq_masks),
            "dm": double_list(memory_grad, seq_masks),
        },
    )
    for _ in seq_masks[1:]:
        traffic.turn((), step=["dc"])
    self_out_grad, grad_gain_two, grad_shift_two, self_branch, self_mixed_grad = back(
        asking_grad, ask_low, cross_out_grad, normed_two, inverse_two, gain_two, self_low
    )
    (self_mixed_grad,) = traffic.turn(
        (self_mixed_grad,),
        lambda done: {"da": double_list(self_branch, seq_masks), "unit2": unit_flow(2)},
    )
    for _ in seq_masks[1:]:
        traffic.turn((), step=["dq", "dm", "da"])
    cross_pair = weight_pair(turned_cross, jnp.concatenate(traffic.done["dc"], 0))
    layer_output = narrow(
        after_cross + jnp.concatenate(traffic.done["term_near"], 0) + drop_bias
    )
    ask_pair = weight_pair(turned_ask, jnp.concatenate(traffic.done["dq"], 0))
    memory_all = traffic.done["dm"]
    half = memory_grad.shape[0] // 2
    memory_pair = weight_pair(
        turned_memory,
        jnp.concatenate([part[:half] for part in memory_all], 0),
        jnp.concatenate([part[half:] for part in memory_all], 0),
    )
    self_mixed_grad, layer_output = traffic.turn(
        (self_mixed_grad, layer_output),
        lambda done: {
            "first": halve_pairs([cross_pair, ask_pair, memory_pair], tail_orders),
        },
    )
    query_back, pair_grad = attend_back(
        query, pairs, seen, self_mixed_grad, back_tables, row_count, scale
    )

    def shed_frames(value):
        for mask in reversed(seq_masks):
            half = value.shape[0] // 2
            (sent,) = yield (value[half:],)
            (got,) = yield hops((sent,), (mask,))
            if mask > seq_masks[0]:
                value = narrow(widen(value[:half]) + widen(got))
        return value, got

    (query_back,) = traffic.turn((query_back,), lambda done: {"pair": shed_frames(pair_grad)}, step=[])
    for _ in seq_masks:
        (query_back,) = traffic.turn((query_back,), step=["pair"])
    triple_back = spin_backward(query_back, *traffic.done["pair"], *back_tables)
    (triple_back,) = traffic.turn(
        (triple_back,), lambda done: {"dt": double_list(triple_back, seq_masks)}
    )
    frame_grad, grad_gain_one, grad_shift_one = back(
        triple_back, triple_low, self_out_grad, normed_one, inverse_one, gain_one
    )
    branch_all = jnp.concatenate(traffic.done["da"], 0)
    third = width // 3
    frame_grad, *sums = traffic.turn(
        (
            frame_grad,
            grad_gain_one,
            grad_shift_one,
            grad_gain_two,
            grad_shift_two,
            grad_gain_three,
            grad_shift_three,
        )
    )
    sums = jnp.concatenate(sums + [grad_drop_bias], 0).reshape(7, device_count, share)
    sums = jnp.transpose(sums, (1, 0, 2)).reshape(device_count, 7 * share)
    sums = jnp.pad(sums, ((0, 0), (0, 1024 - 7 * share)))
    tail_masks = masks_of(tail_orders[0] + seq_masks)
    sums = jnp.take(sums, me ^ jnp.asarray(np.array(tail_masks, np.int32)), axis=0)
    sums = sums.reshape(device_count, 8, 128)
    for _ in seq_masks[1:]:
        traffic.turn((), step=["dt"])
    triple_all = jnp.concatenate(traffic.done["dt"], 0)
    triple_pairs = [
        tuple(
            weight_sums(
                [turned_triple[p], turned_self[p]],
                [
                    triple_all[:, p * width : (p + 1) * width],
                    branch_all[:, p * third : (p + 1) * third],
                ],
            )
        )
        for p in range(3)
    ]
    tied = traffic.turn(
        sum(triple_pairs, ()), lambda done: {"sums": halve_list_rows(sums, seq_masks)}
    )
    triple_pairs = [tied[2 * p : 2 * p + 2] for p in range(3)]
    while "first" in traffic.flows or "sums" in traffic.flows:
        traffic.turn(())
    sums = traffic.done["sums"]
    half = sums.shape[0] // 2
    traffic.turn(
        (),
        lambda done: {
            "tail": halve_pairs(
                triple_pairs + [(sums[:half], sums[half:])], tail_orders + [tail_orders[0]]
            ),
            "unit4": unit_flow(4),
        },
    )
    traffic.turn((), lambda done: {"unit3": unit_flow(3)})
    while traffic.flows:
        traffic.turn(())
    parts = traffic.done["tail"]
    grad_cross, grad_ask, grad_memory = traffic.done["first"]
    grad_self = jnp.concatenate([part[:, width:] for part in parts[:3]], 1)
    drop_sums = jnp.concatenate([traffic.done[name] for name in UNITS[:2]], 0)
    value_sums = jnp.concatenate([traffic.done[name] for name in UNITS[2:4]], 0)
    gate_sums = traffic.done[UNITS[4]]
    grad_triple = jnp.concatenate([part[:, :width] for part in parts[:3]], 1)
    sums = parts[3].reshape(1024)[: 7 * share].reshape(7, share)
    grad_memory = grad_memory.reshape(2, share // 2, width)[:, : cross_memory.shape[0]]
    grad_memory = jnp.concatenate([grad_memory[0], grad_memory[1]], 1)
    grad_lift = jnp.stack([value_sums, gate_sums[:units]], 0)
    grad_drop = drop_sums
    grad_lift_bias = gate_sums[units : units + 2, :units]
    shape = frames.shape
    return (
        layer_output.reshape(shape),
        frame_grad.reshape(shape),
        sums[0],
        sums[1],
        grad_triple,
        grad_self,
        sums[2],
        sums[3],
        grad_ask,
        grad_memory,
        grad_cross,
        sums[4],
        sums[5],
        grad_lift,
        grad_lift_bias,
        grad_drop,
        sums[6],
    )


def solution(mesh):
    both = P(AX)
    wide = P(AX, None)
    rows = P(B, S, None)
    units = P(None, AX, None)
    in_specs = (
        rows,
        P(B, None, None),
        P(B, None),
        rows,
        both,
        both,
        wide,
        wide,
        both,
        both,
        wide,
        wide,
        wide,
        both,
        both,
        units,
        P(None, AX),
        wide,
        both,
    )
    out_specs = (
        rows,
        rows,
        both,
        both,
        wide,
        wide,
        both,
        both,
        wide,
        wide,
        wide,
        both,
        both,
        units,
        P(None, AX),
        wide,
        both,
    )
    return jax.shard_map(local, mesh=mesh, in_specs=in_specs, out_specs=out_specs, check_vma=False)
```

```python
import jax
import jax.numpy as jnp
import numpy as np
from jax import lax
from jax.experimental import pallas as pl
from jax.experimental.pallas import tpu as pltpu
from jax.sharding import PartitionSpec as P

HEAD_DIM = 64
LANES = 512
UNITS = ["unit0", "unit1", "unit2", "unit3", "unit4"]
EPS = 1e-05
NEG = -1e30
B = "batch"
S = "seq"
AX = (B, S)


def narrow(value):
    return value.astype(jnp.bfloat16)


def widen(value):
    return value.astype(jnp.float32)


def mult(left, right, form):
    return jnp.einsum(form, left, right, preferred_element_type=jnp.float32)


def dot(left, right):
    return lax.dot_general(left, right, (((1,), (0,)), ((), ())), preferred_element_type=jnp.float32)


def dot_t(left, right):
    return lax.dot_general(left, right, (((1,), (1,)), ((), ())), preferred_element_type=jnp.float32)


def tdot(left, right):
    return lax.dot_general(left, right, (((0,), (0,)), ((), ())), preferred_element_type=jnp.float32)


def standardize(values):
    center = values - jnp.mean(values, -1, keepdims=True)
    inverse = lax.rsqrt(jnp.mean(center * center, -1, keepdims=True) + EPS)
    return (center * inverse, inverse)


def norm_back(incoming, normed, inverse, gain):
    scaled = incoming * gain
    inner = (
        scaled
        - jnp.mean(scaled, -1, keepdims=True)
        - normed * jnp.mean(scaled * normed, -1, keepdims=True)
    )
    return (
        inner * inverse,
        jnp.sum(incoming * normed, 0, keepdims=True),
        jnp.sum(incoming, 0, keepdims=True),
    )


def clip_tables(lengths, places):
    ends = jnp.cumsum(lengths, 1)
    later = places[None, :, None] >= ends[:, None, :]
    ident = jnp.sum(later.astype(jnp.int32), 2)
    starts = jnp.max(jnp.where(later, ends[:, None, :], 0), 2)
    return (ident, places[None, :] - starts)


def softmax_back(probs, prob_grad):
    return probs * (prob_grad - jnp.sum(probs * prob_grad, 0, keepdims=True))


def hop(value, mask):
    count = lax.axis_size(B) * lax.axis_size(S)
    return lax.ppermute(value, AX, [(i, i ^ mask) for i in range(count)])


def volley(values, masks):
    values = lax.optimization_barrier(tuple(values))
    return lax.optimization_barrier(tuple(hop(value, mask) for value, mask in zip(values, masks)))


def masks_of(order):
    masks = [0]
    for mask in order:
        masks = masks + [old ^ mask for old in masks]
    return masks


def gather(value, order):
    for mask in order:
        value = jnp.concatenate([value, hop(value, mask)], 0)
    return value


def settle(halves, targets, widths, me):
    pieces = [(h, piece, have) for h in range(len(halves)) for piece, have in halves[h]]
    total = sum(len(have) for h, piece, have in pieces if h == 0)
    rows = pieces[0][1].shape[0] // len(pieces[0][2])
    if rows % 16:
        outs = [[] for _ in widths]
        for h in range(len(halves)):
            have = sum([have for _, have in halves[h]], [])
            table = np.zeros(total, np.int32)
            table[np.array(have)] = np.arange(total)
            place = jnp.asarray(table)[me ^ jnp.arange(total, dtype=jnp.int32)]
            blocks = jnp.concatenate([piece for piece, _ in halves[h]], 0).reshape(total, rows, -1)
            blocks = jnp.take(blocks, place, axis=0).reshape(total * rows, -1)
            for source, out, _, count in targets[h]:
                outs[out].append(blocks[:, source : source + count])
        return [jnp.concatenate(out, 1) for out in outs]

    def body(me_ref, *refs):
        ins = refs[: len(pieces)]
        outs = refs[len(pieces) : len(pieces) + len(widths)]
        held = refs[len(pieces) + len(widths) : -2]
        in_sems, out_sems = refs[-2:]
        loads = []
        for i in range(len(pieces)):
            load = pltpu.make_async_copy(ins[i], held[i], in_sems.at[i])
            load.start()
            loads.append(load)
        stores = []
        for i, (h, _, have) in enumerate(pieces):
            loads[i].wait()
            for j, mask in enumerate(have):
                start = pl.multiple_of((me_ref[0] ^ mask) * rows, rows)
                for source, out, column, count in targets[h]:
                    store = pltpu.make_async_copy(
                        held[i].at[pl.ds(j * rows, rows), pl.ds(source, count)],
                        outs[out].at[pl.ds(start, rows), pl.ds(column, count)],
                        out_sems.at[len(stores)],
                    )
                    store.start()
                    stores.append(store)
        for store in stores:
            store.wait()

    count = sum(len(have) * len(targets[h]) for h, _, have in pieces)
    size = 2 * sum(piece.size for _, piece, _ in pieces)
    return pl.pallas_call(
        body,
        out_shape=[jax.ShapeDtypeStruct((total * rows, width), jnp.bfloat16) for width in widths],
        in_specs=[pl.BlockSpec(memory_space=pltpu.SMEM)]
        + [pl.BlockSpec(memory_space=pl.ANY)] * len(pieces),
        out_specs=[pl.BlockSpec(memory_space=pltpu.HBM)] * len(widths),
        scratch_shapes=[pltpu.VMEM(piece.shape, jnp.bfloat16) for _, piece, _ in pieces]
        + [pltpu.SemaphoreType.DMA((len(pieces),)), pltpu.SemaphoreType.DMA((count,))],
        compiler_params=pltpu.CompilerParams(vmem_limit_bytes=size + (2 << 20)),
        cost_estimate=pl.CostEstimate(flops=0, bytes_accessed=size // 16, transcendentals=0),
    )(me.reshape(1), *[piece for _, piece, _ in pieces])


class Traffic:
    def __init__(self):
        self.flows = {}
        self.done = {}
        self.count = {}

    def turn(self, outs, new=None, step=None):
        names = list(self.flows) if step is None else [n for n in step if n in self.flows]
        gots = sum([self.flows[name][1] for name in names], ())
        tied = lax.optimization_barrier(gots + tuple(outs))
        outs = tied[len(gots) :]
        started = []
        for name in names:
            flow, got = self.flows.pop(name)
            got, tied = tied[: len(got)], tied[len(got) :]
            try:
                started.append((name, flow, flow.send(got)))
            except StopIteration as end:
                self.done[name] = end.value
        if new is not None:
            flows = new(self.done)
            for name, flow in ((name, flow) for name, flow in flows.items() if flow is not None):
                started.append((name, flow, next(flow)))
        sents = sum([sent for _, _, sent in started], ())
        tied = lax.optimization_barrier(sents + outs)
        for name, flow, sent in started:
            self.count[name] = self.count.get(name, 0) + 1
            self.flows[name] = (flow, flow.send(tied[: len(sent)]))
            tied = tied[len(sent) :]
        return tied


def hops(values, masks):
    return tuple(hop(value, mask) for value, mask in zip(values, masks))


def once(values, masks):
    values = yield tuple(values)
    return (yield hops(values, masks))


def halve_pairs(pairs, orders):
    for step in list(zip(*orders))[::-1]:
        sent = yield tuple(sent for _, sent in pairs)
        got = yield hops(sent, step)
        sums = [(kept, part) for (kept, _), part in zip(pairs, got)]
        pairs = []
        for kept, part in sums:
            half = kept.shape[0] // 2
            pair = [widen(kept[cut]) + widen(part[cut]) for cut in (slice(half), slice(half, None))]
            pairs.append(pair if kept.ndim == 3 else [narrow(item) for item in pair])
    return [widen(kept) + widen(part) for kept, part in sums]


def halve_list(blocks, masks):
    for mask in reversed(masks):
        half = len(blocks) // 2
        sent = yield tuple(narrow(block) for block in blocks[half:])
        got = yield hops(sent, (mask,) * half)
        blocks = [widen(a) + widen(b) for a, b in zip(blocks[:half], got)]
    return blocks[0]


def halve_rows(blocks, first, last, masks):
    for mask in reversed(masks):
        half = len(blocks) // 2
        sent = yield tuple(narrow(block[first:last]) for block in blocks[half:])
        got = yield hops(sent, (mask,) * half)
        blocks = [widen(a[first:last]) + widen(b) for a, b in zip(blocks[:half], got)]
        first, last = 0, last - first
    return blocks[0]


def double_each(parts, orders):
    for step in zip(*orders):
        parts = yield tuple(parts)
        got = yield hops(parts, step)
        pairs = list(zip(parts, got))
        parts = [jnp.concatenate(pair, 0) for pair in pairs]
    return sum(pairs, ())


def double_list(value, masks):
    blocks = (value,)
    for mask in masks:
        blocks = yield blocks
        got = yield hops(blocks, (mask,) * len(blocks))
        blocks = tuple(blocks) + tuple(got)
    return blocks


def spin(value, cosine, sine):
    lane = lax.broadcasted_iota(jnp.int32, value.shape, 1)
    other = jnp.where(lane % 64 < 32, pltpu.roll(value, 96, 1), pltpu.roll(value, 32, 1))
    return value * cosine + other * sine


def spin_tables(offsets, sign):
    half = HEAD_DIM // 2
    freq = 10000.0 ** (-jnp.arange(half, dtype=jnp.float32) / half)
    angle = offsets.astype(jnp.float32).reshape(-1, 1) * freq
    cosine = jnp.cos(angle)
    sine = sign * jnp.sin(angle)
    return (jnp.concatenate([cosine] * 4, 1), jnp.concatenate([-sine, sine, -sine, sine], 1))


def hint():
    return pl.CostEstimate(flops=1 << 20, bytes_accessed=1 << 20, transcendentals=0)


def whole(array):
    return pl.BlockSpec(array.shape, lambda i: (0,) * array.ndim)


def like(shape, dtype=jnp.float32):
    return jax.ShapeDtypeStruct(shape, dtype)


def room(mebibytes):
    return pltpu.CompilerParams(vmem_limit_bytes=mebibytes << 20)


def project(inputs, gain, shift, weight, tables, scale):
    rows, width = inputs.shape
    block = width

    def body(in_ref, gain_ref, shift_ref, cos_ref, sin_ref, weight_ref, *outs):
        query_ref, pair_ref, normed_ref, inverse_ref, hidden_ref = outs
        step = pl.program_id(0)

        @pl.when(step == 0)
        def _():
            normed, inverse = standardize(widen(in_ref[...]))
            normed_ref[...] = normed
            inverse_ref[...] = inverse
            hidden_ref[...] = narrow(normed * gain_ref[...] + shift_ref[...])

        value = dot(hidden_ref[...], weight_ref[...])

        def turned(factor):
            parts = [
                spin(value[:, j : j + 128], cos_ref[...], sin_ref[...]) for j in range(0, block, 128)
            ]
            return [narrow(part * factor) for part in parts]

        @pl.when(step == 0)
        def _():
            for j, part in enumerate(turned(scale)):
                query_ref[:, 128 * j : 128 * j + 128] = part

        @pl.when(step == 1)
        def _():
            for j, part in enumerate(turned(1.0)):
                pair_ref[:, 128 * j : 128 * j + 128] = part

        @pl.when(step == 2)
        def _():
            pair_ref[...] = narrow(value)

    return pl.pallas_call(
        body,
        grid=(3,),
        out_shape=[
            like((rows, width), jnp.bfloat16),
            like((2 * rows, width), jnp.bfloat16),
            like((rows, width)),
            like((rows, 1)),
            like((rows, width), jnp.bfloat16),
        ],
        in_specs=[
            whole(inputs),
            whole(gain),
            whole(shift),
            whole(tables[0]),
            whole(tables[1]),
            pl.BlockSpec((width, block), lambda i: (0, i)),
        ],
        out_specs=[
            pl.BlockSpec((rows, block), lambda i: (0, 0)),
            pl.BlockSpec((rows, block), lambda i: (jnp.maximum(i - 1, 0), 0)),
            pl.BlockSpec((rows, width), lambda i: (0, 0)),
            pl.BlockSpec((rows, 1), lambda i: (0, 0)),
            pl.BlockSpec((rows, width), lambda i: (0, 0)),
        ],
        compiler_params=room(22),
        cost_estimate=hint(),
    )(inputs, gain, shift, *tables, weight)


def ahead(mixed, low, before, gain, shift, ask=None, scale=1.0):
    rows, width = before.shape
    steps = width // LANES

    def body(mixed_ref, before_ref, gain_ref, shift_ref, *refs):
        low_ref, refs = refs[0], refs[1:]
        if ask is not None:
            ask_ref, refs = refs[0], refs[1:]
        sum_ref, normed_ref, inverse_ref, hidden_ref = refs[:4]
        step = pl.program_id(0)

        @pl.when(step < steps)
        def _():
            lanes = pl.ds(pl.multiple_of(step * LANES, LANES), LANES)
            sum_ref[:, lanes] = widen(before_ref[:, lanes]) + dot(mixed_ref[...], low_ref[...])

        @pl.when(step == steps - 1)
        def _():
            normed, inverse = standardize(sum_ref[...])
            normed_ref[...] = normed
            inverse_ref[...] = inverse
            hidden_ref[...] = narrow(normed * gain_ref[...] + shift_ref[...])

        if ask is not None:

            @pl.when(step >= steps)
            def _():
                refs[4][...] = narrow(dot(hidden_ref[...], ask_ref[...]) * scale)

    full = pl.BlockSpec((rows, width), lambda i: (0, 0))
    args = (mixed, before, gain, shift, low)
    specs = [whole(mixed), whole(before), whole(gain), whole(shift)]
    specs.append(pl.BlockSpec((width, LANES), lambda i: (0, jnp.minimum(i, steps - 1))))
    shapes = [
        like((rows, width)),
        like((rows, width)),
        like((rows, 1)),
        like((rows, width), jnp.bfloat16),
    ]
    outs = [full, full, pl.BlockSpec((rows, 1), lambda i: (0, 0)), full]
    if ask is not None:
        args = args + (ask,)
        specs.append(pl.BlockSpec((width, LANES), lambda i: (0, jnp.maximum(i - steps, 0))))
        shapes.append(like((rows, width), jnp.bfloat16))
        outs.append(pl.BlockSpec((rows, LANES), lambda i: (0, jnp.maximum(i - steps, 0))))
    return pl.pallas_call(
        body,
        grid=(steps if ask is None else 2 * steps,),
        out_shape=shapes,
        in_specs=specs,
        out_specs=outs,
        compiler_params=room(16),
        cost_estimate=hint(),
    )(*args)


def back(incoming, low, grads, normed, inverse, gain, out=None, place=0):
    rows, width = grads.shape
    block = LANES
    first = 0 if low is None else width // block
    last = 0 if out is None else width // LANES
    norm_step = max(first - 1, 0)

    def body(in_ref, grad_ref, normed_ref, inverse_ref, gain_ref, *refs):
        if low is not None:
            low_ref, refs = refs[0], refs[1:]
        if out is not None:
            out_ref, refs = refs[0], refs[1:]
        sum_ref, gain_grad_ref, shift_grad_ref = refs[:3]
        held_ref = refs[-1]
        step = pl.program_id(0)
        if low is not None:

            @pl.when(step < first)
            def _():
                lanes = pl.ds(pl.multiple_of(step * block, block), block)
                held_ref[:, lanes] = dot_t(in_ref[...], low_ref[...])

        @pl.when(step == norm_step)
        def _():
            value = in_ref[...] if low is None else held_ref[...]
            inner, gain_grad, shift_grad = norm_back(
                value, normed_ref[...], inverse_ref[...], gain_ref[...]
            )
            total = widen(grad_ref[...]) + inner
            sum_ref[...] = total
            gain_grad_ref[...] = gain_grad
            shift_grad_ref[...] = shift_grad
            if out is not None:
                refs[3][...] = narrow(total)

        if out is not None:

            @pl.when(step >= first)
            def _():
                refs[4][...] = narrow(dot_t(refs[3][...], out_ref[...]))

    full = pl.BlockSpec((rows, width), lambda i: (0, 0))
    line = pl.BlockSpec((1, width), lambda i: (0, 0))
    args = (incoming, grads, normed, inverse, gain)
    specs = [whole(array) for array in args]
    specs[0] = pl.BlockSpec((rows, incoming.shape[1]), lambda i: (place, 0))
    if low is not None:
        args = args + (low,)
        specs.append(pl.BlockSpec((block, low.shape[1]), lambda i: (jnp.minimum(i, first - 1), 0)))
    shapes = [like((rows, width)), like((1, width)), like((1, width))]
    outs = [full, line, line]
    if out is not None:
        args = args + (out,)
        specs.append(pl.BlockSpec((LANES, width), lambda i: (jnp.maximum(i - first, 0), 0)))
        shapes = shapes + [like((rows, width), jnp.bfloat16)] * 2
        outs = outs + [full, pl.BlockSpec((rows, LANES), lambda i: (0, jnp.maximum(i - first, 0)))]
    return pl.pallas_call(
        body,
        grid=(first + last,),
        out_shape=shapes,
        in_specs=specs,
        out_specs=outs,
        scratch_shapes=[pltpu.VMEM((rows, width), jnp.float32)],
        compiler_params=room(24),
        cost_estimate=hint(),
    )(*args)


def feed_block(rows, ups, value_low, gate_low, drop_low, value_bias, gate_bias):
    count, width = rows.shape
    units = drop_low.shape[0]
    block = min(count, 256)

    def body(row_ref, up_ref, value_ref, gate_ref, drop_ref, value_bias_ref, gate_bias_ref, *outs):
        middle_ref, value_out, gate_out, back_ref = outs
        middle_grad = widen(narrow(dot_t(up_ref[...], drop_ref[...])))
        value = dot_t(row_ref[...], value_ref[...]) + value_bias_ref[...]
        gate = dot_t(row_ref[...], gate_ref[...]) + gate_bias_ref[...]
        sigma = jax.nn.sigmoid(gate)
        middle = narrow(value * gate * sigma)
        value_grad = narrow(middle_grad * gate * sigma)
        gate_grad = narrow(middle_grad * value * sigma * (1.0 + gate * (1.0 - sigma)))
        middle_ref[...] = middle
        value_out[...] = value_grad
        gate_out[...] = gate_grad
        back_ref[...] = narrow(dot(value_grad, value_ref[...]) + dot(gate_grad, gate_ref[...]))

    wide = pl.BlockSpec((block, width), lambda i: (i, 0))
    thin = pl.BlockSpec((block, units), lambda i: (i, 0))
    args = (rows, ups, value_low, gate_low, drop_low, value_bias, gate_bias)
    return pl.pallas_call(
        body,
        grid=(count // block,),
        out_shape=[like((count, units), jnp.bfloat16)] * 3 + [like((count, width), jnp.bfloat16)],
        in_specs=[wide, wide] + [whole(array) for array in args[2:]],
        out_specs=[thin] * 3 + [wide],
        compiler_params=room(32),
        cost_estimate=hint(),
    )(*args)


def unit_grad(lefts, rights, sums):
    units = lefts[0].shape[1]
    width = rights[0].shape[1]
    count = len(lefts)
    block = 128 if units % 128 == 0 else units

    def body(*refs):
        total = 0.0
        for left, right in zip(refs[:count], refs[count : 2 * count]):
            total = total + tdot(left[...], right[...])
        refs[2 * count][...] = narrow(total)
        if sums:
            refs[2 * count + 1][...] = sum(
                jnp.sum(widen(left[...]), 0, keepdims=True) for left in refs[:count]
            )

    specs = [pl.BlockSpec((left.shape[0], block), lambda i: (0, i)) for left in lefts]
    outs = [pl.BlockSpec((block, width), lambda i: (i, 0))]
    shapes = [like((units, width), jnp.bfloat16)]
    if sums:
        outs.append(pl.BlockSpec((1, block), lambda i: (0, i)))
        shapes.append(like((1, units)))
    return pl.pallas_call(
        body,
        grid=(units // block,),
        out_shape=shapes,
        in_specs=specs + [whole(right) for right in rights],
        out_specs=outs,
        compiler_params=room(24),
        cost_estimate=hint(),
    )(*lefts, *rights)


def spin_backward(grads, got, cosine, sine):
    rows, width = got.shape[0] // 2, got.shape[1]
    last = grads.shape[0] // rows - 1

    def body(cos_ref, sin_ref, query_ref, own_ref, got_ref, out_ref):
        step = pl.program_id(0)

        @pl.when(step == 0)
        def _():
            out_ref[...] = query_ref[...]

        @pl.when(step == 1)
        def _():
            for j in range(0, width, 128):
                value = widen(own_ref[:, j : j + 128]) + widen(got_ref[:, j : j + 128])
                out_ref[:, j : j + 128] = narrow(spin(value, cos_ref[...], sin_ref[...]))

        @pl.when(step == 2)
        def _():
            out_ref[...] = narrow(widen(own_ref[...]) + widen(got_ref[...]))

    table = pl.BlockSpec((rows, 128), lambda i: (0, 0))
    part = pl.BlockSpec((rows, width), lambda i: (jnp.maximum(i - 1, 0), 0))
    return pl.pallas_call(
        body,
        grid=(3,),
        out_shape=jax.ShapeDtypeStruct((rows, 3 * width), jnp.bfloat16),
        in_specs=[table, table, pl.BlockSpec((rows, width), lambda i: (last, 0)), part, part],
        out_specs=pl.BlockSpec((rows, width), lambda i: (0, i)),
        compiler_params=room(8),
        cost_estimate=pl.CostEstimate(
            flops=1 << 20, bytes_accessed=1 << 20, transcendentals=0
        ),
    )(cosine, sine, grads, grads, got)


def two_heads(value):
    lane = lax.broadcasted_iota(jnp.int32, value.shape, 1)
    zero = jnp.zeros_like(value)
    first = jnp.where(lane < HEAD_DIM, value, zero)
    second = jnp.where(lane < HEAD_DIM, zero, value)
    return jnp.concatenate([first, second], 0)


def one_row(value):
    half = value.shape[0] // 2
    lane = lax.broadcasted_iota(jnp.int32, (half, value.shape[1]), 1)
    return jnp.where(lane < HEAD_DIM, value[:half], value[half:])


def row_probs(asked, keys, seen):
    scores = dot_t(keys, asked)
    if seen is not None:
        scores = jnp.where(jnp.concatenate([seen, seen], 1) > 0.5, scores, NEG)
    expo = jnp.exp(scores - jnp.max(scores, 0, keepdims=True))
    return expo * (1.0 / jnp.sum(expo, 0, keepdims=True))


def pair_rows(refs, part, r, lanes, row_count):
    keys = refs[0].shape[0] // (2 * row_count)
    start = (part * row_count + r) * keys
    return jnp.concatenate([ref[start : start + keys, lanes] for ref in refs], 0)


def attend(query, pairs, seen, row_count):
    tokens, width = query.shape
    frames = tokens // row_count
    count = len(pairs)

    def body(*refs):
        query_ref, pair_refs, out_ref = refs[0], refs[1 : 1 + count], refs[-1]
        for r in range(row_count):
            span = slice(r * frames, (r + 1) * frames)
            for j in range(0, LANES, 128):
                lanes = slice(j, j + 128)
                asked = two_heads(query_ref[span, lanes])
                key, value = [pair_rows(pair_refs, p, r, lanes, row_count) for p in range(2)]
                probs = row_probs(asked, key, refs[1 + count][r] if seen is not None else None)
                out_ref[span, lanes] = narrow(one_row(tdot(narrow(probs), value)))

    token_spec = pl.BlockSpec((tokens, LANES), lambda i: (0, i))
    args = (query, *pairs)
    specs = [token_spec] + [pl.BlockSpec((pairs[0].shape[0], LANES), lambda i: (0, i))] * count
    if seen is not None:
        args = args + (seen,)
        specs.append(whole(seen))
    return pl.pallas_call(
        body,
        grid=(width // LANES,),
        out_shape=like((tokens, width), jnp.bfloat16),
        in_specs=specs,
        out_specs=token_spec,
        compiler_params=room(8),
        cost_estimate=hint(),
    )(*args)


def attend_back(query, pairs, seen, grads, tables, row_count, scale):
    tokens, width = query.shape
    frames = tokens // row_count
    count = len(pairs)
    block = pairs[0].shape[0]
    keys = block // (2 * row_count)

    def body(*refs):
        query_ref, grad_ref, pair_refs = refs[0], refs[1], refs[2 : 2 + count]
        rest = refs[2 + count :]
        out_ref = refs[-1]

        def put(part, r, lanes, value):
            for b in range(count):
                start = b * block + (part * row_count + r) * keys
                out_ref[start : start + keys, lanes] = narrow(value[b * keys : (b + 1) * keys])

        for r in range(row_count):
            span = slice(r * frames, (r + 1) * frames)
            for j in range(0, LANES, 128):
                lanes = slice(j, j + 128)
                asked = two_heads(query_ref[span, lanes])
                grad = two_heads(grad_ref[span, lanes])
                key, value = [pair_rows(pair_refs, p, r, lanes, row_count) for p in range(2)]
                probs = row_probs(asked, key, rest[2][r] if seen is not None else None)
                score_grad = narrow(softmax_back(probs, dot_t(value, grad)))
                result = one_row(tdot(score_grad, key))
                if tables is not None:
                    result = spin(result, rest[0][span, :], rest[1][span, :])
                start = count * block + r * frames
                out_ref[start : start + frames, lanes] = narrow(result * scale)
                put(0, r, lanes, dot(score_grad, asked))
                put(1, r, lanes, dot(narrow(probs), grad))

    token_spec = pl.BlockSpec((tokens, LANES), lambda i: (0, i))
    specs = [token_spec] * 2 + [pl.BlockSpec((block, LANES), lambda i: (0, i))] * count
    args = (query, grads, *pairs)
    if tables is not None:
        specs = specs + [whole(table) for table in tables]
        args = args + tuple(tables)
    if seen is not None:
        specs.append(whole(seen))
        args = args + (seen,)
    return pl.pallas_call(
        body,
        grid=(width // LANES,),
        out_shape=like((count * block + tokens, width), jnp.bfloat16),
        in_specs=specs,
        out_specs=pl.BlockSpec((count * block + tokens, LANES), lambda i: (0, i)),
        compiler_params=room(12),
        cost_estimate=hint(),
    )(*args)


def multiply(left, right):
    rows, depth = left.shape
    width = right.shape[1]
    block = LANES if width % LANES == 0 else 384 if width % 384 == 0 else width

    def body(left_ref, right_ref, out_ref):
        out_ref[...] = narrow(dot(left_ref[...], right_ref[...]))

    return pl.pallas_call(
        body,
        grid=(width // block,),
        out_shape=like((rows, width), jnp.bfloat16),
        in_specs=[whole(left), pl.BlockSpec((depth, block), lambda i: (0, i))],
        out_specs=pl.BlockSpec((rows, block), lambda i: (0, i)),
        compiler_params=room(12),
        cost_estimate=hint(),
    )(left, right)


def weight_sums(lefts, rights, beside=None):
    rows = lefts[0].shape[1] // 2
    widths = [right.shape[1] for right in rights]
    count = len(lefts)
    if rows % 128:
        sums = [narrow(tdot(left, right)) for left, right in zip(lefts, rights)]
        sums = jnp.concatenate(sums + ([] if beside is None else [beside]), 1)
        return sums[:rows], sums[rows:]
    total = sum(widths) + (0 if beside is None else beside.shape[1])

    def body(*refs):
        for half in range(2):

            @pl.when(pl.program_id(0) == half)
            def _():
                start = 0
                for left, right, width in zip(refs[:count], refs[count : 2 * count], widths):
                    lanes = slice(start, start + width)
                    refs[half - 2][:, lanes] = narrow(tdot(left[...], right[...]))
                    start = start + width
                if beside is not None:
                    refs[half - 2][:, start:] = refs[2 * count][...]

    specs = [pl.BlockSpec((left.shape[0], rows), lambda i: (0, i)) for left in lefts]
    specs = specs + [whole(right) for right in rights]
    args = (*lefts, *rights)
    if beside is not None:
        args = args + (beside,)
        specs.append(pl.BlockSpec((rows, beside.shape[1]), lambda i: (i, 0)))
    out = pl.BlockSpec((rows, total), lambda i: (0, 0))
    return pl.pallas_call(
        body,
        grid=(2,),
        out_shape=[like((rows, total), jnp.bfloat16)] * 2,
        in_specs=specs,
        out_specs=[out, out],
        compiler_params=room(14),
        cost_estimate=hint(),
    )(*args)


def order_matrix(size, rows, order, me):
    masks = jnp.asarray(np.array(masks_of(order), np.int32))
    source = ((me ^ masks)[:, None] * rows + jnp.arange(rows, dtype=jnp.int32)[None, :]).reshape(-1)
    return (jnp.arange(size, dtype=jnp.int32)[:, None] == source[None, :]).astype(jnp.bfloat16)


def local(
    frames,
    prompt,
    clip_frames,
    upstream,
    first_gain,
    first_shift,
    self_project,
    self_output,
    second_gain,
    second_shift,
    cross_query,
    cross_memory,
    cross_output,
    third_gain,
    third_shift,
    feed_input,
    feed_lift,
    feed_output,
    feed_offset,
):
    row_count, frame_count, width = frames.shape
    heads = width // HEAD_DIM
    token_count = row_count * frame_count
    scale = HEAD_DIM ** (-0.5)
    batch_count = lax.axis_size(B)
    seq_count = lax.axis_size(S)
    device_count = batch_count * seq_count
    seq_place = lax.axis_index(S)
    me = lax.axis_index(B) * seq_count + seq_place
    share = first_gain.shape[0]

    seq_masks = [1 << i for i in range(seq_count.bit_length() - 1)]
    batch_masks = [seq_count << i for i in range(batch_count.bit_length() - 1)]
    near = batch_masks[:3]
    far = batch_masks[3:]
    x_mask, y_mask = batch_masks[:2]
    places = [(0, 3, 1, 2), (3, 1, 2, 0), (3, 2, 0, 1)]
    if len(batch_masks) != 4:
        places = [[(i + j) % len(batch_masks) for i in range(len(batch_masks))] for j in range(3)]
    tail_orders = [[batch_masks[i] for i in place] for place in places]
    near_orders = [near[j:] + near[:j] for j in range(3)]
    near_count = len(masks_of(near))
    third = (token_count * 3 // 8) // 16 * 16
    cuts = [0, third, 2 * third, token_count]
    units = feed_output.shape[0]

    vectors = [first_gain, first_shift, second_gain, second_shift, third_gain, third_shift, feed_offset]
    vectors = jnp.pad(jnp.stack(vectors, 1), ((0, 0), (0, 128 - len(vectors))))
    split = 3 * width // 2
    group_one = narrow(jnp.concatenate([vectors, self_project], 1))
    memory_rows = ((0, share // 2 - cross_memory.shape[0]), (0, 0))
    memory_rows = jnp.concatenate(
        [
            jnp.pad(cross_memory[:, :width], memory_rows),
            jnp.pad(cross_memory[:, width:], memory_rows),
        ],
        0,
    )
    group_two = narrow(jnp.concatenate([self_output, cross_query, cross_output, memory_rows], 1))
    lift_rows = jnp.pad(feed_lift, ((0, 14), (0, width - units)))
    feed_sent = narrow(
        jnp.concatenate([feed_input.reshape(2 * units, width), feed_output, lift_rows], 0)
    )
    own_places = seq_place * frame_count + jnp.arange(frame_count, dtype=jnp.int32)
    key_order = masks_of(seq_masks)
    key_places = jnp.concatenate(
        [(seq_place ^ k) * frame_count + jnp.arange(frame_count, dtype=jnp.int32) for k in key_order]
    )
    own_clip, own_offset = clip_tables(clip_frames, own_places)
    key_clip = clip_tables(clip_frames, key_places)[0]
    seen = widen(own_clip[:, None, :] == key_clip[:, :, None])
    prompt_flat = prompt.reshape(-1, prompt.shape[2])
    rows = cross_memory.shape[0]
    place = jnp.arange(prompt.shape[2], dtype=jnp.int32)
    place = place // rows * share + place % rows
    places = jnp.arange(width, dtype=jnp.int32)[None, :]
    prompt_spread = [
        narrow(dot(prompt_flat, (place[:, None] + j * (share // 2) == places).astype(jnp.bfloat16)))
        for j in range(2)
    ]
    prompt_spread = jnp.concatenate(prompt_spread, 0)
    turn_tables = spin_tables(own_offset, 1.0)
    back_tables = spin_tables(own_offset, -1.0)

    def turn_rows(rows, matrix):
        return narrow(dot(rows, matrix))

    turned_memory = turn_rows(
        prompt_flat, order_matrix(prompt.shape[2], cross_memory.shape[0], tail_orders[2], me)
    )
    turned_memory = jnp.concatenate([turned_memory] * seq_count, 0)
    matrices = [order_matrix(width, share, order, me) for order in tail_orders]
    upstream_tokens = upstream.reshape(token_count, width)
    grad_drop_bias = jnp.sum(widen(upstream_tokens), 0, keepdims=True)
    early = [prompt_spread, turned_memory, seen, grad_drop_bias]
    early = early + matrices + list(turn_tables) + list(back_tables)

    known = [0]
    for mask in batch_masks[:1:-1]:
        group_one = jnp.concatenate([group_one, hop(group_one, mask)], 0)
        known = known + [old ^ mask for old in known]
    known = [known + [old ^ mask for old in known] for mask in (x_mask, y_mask)]
    group_one, group_two, *early = lax.optimization_barrier((group_one, group_two, *early))
    prompt_spread, turned_memory, seen, grad_drop_bias = early[:4]
    matrices, turn_tables, back_tables = early[4:7], early[7:9], early[9:]

    def pieces_of(columns, others):
        halves = []
        for h in range(2):
            have = known[h]
            pieces = [(columns[h], have), (others[h], [old ^ (y_mask, x_mask)[h] for old in have])]
            halves.append(pieces)
        return halves

    def add_core(halves, got):
        for h in range(2):
            halves[h] = halves[h] + [
                (piece, [old ^ seq_masks[0] for old in have])
                for piece, (_, have) in zip(got[h], halves[h])
            ]
            for mask in seq_masks[1:]:
                halves[h] = halves[h] + [
                    (hop(piece, mask), [old ^ mask for old in have]) for piece, have in halves[h]
                ]
        return halves

    core = seq_masks[0]
    traffic = Traffic()
    feed_parts = [feed_sent[2 * units :], feed_sent[: 2 * units]]
    ones = (group_one[:, : 128 + split], group_one[:, 128 + split :])
    group_two = gather(group_two, batch_masks[:2:-1])
    got = volley(ones, [x_mask, y_mask])
    ones = tuple(jnp.concatenate(pair, 0) for pair in zip(ones, got))
    got = volley(
        ones + (feed_parts[0], group_two, ones[0]),
        [y_mask, x_mask, far[0], batch_masks[2], core],
    )
    feed_got = [got[2]]
    group_two = jnp.concatenate([group_two, got[3]], 0)
    twos = (group_two[:, : 2 * width], group_two[:, 2 * width :])
    got_one = got[:2] + got[4:]
    got = volley(
        twos + (ones[1],) + got_one[:2], [x_mask, y_mask, core, core, core]
    )
    got_one = got_one + got[2:]
    twos = tuple(jnp.concatenate(pair, 0) for pair in zip(twos, got))
    halves = pieces_of(ones, got_one[:2])
    halves = add_core(halves, ((got_one[2], got_one[4]), (got_one[3], got_one[5])))
    new = {
        "two": once(twos + twos[:1], [y_mask, x_mask, core]),
        "feed": once(feed_parts[1:], far[:1]),
    }
    pieces = traffic.turn([piece for have in halves for piece, _ in have], lambda done: new)
    count = len(pieces) // 2
    halves = [
        [(piece, have) for piece, (_, have) in zip(pieces[h * count : (h + 1) * count], halves[h])]
        for h in range(2)
    ]
    packed, triple_low = settle(
        halves, [[(0, 0, 0, 128), (128, 1, 0, split)], [(0, 1, split, split)]], [128, 3 * width], me
    )
    packed = dot_t(jnp.eye(8, 128, dtype=jnp.bfloat16), packed)
    gain_one, shift_one, gain_two, shift_two, gain_three, shift_three, drop_bias = [
        packed[j : j + 1] for j in range(7)
    ]

    def cut_tokens(value):
        return [value[cuts[p] : cuts[p + 1]] for p in range(3)]

    def token_pairs(kept, got):
        pairs = []
        for p in range(3):
            first, last = near_count * cuts[p], near_count * cuts[p + 1]
            middle = (first + last) // 2
            pairs.append(
                [
                    narrow(widen(kept[rows]) + widen(got[rows]))
                    for rows in (slice(first, middle), slice(middle, last))
                ]
            )
        return pairs

    inputs = frames.reshape(token_count, width)
    query, pairs, normed_one, inverse_one, hidden_one = project(
        inputs, gain_one, shift_one, triple_low, turn_tables, scale
    )
    query, normed_one = traffic.turn(
        (query, normed_one),
        lambda done: {"pairs": double_list(pairs, seq_masks)},
        step=[],
    )
    for _ in seq_masks:
        (query,) = traffic.turn((query,), step=["pairs"])
    pairs = traffic.done["pairs"]
    self_mixed = attend(query, pairs, seen, row_count)

    def started(done):
        return {
            "last": once((twos[1],) + done["two"][:2], [core] * 3),
            "up": double_each(cut_tokens(upstream_tokens), near_orders),
        }

    self_mixed, *feed_all = traffic.turn([self_mixed] + feed_parts + feed_got, started)
    got_two = traffic.done["two"]
    feed_all.append(traffic.done["feed"][0])
    far_count = len(masks_of(far))
    unit_count = far_count * units
    drop_low, value_low, gate_low = [
        jnp.concatenate([part[rows : rows + units] for part in feed_all[p::2]], 0)
        for p, rows in ((0, 0), (1, 0), (1, units))
    ]
    biases = [part[units : units + 2, :units] for part in feed_all[::2]]
    biases = jnp.concatenate(biases, 1)
    for mask in far[1:]:
        drop_low, value_low, gate_low = [
            jnp.concatenate([low, hop(low, mask)], 0) for low in (drop_low, value_low, gate_low)
        ]
        biases = jnp.concatenate([biases, hop(biases, mask)], 1)
    value_bias, gate_bias = widen(biases[:1]), widen(biases[1:])
    self_mixed, value_low, gate_low, drop_low, value_bias, gate_bias = traffic.turn(
        (self_mixed, value_low, gate_low, drop_low, value_bias, gate_bias),
        lambda done: {"mixed": double_list(self_mixed, seq_masks)},
    )
    got = traffic.done["last"]
    halves = add_core(
        pieces_of(twos, got_two[:2]), ((got_two[2], got[1]), (got[0], got[2]))
    )
    lows = settle(
        halves,
        [[(0, 0, 0, width), (width, 1, 0, width)], [(0, 2, 0, width), (width, 3, 0, width)]],
        [width] * 4,
        me,
    )
    self_low, ask_low, cross_low, memory_low, self_mixed = traffic.turn(
        (*lows, self_mixed), lambda done: {"hidden": double_list(hidden_one, seq_masks)}
    )
    after_self, normed_two, inverse_two, hidden_two, asking = ahead(
        self_mixed, self_low, inputs, gain_two, shift_two, ask_low, scale
    )
    asking, prompt_spread = lax.optimization_barrier((asking, prompt_spread))
    memory = multiply(prompt_spread, memory_low)
    cross_mixed = attend(asking, [memory], None, row_count)
    (cross_mixed,) = traffic.turn(
        (cross_mixed,), lambda done: {"asked": double_list(hidden_two, seq_masks)}
    )
    after_cross, normed_three, inverse_three, hidden_three = ahead(
        cross_mixed, cross_low, after_self, gain_three, shift_three
    )

    hidden_three, cross_mixed = traffic.turn(
        (hidden_three, cross_mixed),
        lambda done: {
            "rows": double_each(cut_tokens(hidden_three), near_orders),
            "crossed": double_list(cross_mixed, seq_masks),
        },
        step=["asked"],
    )
    traffic.turn((), step=["rows", "crossed"])
    up = jnp.concatenate(traffic.done["up"], 0)
    traffic.turn((), lambda done: {"ups": double_list(up, seq_masks)}, step=["rows"])
    for _ in seq_masks[1:]:
        traffic.turn((), step=["asked", "crossed", "hidden", "mixed", "ups"])
    hidden_all, mixed_all, asked_all, cross_all = [
        jnp.concatenate(traffic.done[name], 0) for name in ("hidden", "mixed", "asked", "crossed")
    ]
    turned_triple = [turn_rows(hidden_all, matrix) for matrix in matrices]
    turned_cross = turn_rows(cross_all, matrices[0])
    turned_ask = turn_rows(asked_all, matrices[1])

    def rows_there(done):
        if "rows" not in done:
            return {}
        done["rows"] = jnp.concatenate(done["rows"], 0)
        return {"all": double_list(done["rows"], seq_masks)}

    turned_cross, turned_ask, mixed_all, *turned_triple = traffic.turn(
        [turned_cross, turned_ask, mixed_all] + turned_triple, rows_there
    )
    while "rows" in traffic.flows:
        traffic.turn((), rows_there)
    ups = traffic.done["ups"]
    lows = (value_low, gate_low, drop_low, value_bias, gate_bias)
    results = [feed_block(traffic.done["rows"], ups[0], *lows)]
    results[0] = traffic.turn(results[0])
    for _ in seq_masks[1:]:
        traffic.turn((), step=["all"])
    feed_rows = traffic.done["all"]
    for rows, up in zip(feed_rows[1:], ups[1:]):
        results.append(feed_block(rows, up, *lows))
    middles, value_grads, gate_grads, back_sums = [list(item) for item in zip(*results)]

    def back_flow():
        blocks = back_sums
        for mask in reversed(seq_masks):
            half = len(blocks) // 2
            sent = yield tuple(blocks[half:])
            got = yield hops(sent, (mask,) * half)
            if half > 1:
                blocks = [narrow(widen(a) + widen(b)) for a, b in zip(blocks[:half], got)]
        return (yield from halve_pairs(token_pairs(blocks[0], got[0]), near_orders))

    blocks = len(feed_rows)
    tied = traffic.turn(middles + value_grads + gate_grads, lambda done: {"back": back_flow()})
    middles, value_grads, gate_grads = tied[:blocks], tied[blocks : 2 * blocks], tied[2 * blocks :]
    drop_grad = unit_grad(middles, ups, False)[0]
    tied = traffic.turn((drop_grad, *value_grads, *gate_grads))
    for _ in seq_masks[1:]:
        tied = traffic.turn(tied)
    drop_grad, value_grads, gate_grads = tied[0], tied[1 : 1 + blocks], tied[1 + blocks :]
    value_grad, value_bias_grad = unit_grad(value_grads, feed_rows, True)
    gate_grad, gate_bias_grad = unit_grad(gate_grads, feed_rows, True)

    def unit_blocks(grad):
        return [grad[k * units : (k + 1) * units] for k in range(far_count)]

    bias_grads = [
        narrow(
            jnp.pad(
                jnp.concatenate(
                    [bias[:, k * units : (k + 1) * units] for bias in (value_bias_grad, gate_bias_grad)], 0
                ),
                ((0, 14), (0, width - units)),
            )
        )
        for k in range(far_count)
    ]

    def unit_flow(p):
        blocks = unit_blocks((drop_grad, drop_grad, value_grad, value_grad, gate_grad)[p])
        if p == 4:
            blocks = [jnp.concatenate(pair, 0) for pair in zip(blocks, bias_grads)]
            return halve_rows(blocks, 0, units + 16, far)
        half = units // 2
        return halve_rows(blocks, p % 2 * half, (p % 2 + 1) * half, far)

    value_grad, gate_grad, drop_grad, mixed_all = traffic.turn(
        (value_grad, gate_grad, drop_grad, mixed_all),
        lambda done: {"unit0": unit_flow(0)},
    )
    turned_self = [turn_rows(mixed_all, matrix) for matrix in matrices]

    term_sums = [multiply(middle, drop_low) for middle in middles]

    def term_flow():
        blocks = term_sums
        for mask in reversed(seq_masks):
            half = len(blocks) // 2
            sent = yield tuple(blocks[half:])
            got = yield hops(sent, (mask,) * half)
            if half > 1:
                blocks = [narrow(widen(a) + widen(b)) for a, b in zip(blocks[:half], got)]
        return blocks[0], got[0]

    (*turned_self,) = traffic.turn(turned_self, lambda done: {"term": term_flow()})
    for _ in seq_masks[1:]:
        traffic.turn((), step=["term"])
    while "back" in traffic.flows:
        traffic.turn((), step=["back", "term"])

    while "back" in traffic.flows:
        unit_sums = list(traffic.turn(unit_sums, step=["back", "term"]))
    feed_back = jnp.concatenate(traffic.done["back"], 0)
    (feed_back,) = traffic.turn(
        (feed_back,),
        lambda done: {
            "term_near": halve_pairs(token_pairs(*done["term"]), near_orders),
        },
    )
    cross_out_grad, grad_gain_three, grad_shift_three, cross_branch, cross_mixed_grad = back(
        feed_back, None, upstream_tokens, normed_three, inverse_three, gain_three, cross_low
    )

    def weight_pair(turned, *grads):
        half = turned.shape[1] // 2
        pair = []
        for columns in (turned[:, :half], turned[:, half:]):
            sums = [narrow(tdot(columns, grad)) for grad in grads]
            if len(grads) > 1:
                rows = cross_memory.shape[0]
                sums = [
                    jnp.pad(part.reshape(-1, rows, width), ((0, 0), (0, share // 2 - rows), (0, 0)))
                    for part in sums
                ]
                sums = [jnp.concatenate(sums, 1).reshape(-1, width)]
            pair.append(sums[0])
        return tuple(pair)

    (cross_mixed_grad,) = traffic.turn(
        (cross_mixed_grad,),
        lambda done: {"dc": double_list(cross_branch, seq_masks), "unit1": unit_flow(1)},
    )
    asked_grad = attend_back(
        asking, [memory], None, cross_mixed_grad, None, row_count, scale
    )
    (asked_grad,) = traffic.turn(
        (asked_grad,),
        lambda done: {"dq": double_list(asked_grad, seq_masks), "unit2": unit_flow(2)},
    )
    for _ in seq_masks[1:]:
        traffic.turn((), step=["dc"])
    self_out_grad, grad_gain_two, grad_shift_two, self_branch, self_mixed_grad = back(
        asked_grad,
        ask_low,
        cross_out_grad,
        normed_two,
        inverse_two,
        gain_two,
        self_low,
        memory.shape[0] // token_count,
    )
    (self_mixed_grad,) = traffic.turn(
        (self_mixed_grad,),
        lambda done: {"da": double_list(self_branch, seq_masks)},
    )
    for _ in seq_masks[1:]:
        traffic.turn((), step=["dq", "da"])
    cross_pair = weight_pair(turned_cross, jnp.concatenate(traffic.done["dc"], 0))
    layer_output = narrow(
        after_cross + jnp.concatenate(traffic.done["term_near"], 0) + drop_bias
    )
    memory_all = traffic.done["dq"]
    half = memory.shape[0] // 2
    ask_pair = weight_pair(turned_ask, jnp.concatenate([part[2 * half :] for part in memory_all], 0))
    memory_pair = weight_pair(
        turned_memory,
        jnp.concatenate([part[:half] for part in memory_all], 0),
        jnp.concatenate([part[half : 2 * half] for part in memory_all], 0),
    )
    self_mixed_grad, layer_output = traffic.turn(
        (self_mixed_grad, layer_output),
        lambda done: {
            "first": halve_pairs([cross_pair, ask_pair, memory_pair], tail_orders),
        },
    )
    pair_grad = attend_back(
        query, pairs, seen, self_mixed_grad, back_tables, row_count, scale
    )

    def shed_frames(value):
        query_grad = value[-token_count:]
        count = value.shape[0] - token_count
        for mask in reversed(seq_masks):
            half = count // 2
            (sent,) = yield (value[half:count],)
            (got,) = yield hops((sent,), (mask,))
            if mask > seq_masks[0]:
                value = narrow(widen(value[:half]) + widen(got))
                count = half
        if len(seq_masks) > 1:
            value = jnp.concatenate([value, query_grad], 0)
        return value, got

    (pair_grad,) = traffic.turn((pair_grad,), lambda done: {"pair": shed_frames(pair_grad)}, step=[])
    for _ in seq_masks:
        traffic.turn((), step=["pair"])
    triple_back = spin_backward(*traffic.done["pair"], *back_tables)
    (triple_back,) = traffic.turn(
        (triple_back,), lambda done: {"dt": double_list(triple_back, seq_masks)}
    )
    frame_grad, grad_gain_one, grad_shift_one = back(
        triple_back, triple_low, self_out_grad, normed_one, inverse_one, gain_one
    )
    branch_all = jnp.concatenate(traffic.done["da"], 0)
    shares = [0, width // 6, width // 3, width]
    sums = [
        grad_gain_one,
        grad_shift_one,
        grad_gain_two,
        grad_shift_two,
        grad_gain_three,
        grad_shift_three,
        grad_drop_bias,
    ]
    sums = jnp.pad(jnp.concatenate(sums, 0), ((0, 1), (0, 0)))
    frame_grad, sums = traffic.turn((frame_grad, sums), lambda done: {"sums": double_list(sums, seq_masks)})
    for _ in seq_masks:
        traffic.turn((), step=["dt", "sums"])
    triple_all = jnp.concatenate(traffic.done["dt"], 0)
    sums = sum(traffic.done["sums"])
    sums_turned = tdot(matrices[1], narrow(jnp.transpose(sums)))
    sums_turned = narrow(jnp.pad(sums_turned, ((0, 0), (0, 120))))
    triple_pairs = [
        list(
            weight_sums(
                [turned_triple[p], turned_self[p]],
                [
                    triple_all[:, p * width : (p + 1) * width],
                    branch_all[:, shares[p] : shares[p + 1]],
                ],
                sums_turned if p == 1 else None,
            )
        )
        for p in range(3)
    ]
    while traffic.count["first"] < len(batch_masks) - 1:
        traffic.turn(())

    def tail_first(*which):
        return once([triple_pairs[p][1] for p in which], [tail_orders[p][-1] for p in which])

    traffic.turn((), lambda done: {"early": tail_first(0, 2)})
    (triple_pairs[1][1],) = traffic.turn(
        (triple_pairs[1][1],),
        lambda done: {"unit4": unit_flow(4)},
        step=["first"],
    )
    traffic.turn((), lambda done: {"late": tail_first(1)}, step=[])

    def tail_rest(done):
        got = (done["early"][0], done["late"][0], done["early"][1])
        pairs = []
        for (kept, _), part in zip(triple_pairs, got):
            half = kept.shape[0] // 2
            pairs.append(
                [
                    narrow(widen(kept[rows]) + widen(part[rows]))
                    for rows in (slice(half), slice(half, None))
                ]
            )
        orders = [order[:-1] for order in tail_orders]
        return {"tail": halve_pairs(pairs, orders), "unit3": unit_flow(3)}

    traffic.turn((), tail_rest)
    while traffic.flows:
        traffic.turn(())
    parts = traffic.done["tail"]
    grad_cross, grad_ask, grad_memory = traffic.done["first"]
    grad_self = jnp.concatenate(
        [part[:, width : width + shares[p + 1] - shares[p]] for p, part in enumerate(parts)], 1
    )
    drop_sums = jnp.concatenate([traffic.done[name] for name in UNITS[:2]], 0)
    value_sums = jnp.concatenate([traffic.done[name] for name in UNITS[2:4]], 0)
    gate_sums = traffic.done[UNITS[4]]
    grad_triple = jnp.concatenate([part[:, :width] for part in parts], 1)
    sums = width + shares[2] - shares[1]
    sums = jnp.transpose(parts[1][:, sums : sums + 7])
    grad_memory = grad_memory.reshape(2, share // 2, width)[:, : cross_memory.shape[0]]
    grad_memory = jnp.concatenate([grad_memory[0], grad_memory[1]], 1)
    grad_lift = jnp.stack([value_sums, gate_sums[:units]], 0)
    grad_drop = drop_sums
    grad_lift_bias = gate_sums[units : units + 2, :units]
    shape = frames.shape
    return (
        layer_output.reshape(shape),
        frame_grad.reshape(shape),
        sums[0],
        sums[1],
        grad_triple,
        grad_self,
        sums[2],
        sums[3],
        grad_ask,
        grad_memory,
        grad_cross,
        sums[4],
        sums[5],
        grad_lift,
        grad_lift_bias,
        grad_drop,
        sums[6],
    )


def solution(mesh):
    both = P(AX)
    wide = P(AX, None)
    rows = P(B, S, None)
    units = P(None, AX, None)
    in_specs = (
        rows,
        P(B, None, None),
        P(B, None),
        rows,
        both,
        both,
        wide,
        wide,
        both,
        both,
        wide,
        wide,
        wide,
        both,
        both,
        units,
        P(None, AX),
        wide,
        both,
    )
    out_specs = (
        rows,
        rows,
        both,
        both,
        wide,
        wide,
        both,
        both,
        wide,
        wide,
        wide,
        both,
        both,
        units,
        P(None, AX),
        wide,
        both,
    )
    return jax.shard_map(local, mesh=mesh, in_specs=in_specs, out_specs=out_specs, check_vma=False)
```

```python
import jax
import jax.numpy as jnp
import numpy as np
from jax import lax
from jax.experimental import pallas as pl
from jax.experimental.pallas import tpu as pltpu
from jax.sharding import PartitionSpec as P

HEAD_DIM = 64
LANES = 1536
SPAN = 512
UNITS = ["unit0", "unit1", "unit2", "unit3", "unit4"]
EPS = 1e-05
NEG = -1e30
B = "batch"
S = "seq"
AX = (B, S)


def narrow(value):
    return value.astype(jnp.bfloat16)


def widen(value):
    return value.astype(jnp.float32)


def mult(left, right, form):
    return jnp.einsum(form, left, right, preferred_element_type=jnp.float32)


def dot(left, right):
    return lax.dot_general(left, right, (((1,), (0,)), ((), ())), preferred_element_type=jnp.float32)


def dot_t(left, right):
    return lax.dot_general(left, right, (((1,), (1,)), ((), ())), preferred_element_type=jnp.float32)


def tdot(left, right):
    return lax.dot_general(left, right, (((0,), (0,)), ((), ())), preferred_element_type=jnp.float32)


def standardize(values):
    center = values - jnp.mean(values, -1, keepdims=True)
    inverse = lax.rsqrt(jnp.mean(center * center, -1, keepdims=True) + EPS)
    return (center * inverse, inverse)


def norm_back(incoming, normed, inverse, gain):
    scaled = incoming * gain
    inner = (
        scaled
        - jnp.mean(scaled, -1, keepdims=True)
        - normed * jnp.mean(scaled * normed, -1, keepdims=True)
    )
    return (
        inner * inverse,
        jnp.sum(incoming * normed, 0, keepdims=True),
        jnp.sum(incoming, 0, keepdims=True),
    )


def clip_tables(lengths, places):
    ends = jnp.cumsum(lengths, 1)
    later = places[None, :, None] >= ends[:, None, :]
    ident = jnp.sum(later.astype(jnp.int32), 2)
    starts = jnp.max(jnp.where(later, ends[:, None, :], 0), 2)
    return (ident, places[None, :] - starts)


def softmax_back(probs, prob_grad):
    return probs * (prob_grad - jnp.sum(probs * prob_grad, 0, keepdims=True))


def hop(value, mask):
    count = lax.axis_size(B) * lax.axis_size(S)
    return lax.ppermute(value, AX, [(i, i ^ mask) for i in range(count)])


def volley(values, masks):
    values = lax.optimization_barrier(tuple(values))
    return lax.optimization_barrier(tuple(hop(value, mask) for value, mask in zip(values, masks)))


def masks_of(order):
    masks = [0]
    for mask in order:
        masks = masks + [old ^ mask for old in masks]
    return masks


def gather(value, order):
    for mask in order:
        value = jnp.concatenate([value, hop(value, mask)], 0)
    return value


def settle(halves, targets, widths, me):
    pieces = [(h, piece, have) for h in range(len(halves)) for piece, have in halves[h]]
    total = sum(len(have) for h, piece, have in pieces if h == 0)
    rows = pieces[0][1].shape[0] // len(pieces[0][2])
    if rows % 16:
        outs = [[] for _ in widths]
        for h in range(len(halves)):
            have = sum([have for _, have in halves[h]], [])
            table = np.zeros(total, np.int32)
            table[np.array(have)] = np.arange(total)
            place = jnp.asarray(table)[me ^ jnp.arange(total, dtype=jnp.int32)]
            blocks = jnp.concatenate([piece for piece, _ in halves[h]], 0).reshape(total, rows, -1)
            blocks = jnp.take(blocks, place, axis=0).reshape(total * rows, -1)
            for source, out, _, count in targets[h]:
                outs[out].append(blocks[:, source : source + count])
        return [jnp.concatenate(out, 1) for out in outs]

    def body(me_ref, *refs):
        ins = refs[: len(pieces)]
        outs = refs[len(pieces) : len(pieces) + len(widths)]
        held = refs[len(pieces) + len(widths) : -2]
        in_sems, out_sems = refs[-2:]
        loads = []
        for i in range(len(pieces)):
            load = pltpu.make_async_copy(ins[i], held[i], in_sems.at[i])
            load.start()
            loads.append(load)
        stores = []
        for i, (h, _, have) in enumerate(pieces):
            loads[i].wait()
            for j, mask in enumerate(have):
                start = pl.multiple_of((me_ref[0] ^ mask) * rows, rows)
                for source, out, column, count in targets[h]:
                    store = pltpu.make_async_copy(
                        held[i].at[pl.ds(j * rows, rows), pl.ds(source, count)],
                        outs[out].at[pl.ds(start, rows), pl.ds(column, count)],
                        out_sems.at[len(stores)],
                    )
                    store.start()
                    stores.append(store)
        for store in stores:
            store.wait()

    count = sum(len(have) * len(targets[h]) for h, _, have in pieces)
    size = 2 * sum(piece.size for _, piece, _ in pieces)
    return pl.pallas_call(
        body,
        out_shape=[jax.ShapeDtypeStruct((total * rows, width), jnp.bfloat16) for width in widths],
        in_specs=[pl.BlockSpec(memory_space=pltpu.SMEM)]
        + [pl.BlockSpec(memory_space=pl.ANY)] * len(pieces),
        out_specs=[pl.BlockSpec(memory_space=pltpu.HBM)] * len(widths),
        scratch_shapes=[pltpu.VMEM(piece.shape, jnp.bfloat16) for _, piece, _ in pieces]
        + [pltpu.SemaphoreType.DMA((len(pieces),)), pltpu.SemaphoreType.DMA((count,))],
        compiler_params=pltpu.CompilerParams(vmem_limit_bytes=size + (2 << 20)),
        cost_estimate=pl.CostEstimate(flops=0, bytes_accessed=size // 16, transcendentals=0),
    )(me.reshape(1), *[piece for _, piece, _ in pieces])


class Traffic:
    def __init__(self):
        self.flows = {}
        self.done = {}
        self.count = {}

    def turn(self, outs, new=None, step=None):
        names = list(self.flows) if step is None else [n for n in step if n in self.flows]
        gots = sum([self.flows[name][1] for name in names], ())
        tied = lax.optimization_barrier(gots + tuple(outs))
        outs = tied[len(gots) :]
        started = []
        for name in names:
            flow, got = self.flows.pop(name)
            got, tied = tied[: len(got)], tied[len(got) :]
            try:
                started.append((name, flow, flow.send(got)))
            except StopIteration as end:
                self.done[name] = end.value
        if new is not None:
            flows = new(self.done)
            for name, flow in ((name, flow) for name, flow in flows.items() if flow is not None):
                started.append((name, flow, next(flow)))
        sents = sum([sent for _, _, sent in started], ())
        tied = lax.optimization_barrier(sents + outs)
        for name, flow, sent in started:
            self.count[name] = self.count.get(name, 0) + 1
            self.flows[name] = (flow, flow.send(tied[: len(sent)]))
            tied = tied[len(sent) :]
        return tied


def hops(values, masks):
    return tuple(hop(value, mask) for value, mask in zip(values, masks))


def once(values, masks):
    values = yield tuple(values)
    return (yield hops(values, masks))


def halve_pairs(pairs, orders):
    for step in list(zip(*orders))[::-1]:
        sent = yield tuple(sent for _, sent in pairs)
        got = yield hops(sent, step)
        sums = [(kept, part) for (kept, _), part in zip(pairs, got)]
        pairs = []
        for kept, part in sums:
            half = kept.shape[0] // 2
            pair = [widen(kept[cut]) + widen(part[cut]) for cut in (slice(half), slice(half, None))]
            pairs.append(pair if kept.ndim == 3 else [narrow(item) for item in pair])
    return [widen(kept) + widen(part) for kept, part in sums]


def halve_list(blocks, masks):
    for mask in reversed(masks):
        half = len(blocks) // 2
        sent = yield tuple(narrow(block) for block in blocks[half:])
        got = yield hops(sent, (mask,) * half)
        blocks = [widen(a) + widen(b) for a, b in zip(blocks[:half], got)]
    return blocks[0]


def halve_rows(blocks, first, last, masks):
    for mask in reversed(masks):
        half = len(blocks) // 2
        sent = yield tuple(narrow(block[first:last]) for block in blocks[half:])
        got = yield hops(sent, (mask,) * half)
        blocks = [widen(a[first:last]) + widen(b) for a, b in zip(blocks[:half], got)]
        first, last = 0, last - first
    return blocks[0]


def double_each(parts, orders):
    for step in zip(*orders):
        parts = yield tuple(parts)
        got = yield hops(parts, step)
        pairs = list(zip(parts, got))
        parts = [jnp.concatenate(pair, 0) for pair in pairs]
    return sum(pairs, ())


def double_list(value, masks):
    blocks = (value,)
    for mask in masks:
        blocks = yield blocks
        got = yield hops(blocks, (mask,) * len(blocks))
        blocks = tuple(blocks) + tuple(got)
    return blocks


def spin(value, cosine, sine):
    lane = lax.broadcasted_iota(jnp.int32, value.shape, 1)
    other = jnp.where(lane % 64 < 32, pltpu.roll(value, 96, 1), pltpu.roll(value, 32, 1))
    return value * cosine + other * sine


def spin_tables(offsets, sign):
    half = HEAD_DIM // 2
    freq = 10000.0 ** (-jnp.arange(half, dtype=jnp.float32) / half)
    angle = offsets.astype(jnp.float32).reshape(-1, 1) * freq
    cosine = jnp.cos(angle)
    sine = sign * jnp.sin(angle)
    return (jnp.concatenate([cosine] * 4, 1), jnp.concatenate([-sine, sine, -sine, sine], 1))


def hint():
    return pl.CostEstimate(flops=1 << 20, bytes_accessed=1 << 20, transcendentals=0)


def whole(array):
    return pl.BlockSpec(array.shape, lambda i: (0,) * array.ndim)


def like(shape, dtype=jnp.float32):
    return jax.ShapeDtypeStruct(shape, dtype)


def room(mebibytes):
    return pltpu.CompilerParams(vmem_limit_bytes=mebibytes << 20)


def project(inputs, gain, shift, weight, tables, scale):
    rows, width = inputs.shape
    block = width

    def body(in_ref, gain_ref, shift_ref, cos_ref, sin_ref, weight_ref, *outs):
        query_ref, pair_ref, normed_ref, inverse_ref, hidden_ref = outs
        step = pl.program_id(0)

        @pl.when(step == 0)
        def _():
            normed, inverse = standardize(widen(in_ref[...]))
            normed_ref[...] = normed
            inverse_ref[...] = inverse
            hidden_ref[...] = narrow(normed * gain_ref[...] + shift_ref[...])

        value = dot(hidden_ref[...], weight_ref[...])

        def turned(factor):
            parts = [
                spin(value[:, j : j + 128], cos_ref[...], sin_ref[...]) for j in range(0, block, 128)
            ]
            return [narrow(part * factor) for part in parts]

        @pl.when(step == 0)
        def _():
            for j, part in enumerate(turned(scale)):
                query_ref[:, 128 * j : 128 * j + 128] = part

        @pl.when(step == 1)
        def _():
            for j, part in enumerate(turned(1.0)):
                pair_ref[:, 128 * j : 128 * j + 128] = part

        @pl.when(step == 2)
        def _():
            pair_ref[...] = narrow(value)

    return pl.pallas_call(
        body,
        grid=(3,),
        out_shape=[
            like((rows, width), jnp.bfloat16),
            like((2 * rows, width), jnp.bfloat16),
            like((rows, width)),
            like((rows, 1)),
            like((rows, width), jnp.bfloat16),
        ],
        in_specs=[
            whole(inputs),
            whole(gain),
            whole(shift),
            whole(tables[0]),
            whole(tables[1]),
            pl.BlockSpec((width, block), lambda i: (0, i)),
        ],
        out_specs=[
            pl.BlockSpec((rows, block), lambda i: (0, 0)),
            pl.BlockSpec((rows, block), lambda i: (jnp.maximum(i - 1, 0), 0)),
            pl.BlockSpec((rows, width), lambda i: (0, 0)),
            pl.BlockSpec((rows, 1), lambda i: (0, 0)),
            pl.BlockSpec((rows, width), lambda i: (0, 0)),
        ],
        compiler_params=room(22),
        cost_estimate=hint(),
    )(inputs, gain, shift, *tables, weight)


def ahead(mixed, low, before, gain, shift, ask=None, scale=1.0):
    rows, width = before.shape
    steps = width // LANES

    def body(mixed_ref, before_ref, gain_ref, shift_ref, *refs):
        low_ref, refs = refs[0], refs[1:]
        if ask is not None:
            ask_ref, refs = refs[0], refs[1:]
        sum_ref, normed_ref, inverse_ref, hidden_ref = refs[:4]
        step = pl.program_id(0)

        @pl.when(step < steps)
        def _():
            lanes = pl.ds(pl.multiple_of(step * LANES, LANES), LANES)
            sum_ref[:, lanes] = widen(before_ref[:, lanes]) + dot(mixed_ref[...], low_ref[...])

        @pl.when(step == steps - 1)
        def _():
            normed, inverse = standardize(sum_ref[...])
            normed_ref[...] = normed
            inverse_ref[...] = inverse
            hidden_ref[...] = narrow(normed * gain_ref[...] + shift_ref[...])

        if ask is not None:

            @pl.when(step >= steps)
            def _():
                refs[4][...] = narrow(dot(hidden_ref[...], ask_ref[...]) * scale)

    full = pl.BlockSpec((rows, width), lambda i: (0, 0))
    args = (mixed, before, gain, shift, low)
    specs = [whole(mixed), whole(before), whole(gain), whole(shift)]
    specs.append(pl.BlockSpec((width, LANES), lambda i: (0, jnp.minimum(i, steps - 1))))
    shapes = [
        like((rows, width)),
        like((rows, width)),
        like((rows, 1)),
        like((rows, width), jnp.bfloat16),
    ]
    outs = [full, full, pl.BlockSpec((rows, 1), lambda i: (0, 0)), full]
    if ask is not None:
        args = args + (ask,)
        specs.append(pl.BlockSpec((width, LANES), lambda i: (0, jnp.maximum(i - steps, 0))))
        shapes.append(like((rows, width), jnp.bfloat16))
        outs.append(pl.BlockSpec((rows, LANES), lambda i: (0, jnp.maximum(i - steps, 0))))
    return pl.pallas_call(
        body,
        grid=(steps if ask is None else 2 * steps,),
        out_shape=shapes,
        in_specs=specs,
        out_specs=outs,
        compiler_params=room(16),
        cost_estimate=hint(),
    )(*args)


def back(incoming, low, grads, normed, inverse, gain, out=None, place=0):
    rows, width = grads.shape
    block = LANES
    first = 0 if low is None else width // block
    last = 0 if out is None else width // LANES
    norm_step = max(first - 1, 0)

    def body(in_ref, grad_ref, normed_ref, inverse_ref, gain_ref, *refs):
        if low is not None:
            low_ref, refs = refs[0], refs[1:]
        if out is not None:
            out_ref, refs = refs[0], refs[1:]
        sum_ref, gain_grad_ref, shift_grad_ref = refs[:3]
        held_ref = refs[-1]
        step = pl.program_id(0)
        if low is not None:

            @pl.when(step < first)
            def _():
                lanes = pl.ds(pl.multiple_of(step * block, block), block)
                held_ref[:, lanes] = dot_t(in_ref[...], low_ref[...])

        @pl.when(step == norm_step)
        def _():
            value = in_ref[...] if low is None else held_ref[...]
            inner, gain_grad, shift_grad = norm_back(
                value, normed_ref[...], inverse_ref[...], gain_ref[...]
            )
            total = widen(grad_ref[...]) + inner
            sum_ref[...] = total
            gain_grad_ref[...] = gain_grad
            shift_grad_ref[...] = shift_grad
            if out is not None:
                refs[3][...] = narrow(total)

        if out is not None:

            @pl.when(step >= first)
            def _():
                refs[4][...] = narrow(dot_t(refs[3][...], out_ref[...]))

    full = pl.BlockSpec((rows, width), lambda i: (0, 0))
    line = pl.BlockSpec((1, width), lambda i: (0, 0))
    args = (incoming, grads, normed, inverse, gain)
    specs = [whole(array) for array in args]
    specs[0] = pl.BlockSpec((rows, incoming.shape[1]), lambda i: (place, 0))
    if low is not None:
        args = args + (low,)
        specs.append(pl.BlockSpec((block, low.shape[1]), lambda i: (jnp.minimum(i, first - 1), 0)))
    shapes = [like((rows, width)), like((1, width)), like((1, width))]
    outs = [full, line, line]
    if out is not None:
        args = args + (out,)
        specs.append(pl.BlockSpec((LANES, width), lambda i: (jnp.maximum(i - first, 0), 0)))
        shapes = shapes + [like((rows, width), jnp.bfloat16)] * 2
        outs = outs + [full, pl.BlockSpec((rows, LANES), lambda i: (0, jnp.maximum(i - first, 0)))]
    return pl.pallas_call(
        body,
        grid=(first + last,),
        out_shape=shapes,
        in_specs=specs,
        out_specs=outs,
        scratch_shapes=[pltpu.VMEM((rows, width), jnp.float32)],
        compiler_params=room(24),
        cost_estimate=hint(),
    )(*args)


def feed_block(rows, ups, value_low, gate_low, drop_low, value_bias, gate_bias):
    count, width = rows.shape
    units = drop_low.shape[0]
    block = min(count, 256)

    def body(row_ref, up_ref, value_ref, gate_ref, drop_ref, value_bias_ref, gate_bias_ref, *outs):
        middle_ref, value_out, gate_out, back_ref = outs
        middle_grad = widen(narrow(dot_t(up_ref[...], drop_ref[...])))
        value = dot_t(row_ref[...], value_ref[...]) + value_bias_ref[...]
        gate = dot_t(row_ref[...], gate_ref[...]) + gate_bias_ref[...]
        sigma = jax.nn.sigmoid(gate)
        middle = narrow(value * gate * sigma)
        value_grad = narrow(middle_grad * gate * sigma)
        gate_grad = narrow(middle_grad * value * sigma * (1.0 + gate * (1.0 - sigma)))
        middle_ref[...] = middle
        value_out[...] = value_grad
        gate_out[...] = gate_grad
        back_ref[...] = narrow(dot(value_grad, value_ref[...]) + dot(gate_grad, gate_ref[...]))

    wide = pl.BlockSpec((block, width), lambda i: (i, 0))
    thin = pl.BlockSpec((block, units), lambda i: (i, 0))
    args = (rows, ups, value_low, gate_low, drop_low, value_bias, gate_bias)
    return pl.pallas_call(
        body,
        grid=(count // block,),
        out_shape=[like((count, units), jnp.bfloat16)] * 3 + [like((count, width), jnp.bfloat16)],
        in_specs=[wide, wide] + [whole(array) for array in args[2:]],
        out_specs=[thin] * 3 + [wide],
        compiler_params=room(32),
        cost_estimate=hint(),
    )(*args)


def unit_grad(lefts, rights, sums):
    units = lefts[0].shape[1]
    width = rights[0].shape[1]
    count = len(lefts)
    block = 128 if units % 128 == 0 else units

    def body(*refs):
        total = 0.0
        for left, right in zip(refs[:count], refs[count : 2 * count]):
            total = total + tdot(left[...], right[...])
        refs[2 * count][...] = narrow(total)
        if sums:
            refs[2 * count + 1][...] = sum(
                jnp.sum(widen(left[...]), 0, keepdims=True) for left in refs[:count]
            )

    specs = [pl.BlockSpec((left.shape[0], block), lambda i: (0, i)) for left in lefts]
    outs = [pl.BlockSpec((block, width), lambda i: (i, 0))]
    shapes = [like((units, width), jnp.bfloat16)]
    if sums:
        outs.append(pl.BlockSpec((1, block), lambda i: (0, i)))
        shapes.append(like((1, units)))
    return pl.pallas_call(
        body,
        grid=(units // block,),
        out_shape=shapes,
        in_specs=specs + [whole(right) for right in rights],
        out_specs=outs,
        compiler_params=room(24),
        cost_estimate=hint(),
    )(*lefts, *rights)


def spin_backward(grads, got, cosine, sine):
    rows, width = got.shape[0] // 2, got.shape[1]
    last = grads.shape[0] // rows - 1

    def body(cos_ref, sin_ref, query_ref, own_ref, got_ref, out_ref):
        step = pl.program_id(0)

        @pl.when(step == 0)
        def _():
            out_ref[...] = query_ref[...]

        @pl.when(step == 1)
        def _():
            for j in range(0, width, 128):
                value = widen(own_ref[:, j : j + 128]) + widen(got_ref[:, j : j + 128])
                out_ref[:, j : j + 128] = narrow(spin(value, cos_ref[...], sin_ref[...]))

        @pl.when(step == 2)
        def _():
            out_ref[...] = narrow(widen(own_ref[...]) + widen(got_ref[...]))

    table = pl.BlockSpec((rows, 128), lambda i: (0, 0))
    part = pl.BlockSpec((rows, width), lambda i: (jnp.maximum(i - 1, 0), 0))
    return pl.pallas_call(
        body,
        grid=(3,),
        out_shape=jax.ShapeDtypeStruct((rows, 3 * width), jnp.bfloat16),
        in_specs=[table, table, pl.BlockSpec((rows, width), lambda i: (last, 0)), part, part],
        out_specs=pl.BlockSpec((rows, width), lambda i: (0, i)),
        compiler_params=room(8),
        cost_estimate=pl.CostEstimate(
            flops=1 << 20, bytes_accessed=1 << 20, transcendentals=0
        ),
    )(cosine, sine, grads, grads, got)


def two_heads(value):
    lane = lax.broadcasted_iota(jnp.int32, value.shape, 1)
    zero = jnp.zeros_like(value)
    first = jnp.where(lane < HEAD_DIM, value, zero)
    second = jnp.where(lane < HEAD_DIM, zero, value)
    return jnp.concatenate([first, second], 0)


def one_row(value):
    half = value.shape[0] // 2
    lane = lax.broadcasted_iota(jnp.int32, (half, value.shape[1]), 1)
    return jnp.where(lane < HEAD_DIM, value[:half], value[half:])


def row_probs(asked, keys, seen):
    scores = dot_t(keys, asked)
    if seen is not None:
        scores = jnp.where(jnp.concatenate([seen, seen], 1) > 0.5, scores, NEG)
    expo = jnp.exp(scores - jnp.max(scores, 0, keepdims=True))
    return expo * (1.0 / jnp.sum(expo, 0, keepdims=True))


def pair_rows(refs, part, r, lanes, row_count):
    keys = refs[0].shape[0] // (2 * row_count)
    start = (part * row_count + r) * keys
    return jnp.concatenate([ref[start : start + keys, lanes] for ref in refs], 0)


def attend(query, pairs, seen, row_count):
    tokens, width = query.shape
    frames = tokens // row_count
    count = len(pairs)

    def body(*refs):
        query_ref, pair_refs, out_ref = refs[0], refs[1 : 1 + count], refs[-1]
        for r in range(row_count):
            span = slice(r * frames, (r + 1) * frames)
            for j in range(0, SPAN, 128):
                lanes = slice(j, j + 128)
                asked = two_heads(query_ref[span, lanes])
                key, value = [pair_rows(pair_refs, p, r, lanes, row_count) for p in range(2)]
                probs = row_probs(asked, key, refs[1 + count][r] if seen is not None else None)
                out_ref[span, lanes] = narrow(one_row(tdot(narrow(probs), value)))

    token_spec = pl.BlockSpec((tokens, SPAN), lambda i: (0, i))
    args = (query, *pairs)
    specs = [token_spec] + [pl.BlockSpec((pairs[0].shape[0], SPAN), lambda i: (0, i))] * count
    if seen is not None:
        args = args + (seen,)
        specs.append(whole(seen))
    return pl.pallas_call(
        body,
        grid=(width // SPAN,),
        out_shape=like((tokens, width), jnp.bfloat16),
        in_specs=specs,
        out_specs=token_spec,
        compiler_params=room(8),
        cost_estimate=hint(),
    )(*args)


def attend_back(query, pairs, seen, grads, tables, row_count, scale):
    tokens, width = query.shape
    frames = tokens // row_count
    count = len(pairs)
    block = pairs[0].shape[0]
    keys = block // (2 * row_count)

    def body(*refs):
        query_ref, grad_ref, pair_refs = refs[0], refs[1], refs[2 : 2 + count]
        rest = refs[2 + count :]
        out_ref = refs[-1]

        def put(part, r, lanes, value):
            for b in range(count):
                start = b * block + (part * row_count + r) * keys
                out_ref[start : start + keys, lanes] = narrow(value[b * keys : (b + 1) * keys])

        for r in range(row_count):
            span = slice(r * frames, (r + 1) * frames)
            for j in range(0, SPAN, 128):
                lanes = slice(j, j + 128)
                asked = two_heads(query_ref[span, lanes])
                grad = two_heads(grad_ref[span, lanes])
                key, value = [pair_rows(pair_refs, p, r, lanes, row_count) for p in range(2)]
                probs = row_probs(asked, key, rest[2][r] if seen is not None else None)
                score_grad = narrow(softmax_back(probs, dot_t(value, grad)))
                result = one_row(tdot(score_grad, key))
                if tables is not None:
                    result = spin(result, rest[0][span, :], rest[1][span, :])
                start = count * block + r * frames
                out_ref[start : start + frames, lanes] = narrow(result * scale)
                put(0, r, lanes, dot(score_grad, asked))
                put(1, r, lanes, dot(narrow(probs), grad))

    token_spec = pl.BlockSpec((tokens, SPAN), lambda i: (0, i))
    specs = [token_spec] * 2 + [pl.BlockSpec((block, SPAN), lambda i: (0, i))] * count
    args = (query, grads, *pairs)
    if tables is not None:
        specs = specs + [whole(table) for table in tables]
        args = args + tuple(tables)
    if seen is not None:
        specs.append(whole(seen))
        args = args + (seen,)
    return pl.pallas_call(
        body,
        grid=(width // SPAN,),
        out_shape=like((count * block + tokens, width), jnp.bfloat16),
        in_specs=specs,
        out_specs=pl.BlockSpec((count * block + tokens, SPAN), lambda i: (0, i)),
        compiler_params=room(12),
        cost_estimate=hint(),
    )(*args)


def multiply(left, right):
    rows, depth = left.shape
    width = right.shape[1]
    block = LANES if width % LANES == 0 else 384 if width % 384 == 0 else width

    def body(left_ref, right_ref, out_ref):
        out_ref[...] = narrow(dot(left_ref[...], right_ref[...]))

    return pl.pallas_call(
        body,
        grid=(width // block,),
        out_shape=like((rows, width), jnp.bfloat16),
        in_specs=[whole(left), pl.BlockSpec((depth, block), lambda i: (0, i))],
        out_specs=pl.BlockSpec((rows, block), lambda i: (0, i)),
        compiler_params=room(12),
        cost_estimate=hint(),
    )(left, right)


def weight_sums(lefts, rights, beside=None):
    rows = lefts[0].shape[1] // 2
    widths = [right.shape[1] for right in rights]
    count = len(lefts)
    if rows % 128:
        sums = [narrow(tdot(left, right)) for left, right in zip(lefts, rights)]
        sums = jnp.concatenate(sums + ([] if beside is None else [beside]), 1)
        return sums[:rows], sums[rows:]
    total = sum(widths) + (0 if beside is None else beside.shape[1])

    def body(*refs):
        for half in range(2):

            @pl.when(pl.program_id(0) == half)
            def _():
                start = 0
                for left, right, width in zip(refs[:count], refs[count : 2 * count], widths):
                    lanes = slice(start, start + width)
                    refs[half - 2][:, lanes] = narrow(tdot(left[...], right[...]))
                    start = start + width
                if beside is not None:
                    refs[half - 2][:, start:] = refs[2 * count][...]

    specs = [pl.BlockSpec((left.shape[0], rows), lambda i: (0, i)) for left in lefts]
    specs = specs + [whole(right) for right in rights]
    args = (*lefts, *rights)
    if beside is not None:
        args = args + (beside,)
        specs.append(pl.BlockSpec((rows, beside.shape[1]), lambda i: (i, 0)))
    out = pl.BlockSpec((rows, total), lambda i: (0, 0))
    return pl.pallas_call(
        body,
        grid=(2,),
        out_shape=[like((rows, total), jnp.bfloat16)] * 2,
        in_specs=specs,
        out_specs=[out, out],
        compiler_params=room(20),
        cost_estimate=hint(),
    )(*args)


def order_matrix(size, rows, order, me):
    masks = jnp.asarray(np.array(masks_of(order), np.int32))
    source = ((me ^ masks)[:, None] * rows + jnp.arange(rows, dtype=jnp.int32)[None, :]).reshape(-1)
    return (jnp.arange(size, dtype=jnp.int32)[:, None] == source[None, :]).astype(jnp.bfloat16)


def local(
    frames,
    prompt,
    clip_frames,
    upstream,
    first_gain,
    first_shift,
    self_project,
    self_output,
    second_gain,
    second_shift,
    cross_query,
    cross_memory,
    cross_output,
    third_gain,
    third_shift,
    feed_input,
    feed_lift,
    feed_output,
    feed_offset,
):
    row_count, frame_count, width = frames.shape
    heads = width // HEAD_DIM
    token_count = row_count * frame_count
    scale = HEAD_DIM ** (-0.5)
    batch_count = lax.axis_size(B)
    seq_count = lax.axis_size(S)
    device_count = batch_count * seq_count
    seq_place = lax.axis_index(S)
    me = lax.axis_index(B) * seq_count + seq_place
    share = first_gain.shape[0]

    seq_masks = [1 << i for i in range(seq_count.bit_length() - 1)]
    batch_masks = [seq_count << i for i in range(batch_count.bit_length() - 1)]
    near = batch_masks[:3]
    far = batch_masks[3:]
    x_mask, y_mask = batch_masks[:2]
    places = [(0, 3, 1, 2), (3, 1, 2, 0), (3, 2, 0, 1)]
    if len(batch_masks) != 4:
        places = [[(i + j) % len(batch_masks) for i in range(len(batch_masks))] for j in range(3)]
    tail_orders = [[batch_masks[i] for i in place] for place in places]
    near_orders = [near[j:] + near[:j] for j in range(3)]
    near_count = len(masks_of(near))
    third = (token_count * 3 // 8) // 16 * 16
    cuts = [0, third, 2 * third, token_count]
    units = feed_output.shape[0]

    vectors = [first_gain, first_shift, second_gain, second_shift, third_gain, third_shift, feed_offset]
    vectors = jnp.transpose(jnp.pad(jnp.stack(vectors, 0), ((0, 128 - len(vectors)), (0, 0))))
    split = 3 * width // 2
    group_one = narrow(jnp.concatenate([vectors, self_project], 1))
    memory_rows = ((0, share // 2 - cross_memory.shape[0]), (0, 0))
    memory_rows = jnp.concatenate(
        [
            jnp.pad(cross_memory[:, :width], memory_rows),
            jnp.pad(cross_memory[:, width:], memory_rows),
        ],
        0,
    )
    group_two = narrow(jnp.concatenate([self_output, cross_query, cross_output, memory_rows], 1))
    lift_rows = jnp.pad(feed_lift, ((0, 14), (0, width - units)))
    feed_sent = narrow(
        jnp.concatenate([feed_input.reshape(2 * units, width), feed_output, lift_rows], 0)
    )
    own_places = seq_place * frame_count + jnp.arange(frame_count, dtype=jnp.int32)
    key_order = masks_of(seq_masks)
    key_places = jnp.concatenate(
        [(seq_place ^ k) * frame_count + jnp.arange(frame_count, dtype=jnp.int32) for k in key_order]
    )
    own_clip, own_offset = clip_tables(clip_frames, own_places)
    key_clip = clip_tables(clip_frames, key_places)[0]
    seen = widen(own_clip[:, None, :] == key_clip[:, :, None])
    prompt_flat = prompt.reshape(-1, prompt.shape[2])
    rows = cross_memory.shape[0]
    place = jnp.arange(prompt.shape[2], dtype=jnp.int32)
    place = place // rows * share + place % rows
    places = jnp.arange(width, dtype=jnp.int32)[None, :]
    prompt_spread = [
        narrow(dot(prompt_flat, (place[:, None] + j * (share // 2) == places).astype(jnp.bfloat16)))
        for j in range(2)
    ]
    prompt_spread = jnp.concatenate(prompt_spread, 0)
    turn_tables = spin_tables(own_offset, 1.0)
    back_tables = spin_tables(own_offset, -1.0)

    def turn_rows(rows, matrix):
        return narrow(dot(rows, matrix))

    turned_memory = turn_rows(
        prompt_flat, order_matrix(prompt.shape[2], cross_memory.shape[0], tail_orders[2], me)
    )
    turned_memory = jnp.concatenate([turned_memory] * seq_count, 0)
    matrices = [order_matrix(width, share, order, me) for order in tail_orders]
    upstream_tokens = upstream.reshape(token_count, width)
    grad_drop_bias = jnp.sum(widen(upstream_tokens), 0, keepdims=True)
    early = [prompt_spread, turned_memory, seen, grad_drop_bias]
    early = early + matrices + list(turn_tables) + list(back_tables)

    known = [0]
    for mask in batch_masks[:1:-1]:
        group_one = jnp.concatenate([group_one, hop(group_one, mask)], 0)
        known = known + [old ^ mask for old in known]
    known = [known + [old ^ mask for old in known] for mask in (x_mask, y_mask)]
    group_one, group_two, *early = lax.optimization_barrier((group_one, group_two, *early))
    prompt_spread, turned_memory, seen, grad_drop_bias = early[:4]
    matrices, turn_tables, back_tables = early[4:7], early[7:9], early[9:]

    def pieces_of(columns, others):
        halves = []
        for h in range(2):
            have = known[h]
            pieces = [(columns[h], have), (others[h], [old ^ (y_mask, x_mask)[h] for old in have])]
            halves.append(pieces)
        return halves

    def add_core(halves, got):
        for h in range(2):
            halves[h] = halves[h] + [
                (piece, [old ^ seq_masks[0] for old in have])
                for piece, (_, have) in zip(got[h], halves[h])
            ]
            for mask in seq_masks[1:]:
                halves[h] = halves[h] + [
                    (hop(piece, mask), [old ^ mask for old in have]) for piece, have in halves[h]
                ]
        return halves

    core = seq_masks[0]
    traffic = Traffic()
    feed_parts = [feed_sent[2 * units :], feed_sent[: 2 * units]]
    ones = (group_one[:, : 128 + split], group_one[:, 128 + split :])
    group_two = gather(group_two, batch_masks[:2:-1])
    got = volley(ones, [x_mask, y_mask])
    ones = tuple(jnp.concatenate(pair, 0) for pair in zip(ones, got))
    got = volley(
        ones + (feed_parts[0], group_two, ones[0]),
        [y_mask, x_mask, far[0], batch_masks[2], core],
    )
    feed_got = [got[2]]
    group_two = jnp.concatenate([group_two, got[3]], 0)
    twos = (group_two[:, : 2 * width], group_two[:, 2 * width :])
    got_one = got[:2] + got[4:]
    got = volley(
        twos + (ones[1],) + got_one[:2], [x_mask, y_mask, core, core, core]
    )
    got_one = got_one + got[2:]
    twos = tuple(jnp.concatenate(pair, 0) for pair in zip(twos, got))
    halves = pieces_of(ones, got_one[:2])
    halves = add_core(halves, ((got_one[2], got_one[4]), (got_one[3], got_one[5])))
    new = {
        "two": once(twos + twos[:1], [y_mask, x_mask, core]),
        "feed": once(feed_parts[1:], far[:1]),
    }
    pieces = traffic.turn([piece for have in halves for piece, _ in have], lambda done: new)
    count = len(pieces) // 2
    halves = [
        [(piece, have) for piece, (_, have) in zip(pieces[h * count : (h + 1) * count], halves[h])]
        for h in range(2)
    ]
    packed, triple_low = settle(
        halves, [[(0, 0, 0, 128), (128, 1, 0, split)], [(0, 1, split, split)]], [128, 3 * width], me
    )
    packed = dot_t(jnp.eye(8, 128, dtype=jnp.bfloat16), packed)
    gain_one, shift_one, gain_two, shift_two, gain_three, shift_three, drop_bias = [
        packed[j : j + 1] for j in range(7)
    ]

    def cut_tokens(value):
        return [value[cuts[p] : cuts[p + 1]] for p in range(3)]

    def token_pairs(kept, got):
        pairs = []
        for p in range(3):
            first, last = near_count * cuts[p], near_count * cuts[p + 1]
            middle = (first + last) // 2
            pairs.append(
                [
                    narrow(widen(kept[rows]) + widen(got[rows]))
                    for rows in (slice(first, middle), slice(middle, last))
                ]
            )
        return pairs

    inputs = frames.reshape(token_count, width)
    query, pairs, normed_one, inverse_one, hidden_one = project(
        inputs, gain_one, shift_one, triple_low, turn_tables, scale
    )
    query, normed_one = traffic.turn(
        (query, normed_one),
        lambda done: {"pairs": double_list(pairs, seq_masks)},
        step=[],
    )
    for _ in seq_masks:
        (query,) = traffic.turn((query,), step=["pairs"])
    pairs = traffic.done["pairs"]
    self_mixed = attend(query, pairs, seen, row_count)

    def started(done):
        return {
            "last": once((twos[1],) + done["two"][:2], [core] * 3),
            "up": double_each(cut_tokens(upstream_tokens), near_orders),
        }

    self_mixed, *feed_all = traffic.turn([self_mixed] + feed_parts + feed_got, started)
    got_two = traffic.done["two"]
    feed_all.append(traffic.done["feed"][0])
    far_count = len(masks_of(far))
    unit_count = far_count * units
    drop_low, value_low, gate_low = [
        jnp.concatenate([part[rows : rows + units] for part in feed_all[p::2]], 0)
        for p, rows in ((0, 0), (1, 0), (1, units))
    ]
    biases = [part[units : units + 2, :units] for part in feed_all[::2]]
    biases = jnp.concatenate(biases, 1)
    for mask in far[1:]:
        drop_low, value_low, gate_low = [
            jnp.concatenate([low, hop(low, mask)], 0) for low in (drop_low, value_low, gate_low)
        ]
        biases = jnp.concatenate([biases, hop(biases, mask)], 1)
    value_bias, gate_bias = widen(biases[:1]), widen(biases[1:])
    self_mixed, value_low, gate_low, drop_low, value_bias, gate_bias = traffic.turn(
        (self_mixed, value_low, gate_low, drop_low, value_bias, gate_bias),
        lambda done: {"mixed": double_list(self_mixed, seq_masks)},
    )
    got = traffic.done["last"]
    halves = add_core(
        pieces_of(twos, got_two[:2]), ((got_two[2], got[1]), (got[0], got[2]))
    )
    lows = settle(
        halves,
        [[(0, 0, 0, width), (width, 1, 0, width)], [(0, 2, 0, width), (width, 3, 0, width)]],
        [width] * 4,
        me,
    )
    self_low, ask_low, cross_low, memory_low, self_mixed = traffic.turn(
        (*lows, self_mixed), lambda done: {"hidden": double_list(hidden_one, seq_masks)}
    )
    after_self, normed_two, inverse_two, hidden_two, asking = ahead(
        self_mixed, self_low, inputs, gain_two, shift_two, ask_low, scale
    )
    asking, prompt_spread = lax.optimization_barrier((asking, prompt_spread))
    memory = multiply(prompt_spread, memory_low)
    cross_mixed = attend(asking, [memory], None, row_count)
    (cross_mixed,) = traffic.turn(
        (cross_mixed,), lambda done: {"asked": double_list(hidden_two, seq_masks)}
    )
    after_cross, normed_three, inverse_three, hidden_three = ahead(
        cross_mixed, cross_low, after_self, gain_three, shift_three
    )

    hidden_three, cross_mixed = traffic.turn(
        (hidden_three, cross_mixed),
        lambda done: {
            "rows": double_each(cut_tokens(hidden_three), near_orders),
            "crossed": double_list(cross_mixed, seq_masks),
        },
        step=["asked"],
    )
    traffic.turn((), step=["rows", "crossed"])
    up = jnp.concatenate(traffic.done["up"], 0)
    traffic.turn((), lambda done: {"ups": double_list(up, seq_masks)}, step=["rows"])
    for _ in seq_masks[1:]:
        traffic.turn((), step=["asked", "crossed", "hidden", "mixed", "ups"])
    hidden_all, mixed_all, asked_all, cross_all = [
        jnp.concatenate(traffic.done[name], 0) for name in ("hidden", "mixed", "asked", "crossed")
    ]
    def rows_there(done):
        if "rows" not in done:
            return {}
        done["rows"] = jnp.concatenate(done["rows"], 0)
        return {"all": double_list(done["rows"], seq_masks)}

    hidden_all, mixed_all, asked_all, cross_all = traffic.turn(
        (hidden_all, mixed_all, asked_all, cross_all), rows_there
    )
    while "rows" in traffic.flows:
        traffic.turn((), rows_there)
    ups = traffic.done["ups"]
    lows = (value_low, gate_low, drop_low, value_bias, gate_bias)
    results = [feed_block(traffic.done["rows"], ups[0], *lows)]
    results[0] = traffic.turn(results[0])
    for _ in seq_masks[1:]:
        traffic.turn((), step=["all"])
    feed_rows = traffic.done["all"]
    for rows, up in zip(feed_rows[1:], ups[1:]):
        results.append(feed_block(rows, up, *lows))
    middles, value_grads, gate_grads, back_sums = [list(item) for item in zip(*results)]

    def back_flow():
        blocks = back_sums
        for mask in reversed(seq_masks):
            half = len(blocks) // 2
            sent = yield tuple(blocks[half:])
            got = yield hops(sent, (mask,) * half)
            if half > 1:
                blocks = [narrow(widen(a) + widen(b)) for a, b in zip(blocks[:half], got)]
        return (yield from halve_pairs(token_pairs(blocks[0], got[0]), near_orders))

    blocks = len(feed_rows)
    tied = traffic.turn(middles + value_grads + gate_grads, lambda done: {"back": back_flow()})
    middles, value_grads, gate_grads = tied[:blocks], tied[blocks : 2 * blocks], tied[2 * blocks :]
    drop_grad = unit_grad(middles, ups, False)[0]
    tied = traffic.turn((drop_grad, hidden_all, *value_grads, *gate_grads))
    for _ in seq_masks[1:]:
        tied = traffic.turn(tied)
    drop_grad, hidden_all, tied = tied[0], tied[1], tied[2:]
    value_grads, gate_grads = tied[:blocks], tied[blocks:]
    turned_triple = [turn_rows(hidden_all, matrix) for matrix in matrices]
    value_grad, value_bias_grad = unit_grad(value_grads, feed_rows, True)
    gate_grad, gate_bias_grad = unit_grad(gate_grads, feed_rows, True)

    def unit_blocks(grad):
        return [grad[k * units : (k + 1) * units] for k in range(far_count)]

    bias_grads = [
        narrow(
            jnp.pad(
                jnp.concatenate(
                    [bias[:, k * units : (k + 1) * units] for bias in (value_bias_grad, gate_bias_grad)], 0
                ),
                ((0, 14), (0, width - units)),
            )
        )
        for k in range(far_count)
    ]

    def unit_flow(p):
        blocks = unit_blocks((drop_grad, drop_grad, value_grad, value_grad, gate_grad)[p])
        if p == 4:
            blocks = [jnp.concatenate(pair, 0) for pair in zip(blocks, bias_grads)]
            return halve_rows(blocks, 0, units + 16, far)
        half = units // 2
        return halve_rows(blocks, p % 2 * half, (p % 2 + 1) * half, far)

    value_grad, gate_grad, drop_grad, mixed_all, *turned_triple = traffic.turn(
        [value_grad, gate_grad, drop_grad, mixed_all] + turned_triple,
        lambda done: {"unit0": unit_flow(0)},
    )
    turned_self = [turn_rows(mixed_all, matrix) for matrix in matrices]

    term_sums = [multiply(middle, drop_low) for middle in middles]

    def term_flow():
        blocks = term_sums
        for mask in reversed(seq_masks):
            half = len(blocks) // 2
            sent = yield tuple(blocks[half:])
            got = yield hops(sent, (mask,) * half)
            if half > 1:
                blocks = [narrow(widen(a) + widen(b)) for a, b in zip(blocks[:half], got)]
        return blocks[0], got[0]

    cross_all, asked_all, *turned_self = traffic.turn(
        [cross_all, asked_all] + turned_self, lambda done: {"term": term_flow()}
    )
    turned_cross = turn_rows(cross_all, matrices[0])
    turned_ask = turn_rows(asked_all, matrices[1])
    for _ in seq_masks[1:]:
        traffic.turn((), step=["term"])
    while "back" in traffic.flows:
        turned_cross, turned_ask = traffic.turn((turned_cross, turned_ask), step=["back", "term"])

    while "back" in traffic.flows:
        unit_sums = list(traffic.turn(unit_sums, step=["back", "term"]))
    feed_back = jnp.concatenate(traffic.done["back"], 0)
    (feed_back,) = traffic.turn(
        (feed_back,),
        lambda done: {
            "term_near": halve_pairs(token_pairs(*done["term"]), near_orders),
        },
    )
    cross_out_grad, grad_gain_three, grad_shift_three, cross_branch, cross_mixed_grad = back(
        feed_back, None, upstream_tokens, normed_three, inverse_three, gain_three, cross_low
    )

    def weight_pair(turned, *grads):
        half = turned.shape[1] // 2
        pair = []
        for columns in (turned[:, :half], turned[:, half:]):
            sums = [narrow(tdot(columns, grad)) for grad in grads]
            if len(grads) > 1:
                rows = cross_memory.shape[0]
                sums = [
                    jnp.pad(part.reshape(-1, rows, width), ((0, 0), (0, share // 2 - rows), (0, 0)))
                    for part in sums
                ]
                sums = [jnp.concatenate(sums, 1).reshape(-1, width)]
            pair.append(sums[0])
        return tuple(pair)

    (cross_mixed_grad,) = traffic.turn(
        (cross_mixed_grad,),
        lambda done: {"dc": double_list(cross_branch, seq_masks), "unit1": unit_flow(1)},
    )
    asked_grad = attend_back(
        asking, [memory], None, cross_mixed_grad, None, row_count, scale
    )
    (asked_grad,) = traffic.turn(
        (asked_grad,),
        lambda done: {"dq": double_list(asked_grad, seq_masks), "unit2": unit_flow(2)},
    )
    for _ in seq_masks[1:]:
        traffic.turn((), step=["dc"])
    self_out_grad, grad_gain_two, grad_shift_two, self_branch, self_mixed_grad = back(
        asked_grad,
        ask_low,
        cross_out_grad,
        normed_two,
        inverse_two,
        gain_two,
        self_low,
        memory.shape[0] // token_count,
    )
    (self_mixed_grad,) = traffic.turn(
        (self_mixed_grad,),
        lambda done: {"da": double_list(self_branch, seq_masks)},
    )
    for _ in seq_masks[1:]:
        traffic.turn((), step=["dq", "da"])
    cross_pair = weight_pair(turned_cross, jnp.concatenate(traffic.done["dc"], 0))
    layer_output = narrow(
        after_cross + jnp.concatenate(traffic.done["term_near"], 0) + drop_bias
    )
    memory_all = traffic.done["dq"]
    half = memory.shape[0] // 2
    ask_pair = weight_pair(turned_ask, jnp.concatenate([part[2 * half :] for part in memory_all], 0))
    memory_pair = weight_pair(
        turned_memory,
        jnp.concatenate([part[:half] for part in memory_all], 0),
        jnp.concatenate([part[half : 2 * half] for part in memory_all], 0),
    )
    self_mixed_grad, layer_output = traffic.turn(
        (self_mixed_grad, layer_output),
        lambda done: {
            "first": halve_pairs([cross_pair, ask_pair, memory_pair], tail_orders),
        },
    )
    pair_grad = attend_back(
        query, pairs, seen, self_mixed_grad, back_tables, row_count, scale
    )

    def shed_frames(value):
        query_grad = value[-token_count:]
        count = value.shape[0] - token_count
        for mask in reversed(seq_masks):
            half = count // 2
            (sent,) = yield (value[half:count],)
            (got,) = yield hops((sent,), (mask,))
            if mask > seq_masks[0]:
                value = narrow(widen(value[:half]) + widen(got))
                count = half
        if len(seq_masks) > 1:
            value = jnp.concatenate([value, query_grad], 0)
        return value, got

    (pair_grad,) = traffic.turn((pair_grad,), lambda done: {"pair": shed_frames(pair_grad)}, step=[])
    for _ in seq_masks:
        traffic.turn((), step=["pair"])
    triple_back = spin_backward(*traffic.done["pair"], *back_tables)
    (triple_back,) = traffic.turn(
        (triple_back,), lambda done: {"dt": double_list(triple_back, seq_masks)}
    )
    frame_grad, grad_gain_one, grad_shift_one = back(
        triple_back, triple_low, self_out_grad, normed_one, inverse_one, gain_one
    )
    branch_all = jnp.concatenate(traffic.done["da"], 0)
    shares = [0, width // 6, width // 3, width]
    sums = [
        grad_gain_one,
        grad_shift_one,
        grad_gain_two,
        grad_shift_two,
        grad_gain_three,
        grad_shift_three,
        grad_drop_bias,
    ]
    sums = jnp.pad(jnp.concatenate(sums, 0), ((0, 1), (0, 0)))
    frame_grad, sums = traffic.turn((frame_grad, sums), lambda done: {"sums": double_list(sums, seq_masks)})
    for _ in seq_masks:
        traffic.turn((), step=["dt", "sums"])
    triple_all = jnp.concatenate(traffic.done["dt"], 0)
    sums = sum(traffic.done["sums"])
    sums_turned = tdot(matrices[1], narrow(jnp.transpose(sums)))
    sums_turned = narrow(jnp.pad(sums_turned, ((0, 0), (0, 120))))

    def triple_pair(p, beside=None):
        grads = [
            triple_all[:, p * width : (p + 1) * width],
            branch_all[:, shares[p] : shares[p + 1]],
        ]
        return list(weight_sums([turned_triple[p], turned_self[p]], grads, beside))

    triple_pairs = [triple_pair(0), None, triple_pair(2)]
    while traffic.count["first"] < len(batch_masks) - 1:
        traffic.turn(())

    def tail_first(*which):
        return once([triple_pairs[p][1] for p in which], [tail_orders[p][-1] for p in which])

    (sums_turned,) = traffic.turn((sums_turned,), lambda done: {"early": tail_first(0, 2)})
    triple_pairs[1] = triple_pair(1, sums_turned)
    (triple_pairs[1][1],) = traffic.turn(
        (triple_pairs[1][1],),
        lambda done: {"unit4": unit_flow(4)},
        step=["first"],
    )
    traffic.turn((), lambda done: {"late": tail_first(1)}, step=[])

    def tail_rest(done):
        got = (done["early"][0], done["late"][0], done["early"][1])
        pairs = []
        for (kept, _), part in zip(triple_pairs, got):
            half = kept.shape[0] // 2
            pairs.append(
                [
                    narrow(widen(kept[rows]) + widen(part[rows]))
                    for rows in (slice(half), slice(half, None))
                ]
            )
        orders = [order[:-1] for order in tail_orders]
        return {"tail": halve_pairs(pairs, orders), "unit3": unit_flow(3)}

    traffic.turn((), tail_rest)
    while traffic.flows:
        traffic.turn(())
    parts = traffic.done["tail"]
    grad_cross, grad_ask, grad_memory = traffic.done["first"]
    grad_self = jnp.concatenate(
        [part[:, width : width + shares[p + 1] - shares[p]] for p, part in enumerate(parts)], 1
    )
    drop_sums = jnp.concatenate([traffic.done[name] for name in UNITS[:2]], 0)
    value_sums = jnp.concatenate([traffic.done[name] for name in UNITS[2:4]], 0)
    gate_sums = traffic.done[UNITS[4]]
    grad_triple = jnp.concatenate([part[:, :width] for part in parts], 1)
    sums = width + shares[2] - shares[1]
    sums = jnp.transpose(parts[1][:, sums : sums + 7])
    grad_memory = grad_memory.reshape(2, share // 2, width)[:, : cross_memory.shape[0]]
    grad_memory = jnp.concatenate([grad_memory[0], grad_memory[1]], 1)
    grad_lift = jnp.stack([value_sums, gate_sums[:units]], 0)
    grad_drop = drop_sums
    grad_lift_bias = gate_sums[units : units + 2, :units]
    shape = frames.shape
    return (
        layer_output.reshape(shape),
        frame_grad.reshape(shape),
        sums[0],
        sums[1],
        grad_triple,
        grad_self,
        sums[2],
        sums[3],
        grad_ask,
        grad_memory,
        grad_cross,
        sums[4],
        sums[5],
        grad_lift,
        grad_lift_bias,
        grad_drop,
        sums[6],
    )


def solution(mesh):
    both = P(AX)
    wide = P(AX, None)
    rows = P(B, S, None)
    units = P(None, AX, None)
    in_specs = (
        rows,
        P(B, None, None),
        P(B, None),
        rows,
        both,
        both,
        wide,
        wide,
        both,
        both,
        wide,
        wide,
        wide,
        both,
        both,
        units,
        P(None, AX),
        wide,
        both,
    )
    out_specs = (
        rows,
        rows,
        both,
        both,
        wide,
        wide,
        both,
        both,
        wide,
        wide,
        wide,
        both,
        both,
        units,
        P(None, AX),
        wide,
        both,
    )
    return jax.shard_map(local, mesh=mesh, in_specs=in_specs, out_specs=out_specs, check_vma=False)
```

```python
import jax
import jax.numpy as jnp
import numpy as np
from jax import lax
from jax.experimental import pallas as pl
from jax.experimental.pallas import tpu as pltpu
from jax.sharding import PartitionSpec as P

HEAD_DIM = 64
LANES = 1536
SPAN = 512
UNITS = ["unit0", "unit1", "unit2", "unit3", "unit4"]
EPS = 1e-05
NEG = -1e30
B = "batch"
S = "seq"
AX = (B, S)


def narrow(value):
    return value.astype(jnp.bfloat16)


def widen(value):
    return value.astype(jnp.float32)


def mult(left, right, form):
    return jnp.einsum(form, left, right, preferred_element_type=jnp.float32)


def dot(left, right):
    return lax.dot_general(left, right, (((1,), (0,)), ((), ())), preferred_element_type=jnp.float32)


def dot_t(left, right):
    return lax.dot_general(left, right, (((1,), (1,)), ((), ())), preferred_element_type=jnp.float32)


def tdot(left, right):
    return lax.dot_general(left, right, (((0,), (0,)), ((), ())), preferred_element_type=jnp.float32)


def standardize(values):
    center = values - jnp.mean(values, -1, keepdims=True)
    inverse = lax.rsqrt(jnp.mean(center * center, -1, keepdims=True) + EPS)
    return (center * inverse, inverse)


def norm_back(incoming, normed, inverse, gain):
    scaled = incoming * gain
    inner = (
        scaled
        - jnp.mean(scaled, -1, keepdims=True)
        - normed * jnp.mean(scaled * normed, -1, keepdims=True)
    )
    return (
        inner * inverse,
        jnp.sum(incoming * normed, 0, keepdims=True),
        jnp.sum(incoming, 0, keepdims=True),
    )


def clip_tables(lengths, places):
    ends = jnp.cumsum(lengths, 1)
    later = places[None, :, None] >= ends[:, None, :]
    ident = jnp.sum(later.astype(jnp.int32), 2)
    starts = jnp.max(jnp.where(later, ends[:, None, :], 0), 2)
    return (ident, places[None, :] - starts)


def softmax_back(probs, prob_grad):
    return probs * (prob_grad - jnp.sum(probs * prob_grad, 0, keepdims=True))


def hop(value, mask):
    count = lax.axis_size(B) * lax.axis_size(S)
    return lax.ppermute(value, AX, [(i, i ^ mask) for i in range(count)])


def volley(values, masks):
    values = lax.optimization_barrier(tuple(values))
    return lax.optimization_barrier(tuple(hop(value, mask) for value, mask in zip(values, masks)))


def masks_of(order):
    masks = [0]
    for mask in order:
        masks = masks + [old ^ mask for old in masks]
    return masks


def gather(value, order):
    for mask in order:
        value = jnp.concatenate([value, hop(value, mask)], 0)
    return value


def settle(halves, targets, widths, me):
    pieces = [(h, piece, have) for h in range(len(halves)) for piece, have in halves[h]]
    total = sum(len(have) for h, piece, have in pieces if h == 0)
    rows = pieces[0][1].shape[0] // len(pieces[0][2])
    if rows % 16:
        outs = [[] for _ in widths]
        for h in range(len(halves)):
            have = sum([have for _, have in halves[h]], [])
            table = np.zeros(total, np.int32)
            table[np.array(have)] = np.arange(total)
            place = jnp.asarray(table)[me ^ jnp.arange(total, dtype=jnp.int32)]
            blocks = jnp.concatenate([piece for piece, _ in halves[h]], 0).reshape(total, rows, -1)
            blocks = jnp.take(blocks, place, axis=0).reshape(total * rows, -1)
            for source, out, _, count in targets[h]:
                outs[out].append(blocks[:, source : source + count])
        return [jnp.concatenate(out, 1) for out in outs]

    def body(me_ref, *refs):
        ins = refs[: len(pieces)]
        outs = refs[len(pieces) : len(pieces) + len(widths)]
        held = refs[len(pieces) + len(widths) : -2]
        in_sems, out_sems = refs[-2:]
        loads = []
        for i in range(len(pieces)):
            load = pltpu.make_async_copy(ins[i], held[i], in_sems.at[i])
            load.start()
            loads.append(load)
        stores = []
        for i, (h, _, have) in enumerate(pieces):
            loads[i].wait()
            for j, mask in enumerate(have):
                start = pl.multiple_of((me_ref[0] ^ mask) * rows, rows)
                for source, out, column, count in targets[h]:
                    store = pltpu.make_async_copy(
                        held[i].at[pl.ds(j * rows, rows), pl.ds(source, count)],
                        outs[out].at[pl.ds(start, rows), pl.ds(column, count)],
                        out_sems.at[len(stores)],
                    )
                    store.start()
                    stores.append(store)
        for store in stores:
            store.wait()

    count = sum(len(have) * len(targets[h]) for h, _, have in pieces)
    size = 2 * sum(piece.size for _, piece, _ in pieces)
    return pl.pallas_call(
        body,
        out_shape=[jax.ShapeDtypeStruct((total * rows, width), jnp.bfloat16) for width in widths],
        in_specs=[pl.BlockSpec(memory_space=pltpu.SMEM)]
        + [pl.BlockSpec(memory_space=pl.ANY)] * len(pieces),
        out_specs=[pl.BlockSpec(memory_space=pltpu.HBM)] * len(widths),
        scratch_shapes=[pltpu.VMEM(piece.shape, jnp.bfloat16) for _, piece, _ in pieces]
        + [pltpu.SemaphoreType.DMA((len(pieces),)), pltpu.SemaphoreType.DMA((count,))],
        compiler_params=pltpu.CompilerParams(vmem_limit_bytes=size + (2 << 20)),
        cost_estimate=pl.CostEstimate(flops=0, bytes_accessed=size // 16, transcendentals=0),
    )(me.reshape(1), *[piece for _, piece, _ in pieces])


class Traffic:
    def __init__(self):
        self.flows = {}
        self.done = {}
        self.count = {}

    def turn(self, outs, new=None, step=None):
        names = list(self.flows) if step is None else [n for n in step if n in self.flows]
        gots = sum([self.flows[name][1] for name in names], ())
        tied = lax.optimization_barrier(gots + tuple(outs))
        outs = tied[len(gots) :]
        started = []
        for name in names:
            flow, got = self.flows.pop(name)
            got, tied = tied[: len(got)], tied[len(got) :]
            try:
                started.append((name, flow, flow.send(got)))
            except StopIteration as end:
                self.done[name] = end.value
        if new is not None:
            flows = new(self.done)
            for name, flow in ((name, flow) for name, flow in flows.items() if flow is not None):
                started.append((name, flow, next(flow)))
        sents = sum([sent for _, _, sent in started], ())
        tied = lax.optimization_barrier(sents + outs)
        for name, flow, sent in started:
            self.count[name] = self.count.get(name, 0) + 1
            self.flows[name] = (flow, flow.send(tied[: len(sent)]))
            tied = tied[len(sent) :]
        return tied


def hops(values, masks):
    return tuple(hop(value, mask) for value, mask in zip(values, masks))


def once(values, masks):
    values = yield tuple(values)
    return (yield hops(values, masks))


def halve_pairs(pairs, orders):
    for step in list(zip(*orders))[::-1]:
        sent = yield tuple(sent for _, sent in pairs)
        got = yield hops(sent, step)
        sums = [(kept, part) for (kept, _), part in zip(pairs, got)]
        pairs = []
        for kept, part in sums:
            half = kept.shape[0] // 2
            pair = [widen(kept[cut]) + widen(part[cut]) for cut in (slice(half), slice(half, None))]
            pairs.append(pair if kept.ndim == 3 else [narrow(item) for item in pair])
    return [widen(kept) + widen(part) for kept, part in sums]


def halve_list(blocks, masks):
    for mask in reversed(masks):
        half = len(blocks) // 2
        sent = yield tuple(narrow(block) for block in blocks[half:])
        got = yield hops(sent, (mask,) * half)
        blocks = [widen(a) + widen(b) for a, b in zip(blocks[:half], got)]
    return blocks[0]


def halve_rows(blocks, first, last, masks):
    for mask in reversed(masks):
        half = len(blocks) // 2
        sent = yield tuple(narrow(block[first:last]) for block in blocks[half:])
        got = yield hops(sent, (mask,) * half)
        blocks = [widen(a[first:last]) + widen(b) for a, b in zip(blocks[:half], got)]
        first, last = 0, last - first
    return blocks[0]


def double_each(parts, orders):
    for step in zip(*orders):
        parts = yield tuple(parts)
        got = yield hops(parts, step)
        pairs = list(zip(parts, got))
        parts = [jnp.concatenate(pair, 0) for pair in pairs]
    return sum(pairs, ())


def double_list(value, masks):
    blocks = (value,)
    for mask in masks:
        blocks = yield blocks
        got = yield hops(blocks, (mask,) * len(blocks))
        blocks = tuple(blocks) + tuple(got)
    return blocks


def spin(value, cosine, sine):
    lane = lax.broadcasted_iota(jnp.int32, value.shape, 1)
    other = jnp.where(lane % 64 < 32, pltpu.roll(value, 96, 1), pltpu.roll(value, 32, 1))
    return value * cosine + other * sine


def spin_tables(offsets, sign):
    half = HEAD_DIM // 2
    freq = 10000.0 ** (-jnp.arange(half, dtype=jnp.float32) / half)
    angle = offsets.astype(jnp.float32).reshape(-1, 1) * freq
    cosine = jnp.cos(angle)
    sine = sign * jnp.sin(angle)
    return (jnp.concatenate([cosine] * 4, 1), jnp.concatenate([-sine, sine, -sine, sine], 1))


def hint():
    return pl.CostEstimate(flops=1 << 20, bytes_accessed=1 << 20, transcendentals=0)


def whole(array):
    return pl.BlockSpec(array.shape, lambda i: (0,) * array.ndim)


def like(shape, dtype=jnp.float32):
    return jax.ShapeDtypeStruct(shape, dtype)


def room(mebibytes):
    return pltpu.CompilerParams(vmem_limit_bytes=mebibytes << 20)


def project(inputs, gain, shift, weight, tables, scale):
    rows, width = inputs.shape
    block = width

    def body(in_ref, gain_ref, shift_ref, cos_ref, sin_ref, weight_ref, *outs):
        query_ref, pair_ref, normed_ref, inverse_ref, hidden_ref = outs
        step = pl.program_id(0)

        @pl.when(step == 0)
        def _():
            normed, inverse = standardize(widen(in_ref[...]))
            normed_ref[...] = normed
            inverse_ref[...] = inverse
            hidden_ref[...] = narrow(normed * gain_ref[...] + shift_ref[...])

        value = dot(hidden_ref[...], weight_ref[...])

        def turned(factor):
            parts = [
                spin(value[:, j : j + 128], cos_ref[...], sin_ref[...]) for j in range(0, block, 128)
            ]
            return [narrow(part * factor) for part in parts]

        @pl.when(step == 0)
        def _():
            for j, part in enumerate(turned(scale)):
                query_ref[:, 128 * j : 128 * j + 128] = part

        @pl.when(step == 1)
        def _():
            for j, part in enumerate(turned(1.0)):
                pair_ref[:, 128 * j : 128 * j + 128] = part

        @pl.when(step == 2)
        def _():
            pair_ref[...] = narrow(value)

    return pl.pallas_call(
        body,
        grid=(3,),
        out_shape=[
            like((rows, width), jnp.bfloat16),
            like((2 * rows, width), jnp.bfloat16),
            like((rows, width)),
            like((rows, 1)),
            like((rows, width), jnp.bfloat16),
        ],
        in_specs=[
            whole(inputs),
            whole(gain),
            whole(shift),
            whole(tables[0]),
            whole(tables[1]),
            pl.BlockSpec((width, block), lambda i: (0, i)),
        ],
        out_specs=[
            pl.BlockSpec((rows, block), lambda i: (0, 0)),
            pl.BlockSpec((rows, block), lambda i: (jnp.maximum(i - 1, 0), 0)),
            pl.BlockSpec((rows, width), lambda i: (0, 0)),
            pl.BlockSpec((rows, 1), lambda i: (0, 0)),
            pl.BlockSpec((rows, width), lambda i: (0, 0)),
        ],
        compiler_params=room(22),
        cost_estimate=hint(),
    )(inputs, gain, shift, *tables, weight)


def ahead(mixed, low, before, gain, shift, ask=None, scale=1.0):
    rows, width = before.shape
    steps = width // LANES

    def body(mixed_ref, before_ref, gain_ref, shift_ref, *refs):
        low_ref, refs = refs[0], refs[1:]
        if ask is not None:
            ask_ref, refs = refs[0], refs[1:]
        sum_ref, normed_ref, inverse_ref, hidden_ref = refs[:4]
        step = pl.program_id(0)

        @pl.when(step < steps)
        def _():
            lanes = pl.ds(pl.multiple_of(step * LANES, LANES), LANES)
            sum_ref[:, lanes] = widen(before_ref[:, lanes]) + dot(mixed_ref[...], low_ref[...])

        @pl.when(step == steps - 1)
        def _():
            normed, inverse = standardize(sum_ref[...])
            normed_ref[...] = normed
            inverse_ref[...] = inverse
            hidden_ref[...] = narrow(normed * gain_ref[...] + shift_ref[...])

        if ask is not None:

            @pl.when(step >= steps)
            def _():
                refs[4][...] = narrow(dot(hidden_ref[...], ask_ref[...]) * scale)

    full = pl.BlockSpec((rows, width), lambda i: (0, 0))
    args = (mixed, before, gain, shift, low)
    specs = [whole(mixed), whole(before), whole(gain), whole(shift)]
    specs.append(pl.BlockSpec((width, LANES), lambda i: (0, jnp.minimum(i, steps - 1))))
    shapes = [
        like((rows, width)),
        like((rows, width)),
        like((rows, 1)),
        like((rows, width), jnp.bfloat16),
    ]
    outs = [full, full, pl.BlockSpec((rows, 1), lambda i: (0, 0)), full]
    if ask is not None:
        args = args + (ask,)
        specs.append(pl.BlockSpec((width, LANES), lambda i: (0, jnp.maximum(i - steps, 0))))
        shapes.append(like((rows, width), jnp.bfloat16))
        outs.append(pl.BlockSpec((rows, LANES), lambda i: (0, jnp.maximum(i - steps, 0))))
    return pl.pallas_call(
        body,
        grid=(steps if ask is None else 2 * steps,),
        out_shape=shapes,
        in_specs=specs,
        out_specs=outs,
        compiler_params=room(16),
        cost_estimate=hint(),
    )(*args)


def back(incoming, low, grads, normed, inverse, gain, out=None, place=0):
    rows, width = grads.shape
    block = LANES
    first = 0 if low is None else width // block
    last = 0 if out is None else width // LANES
    norm_step = max(first - 1, 0)

    def body(in_ref, grad_ref, normed_ref, inverse_ref, gain_ref, *refs):
        if low is not None:
            low_ref, refs = refs[0], refs[1:]
        if out is not None:
            out_ref, refs = refs[0], refs[1:]
        sum_ref, gain_grad_ref, shift_grad_ref = refs[:3]
        held_ref = refs[-1]
        step = pl.program_id(0)
        if low is not None:

            @pl.when(step < first)
            def _():
                lanes = pl.ds(pl.multiple_of(step * block, block), block)
                held_ref[:, lanes] = dot_t(in_ref[...], low_ref[...])

        @pl.when(step == norm_step)
        def _():
            value = in_ref[...] if low is None else held_ref[...]
            inner, gain_grad, shift_grad = norm_back(
                value, normed_ref[...], inverse_ref[...], gain_ref[...]
            )
            total = widen(grad_ref[...]) + inner
            sum_ref[...] = total
            gain_grad_ref[...] = gain_grad
            shift_grad_ref[...] = shift_grad
            if out is not None:
                refs[3][...] = narrow(total)

        if out is not None:

            @pl.when(step >= first)
            def _():
                refs[4][...] = narrow(dot_t(refs[3][...], out_ref[...]))

    full = pl.BlockSpec((rows, width), lambda i: (0, 0))
    line = pl.BlockSpec((1, width), lambda i: (0, 0))
    args = (incoming, grads, normed, inverse, gain)
    specs = [whole(array) for array in args]
    specs[0] = pl.BlockSpec((rows, incoming.shape[1]), lambda i: (place, 0))
    if low is not None:
        args = args + (low,)
        specs.append(pl.BlockSpec((block, low.shape[1]), lambda i: (jnp.minimum(i, first - 1), 0)))
    shapes = [like((rows, width)), like((1, width)), like((1, width))]
    outs = [full, line, line]
    if out is not None:
        args = args + (out,)
        specs.append(pl.BlockSpec((LANES, width), lambda i: (jnp.maximum(i - first, 0), 0)))
        shapes = shapes + [like((rows, width), jnp.bfloat16)] * 2
        outs = outs + [full, pl.BlockSpec((rows, LANES), lambda i: (0, jnp.maximum(i - first, 0)))]
    return pl.pallas_call(
        body,
        grid=(first + last,),
        out_shape=shapes,
        in_specs=specs,
        out_specs=outs,
        scratch_shapes=[pltpu.VMEM((rows, width), jnp.float32)],
        compiler_params=room(24),
        cost_estimate=hint(),
    )(*args)


def feed_block(rows, ups, value_low, gate_low, drop_low, value_bias, gate_bias):
    count, width = rows.shape
    units = drop_low.shape[0]
    block = min(count, 256)

    def body(row_ref, up_ref, value_ref, gate_ref, drop_ref, value_bias_ref, gate_bias_ref, *outs):
        middle_ref, value_out, gate_out, back_ref = outs
        middle_grad = widen(narrow(dot_t(up_ref[...], drop_ref[...])))
        value = dot_t(row_ref[...], value_ref[...]) + value_bias_ref[...]
        gate = dot_t(row_ref[...], gate_ref[...]) + gate_bias_ref[...]
        sigma = jax.nn.sigmoid(gate)
        middle = narrow(value * gate * sigma)
        value_grad = narrow(middle_grad * gate * sigma)
        gate_grad = narrow(middle_grad * value * sigma * (1.0 + gate * (1.0 - sigma)))
        middle_ref[...] = middle
        value_out[...] = value_grad
        gate_out[...] = gate_grad
        back_ref[...] = narrow(dot(value_grad, value_ref[...]) + dot(gate_grad, gate_ref[...]))

    wide = pl.BlockSpec((block, width), lambda i: (i, 0))
    thin = pl.BlockSpec((block, units), lambda i: (i, 0))
    args = (rows, ups, value_low, gate_low, drop_low, value_bias, gate_bias)
    return pl.pallas_call(
        body,
        grid=(count // block,),
        out_shape=[like((count, units), jnp.bfloat16)] * 3 + [like((count, width), jnp.bfloat16)],
        in_specs=[wide, wide] + [whole(array) for array in args[2:]],
        out_specs=[thin] * 3 + [wide],
        compiler_params=room(32),
        cost_estimate=hint(),
    )(*args)


def unit_grad(lefts, rights, sums):
    units = lefts[0].shape[1]
    width = rights[0].shape[1]
    count = len(lefts)
    block = 128 if units % 128 == 0 else units

    def body(*refs):
        total = 0.0
        for left, right in zip(refs[:count], refs[count : 2 * count]):
            total = total + tdot(left[...], right[...])
        refs[2 * count][...] = narrow(total)
        if sums:
            refs[2 * count + 1][...] = sum(
                jnp.sum(widen(left[...]), 0, keepdims=True) for left in refs[:count]
            )

    specs = [pl.BlockSpec((left.shape[0], block), lambda i: (0, i)) for left in lefts]
    outs = [pl.BlockSpec((block, width), lambda i: (i, 0))]
    shapes = [like((units, width), jnp.bfloat16)]
    if sums:
        outs.append(pl.BlockSpec((1, block), lambda i: (0, i)))
        shapes.append(like((1, units)))
    return pl.pallas_call(
        body,
        grid=(units // block,),
        out_shape=shapes,
        in_specs=specs + [whole(right) for right in rights],
        out_specs=outs,
        compiler_params=room(24),
        cost_estimate=hint(),
    )(*lefts, *rights)


def spin_backward(grads, got, cosine, sine):
    rows, width = got.shape[0] // 2, got.shape[1]
    last = grads.shape[0] // rows - 1

    def body(cos_ref, sin_ref, query_ref, own_ref, got_ref, out_ref):
        step = pl.program_id(0)

        @pl.when(step == 0)
        def _():
            out_ref[...] = query_ref[...]

        @pl.when(step == 1)
        def _():
            for j in range(0, width, 128):
                value = widen(own_ref[:, j : j + 128]) + widen(got_ref[:, j : j + 128])
                out_ref[:, j : j + 128] = narrow(spin(value, cos_ref[...], sin_ref[...]))

        @pl.when(step == 2)
        def _():
            out_ref[...] = narrow(widen(own_ref[...]) + widen(got_ref[...]))

    table = pl.BlockSpec((rows, 128), lambda i: (0, 0))
    part = pl.BlockSpec((rows, width), lambda i: (jnp.maximum(i - 1, 0), 0))
    return pl.pallas_call(
        body,
        grid=(3,),
        out_shape=jax.ShapeDtypeStruct((rows, 3 * width), jnp.bfloat16),
        in_specs=[table, table, pl.BlockSpec((rows, width), lambda i: (last, 0)), part, part],
        out_specs=pl.BlockSpec((rows, width), lambda i: (0, i)),
        compiler_params=room(8),
        cost_estimate=pl.CostEstimate(
            flops=1 << 20, bytes_accessed=1 << 20, transcendentals=0
        ),
    )(cosine, sine, grads, grads, got)


def two_heads(value):
    lane = lax.broadcasted_iota(jnp.int32, value.shape, 1)
    zero = jnp.zeros_like(value)
    first = jnp.where(lane < HEAD_DIM, value, zero)
    second = jnp.where(lane < HEAD_DIM, zero, value)
    return jnp.concatenate([first, second], 0)


def one_row(value):
    half = value.shape[0] // 2
    lane = lax.broadcasted_iota(jnp.int32, (half, value.shape[1]), 1)
    return jnp.where(lane < HEAD_DIM, value[:half], value[half:])


def row_probs(asked, keys, seen):
    scores = dot_t(keys, asked)
    if seen is not None:
        scores = jnp.where(jnp.concatenate([seen, seen], 1) > 0.5, scores, NEG)
    expo = jnp.exp(scores - jnp.max(scores, 0, keepdims=True))
    return expo * (1.0 / jnp.sum(expo, 0, keepdims=True))


def pair_rows(refs, part, r, lanes, row_count):
    keys = refs[0].shape[0] // (2 * row_count)
    start = (part * row_count + r) * keys
    return jnp.concatenate([ref[start : start + keys, lanes] for ref in refs], 0)


def attend(query, pairs, seen, row_count):
    tokens, width = query.shape
    frames = tokens // row_count
    count = len(pairs)

    def body(*refs):
        query_ref, pair_refs, out_ref = refs[0], refs[1 : 1 + count], refs[-1]
        for r in range(row_count):
            span = slice(r * frames, (r + 1) * frames)
            for j in range(0, SPAN, 128):
                lanes = slice(j, j + 128)
                asked = two_heads(query_ref[span, lanes])
                key, value = [pair_rows(pair_refs, p, r, lanes, row_count) for p in range(2)]
                probs = row_probs(asked, key, refs[1 + count][r] if seen is not None else None)
                out_ref[span, lanes] = narrow(one_row(tdot(narrow(probs), value)))

    token_spec = pl.BlockSpec((tokens, SPAN), lambda i: (0, i))
    args = (query, *pairs)
    specs = [token_spec] + [pl.BlockSpec((pairs[0].shape[0], SPAN), lambda i: (0, i))] * count
    if seen is not None:
        args = args + (seen,)
        specs.append(whole(seen))
    return pl.pallas_call(
        body,
        grid=(width // SPAN,),
        out_shape=like((tokens, width), jnp.bfloat16),
        in_specs=specs,
        out_specs=token_spec,
        compiler_params=room(8),
        cost_estimate=hint(),
    )(*args)


def attend_back(query, pairs, seen, grads, tables, row_count, scale):
    tokens, width = query.shape
    frames = tokens // row_count
    count = len(pairs)
    block = pairs[0].shape[0]
    keys = block // (2 * row_count)

    def body(*refs):
        query_ref, grad_ref, pair_refs = refs[0], refs[1], refs[2 : 2 + count]
        rest = refs[2 + count :]
        out_ref = refs[-1]

        def put(part, r, lanes, value):
            for b in range(count):
                start = b * block + (part * row_count + r) * keys
                out_ref[start : start + keys, lanes] = narrow(value[b * keys : (b + 1) * keys])

        for r in range(row_count):
            span = slice(r * frames, (r + 1) * frames)
            for j in range(0, SPAN, 128):
                lanes = slice(j, j + 128)
                asked = two_heads(query_ref[span, lanes])
                grad = two_heads(grad_ref[span, lanes])
                key, value = [pair_rows(pair_refs, p, r, lanes, row_count) for p in range(2)]
                probs = row_probs(asked, key, rest[2][r] if seen is not None else None)
                score_grad = narrow(softmax_back(probs, dot_t(value, grad)))
                result = one_row(tdot(score_grad, key))
                if tables is not None:
                    result = spin(result, rest[0][span, :], rest[1][span, :])
                start = count * block + r * frames
                out_ref[start : start + frames, lanes] = narrow(result * scale)
                put(0, r, lanes, dot(score_grad, asked))
                put(1, r, lanes, dot(narrow(probs), grad))

    token_spec = pl.BlockSpec((tokens, SPAN), lambda i: (0, i))
    specs = [token_spec] * 2 + [pl.BlockSpec((block, SPAN), lambda i: (0, i))] * count
    args = (query, grads, *pairs)
    if tables is not None:
        specs = specs + [whole(table) for table in tables]
        args = args + tuple(tables)
    if seen is not None:
        specs.append(whole(seen))
        args = args + (seen,)
    return pl.pallas_call(
        body,
        grid=(width // SPAN,),
        out_shape=like((count * block + tokens, width), jnp.bfloat16),
        in_specs=specs,
        out_specs=pl.BlockSpec((count * block + tokens, SPAN), lambda i: (0, i)),
        compiler_params=room(12),
        cost_estimate=hint(),
    )(*args)


def multiply(left, right):
    rows, depth = left.shape
    width = right.shape[1]
    block = LANES if width % LANES == 0 else 384 if width % 384 == 0 else width

    def body(left_ref, right_ref, out_ref):
        out_ref[...] = narrow(dot(left_ref[...], right_ref[...]))

    return pl.pallas_call(
        body,
        grid=(width // block,),
        out_shape=like((rows, width), jnp.bfloat16),
        in_specs=[whole(left), pl.BlockSpec((depth, block), lambda i: (0, i))],
        out_specs=pl.BlockSpec((rows, block), lambda i: (0, i)),
        compiler_params=room(12),
        cost_estimate=hint(),
    )(left, right)


def weight_sums(lefts, rights, beside=None):
    rows = lefts[0].shape[1] // 2
    widths = [right.shape[1] for right in rights]
    count = len(lefts)
    if rows % 128:
        sums = [narrow(tdot(left, right)) for left, right in zip(lefts, rights)]
        sums = jnp.concatenate(sums + ([] if beside is None else [beside]), 1)
        return sums[:rows], sums[rows:]
    total = sum(widths) + (0 if beside is None else beside.shape[1])

    def body(*refs):
        for half in range(2):

            @pl.when(pl.program_id(0) == half)
            def _():
                start = 0
                for left, right, width in zip(refs[:count], refs[count : 2 * count], widths):
                    lanes = slice(start, start + width)
                    refs[half - 2][:, lanes] = narrow(tdot(left[...], right[...]))
                    start = start + width
                if beside is not None:
                    refs[half - 2][:, start:] = refs[2 * count][...]

    specs = [pl.BlockSpec((left.shape[0], rows), lambda i: (0, i)) for left in lefts]
    specs = specs + [whole(right) for right in rights]
    args = (*lefts, *rights)
    if beside is not None:
        args = args + (beside,)
        specs.append(pl.BlockSpec((rows, beside.shape[1]), lambda i: (i, 0)))
    out = pl.BlockSpec((rows, total), lambda i: (0, 0))
    return pl.pallas_call(
        body,
        grid=(2,),
        out_shape=[like((rows, total), jnp.bfloat16)] * 2,
        in_specs=specs,
        out_specs=[out, out],
        compiler_params=room(20),
        cost_estimate=hint(),
    )(*args)


def order_matrix(size, rows, order, me):
    masks = jnp.asarray(np.array(masks_of(order), np.int32))
    source = ((me ^ masks)[:, None] * rows + jnp.arange(rows, dtype=jnp.int32)[None, :]).reshape(-1)
    return (jnp.arange(size, dtype=jnp.int32)[:, None] == source[None, :]).astype(jnp.bfloat16)


def local(
    frames,
    prompt,
    clip_frames,
    upstream,
    first_gain,
    first_shift,
    self_project,
    self_output,
    second_gain,
    second_shift,
    cross_query,
    cross_memory,
    cross_output,
    third_gain,
    third_shift,
    feed_input,
    feed_lift,
    feed_output,
    feed_offset,
):
    row_count, frame_count, width = frames.shape
    heads = width // HEAD_DIM
    token_count = row_count * frame_count
    scale = HEAD_DIM ** (-0.5)
    batch_count = lax.axis_size(B)
    seq_count = lax.axis_size(S)
    device_count = batch_count * seq_count
    seq_place = lax.axis_index(S)
    me = lax.axis_index(B) * seq_count + seq_place
    share = first_gain.shape[0]

    seq_masks = [1 << i for i in range(seq_count.bit_length() - 1)]
    batch_masks = [seq_count << i for i in range(batch_count.bit_length() - 1)]
    near = batch_masks[:3]
    far = batch_masks[3:]
    x_mask, y_mask = batch_masks[:2]
    places = [(0, 3, 1, 2), (3, 1, 2, 0), (3, 2, 0, 1)]
    if len(batch_masks) != 4:
        places = [[(i + j) % len(batch_masks) for i in range(len(batch_masks))] for j in range(3)]
    tail_orders = [[batch_masks[i] for i in place] for place in places]
    near_orders = [near[j:] + near[:j] for j in range(3)]
    near_count = len(masks_of(near))
    third = (token_count * 3 // 8) // 16 * 16
    cuts = [0, third, 2 * third, token_count]
    units = feed_output.shape[0]

    vectors = [first_gain, first_shift, second_gain, second_shift, third_gain, third_shift, feed_offset]
    vectors = jnp.transpose(jnp.pad(jnp.stack(vectors, 0), ((0, 128 - len(vectors)), (0, 0))))
    split = 3 * width // 2
    group_one = narrow(jnp.concatenate([vectors, self_project], 1))
    memory_rows = ((0, share // 2 - cross_memory.shape[0]), (0, 0))
    memory_rows = jnp.concatenate(
        [
            jnp.pad(cross_memory[:, :width], memory_rows),
            jnp.pad(cross_memory[:, width:], memory_rows),
        ],
        0,
    )
    group_two = narrow(jnp.concatenate([self_output, cross_query, cross_output, memory_rows], 1))
    lift_rows = jnp.pad(feed_lift, ((0, 14), (0, width - units)))
    feed_sent = narrow(
        jnp.concatenate([feed_input.reshape(2 * units, width), feed_output, lift_rows], 0)
    )
    own_places = seq_place * frame_count + jnp.arange(frame_count, dtype=jnp.int32)
    key_order = masks_of(seq_masks)
    key_places = jnp.concatenate(
        [(seq_place ^ k) * frame_count + jnp.arange(frame_count, dtype=jnp.int32) for k in key_order]
    )
    own_clip, own_offset = clip_tables(clip_frames, own_places)
    key_clip = clip_tables(clip_frames, key_places)[0]
    seen = widen(own_clip[:, None, :] == key_clip[:, :, None])
    prompt_flat = prompt.reshape(-1, prompt.shape[2])
    rows = cross_memory.shape[0]
    place = jnp.arange(prompt.shape[2], dtype=jnp.int32)
    place = place // rows * share + place % rows
    places = jnp.arange(width, dtype=jnp.int32)[None, :]
    prompt_spread = [
        narrow(dot(prompt_flat, (place[:, None] + j * (share // 2) == places).astype(jnp.bfloat16)))
        for j in range(2)
    ]
    prompt_spread = jnp.concatenate(prompt_spread, 0)
    turn_tables = spin_tables(own_offset, 1.0)
    back_tables = spin_tables(own_offset, -1.0)

    def turn_rows(rows, matrix):
        return narrow(dot(rows, matrix))

    turned_memory = turn_rows(
        prompt_flat, order_matrix(prompt.shape[2], cross_memory.shape[0], tail_orders[2], me)
    )
    turned_memory = jnp.concatenate([turned_memory] * seq_count, 0)
    matrices = [order_matrix(width, share, order, me) for order in tail_orders]
    upstream_tokens = upstream.reshape(token_count, width)
    grad_drop_bias = jnp.sum(widen(upstream_tokens), 0, keepdims=True)
    early = [prompt_spread, turned_memory, seen, grad_drop_bias]
    early = early + matrices + list(turn_tables) + list(back_tables)

    known = [0]
    for mask in batch_masks[:1:-1]:
        group_one = jnp.concatenate([group_one, hop(group_one, mask)], 0)
        known = known + [old ^ mask for old in known]
    known = [known + [old ^ mask for old in known] for mask in (x_mask, y_mask)]
    group_one, group_two, *early = lax.optimization_barrier((group_one, group_two, *early))
    prompt_spread, turned_memory, seen, grad_drop_bias = early[:4]
    matrices, turn_tables, back_tables = early[4:7], early[7:9], early[9:]

    def pieces_of(columns, others):
        halves = []
        for h in range(2):
            have = known[h]
            pieces = [(columns[h], have), (others[h], [old ^ (y_mask, x_mask)[h] for old in have])]
            halves.append(pieces)
        return halves

    def add_core(halves, got):
        for h in range(2):
            halves[h] = halves[h] + [
                (piece, [old ^ seq_masks[0] for old in have])
                for piece, (_, have) in zip(got[h], halves[h])
            ]
            for mask in seq_masks[1:]:
                halves[h] = halves[h] + [
                    (hop(piece, mask), [old ^ mask for old in have]) for piece, have in halves[h]
                ]
        return halves

    core = seq_masks[0]
    traffic = Traffic()
    feed_parts = [feed_sent[2 * units :], feed_sent[: 2 * units]]
    ones = (group_one[:, : 128 + split], group_one[:, 128 + split :])
    group_two = gather(group_two, batch_masks[:2:-1])
    got = volley(ones, [x_mask, y_mask])
    ones = tuple(jnp.concatenate(pair, 0) for pair in zip(ones, got))
    got = volley(
        ones + (feed_parts[0], group_two, ones[0]),
        [y_mask, x_mask, far[0], batch_masks[2], core],
    )
    feed_got = [got[2]]
    group_two = jnp.concatenate([group_two, got[3]], 0)
    twos = (group_two[:, : 2 * width], group_two[:, 2 * width :])
    got_one = got[:2] + got[4:]
    got = volley(
        twos + (ones[1],) + got_one[:2], [x_mask, y_mask, core, core, core]
    )
    got_one = got_one + got[2:]
    twos = tuple(jnp.concatenate(pair, 0) for pair in zip(twos, got))
    halves = pieces_of(ones, got_one[:2])
    halves = add_core(halves, ((got_one[2], got_one[4]), (got_one[3], got_one[5])))
    new = {
        "two": once(twos + twos[:1], [y_mask, x_mask, core]),
        "feed": once(feed_parts[1:], far[:1]),
    }
    pieces = traffic.turn([piece for have in halves for piece, _ in have], lambda done: new)
    count = len(pieces) // 2
    halves = [
        [(piece, have) for piece, (_, have) in zip(pieces[h * count : (h + 1) * count], halves[h])]
        for h in range(2)
    ]
    packed, triple_low = settle(
        halves, [[(0, 0, 0, 128), (128, 1, 0, split)], [(0, 1, split, split)]], [128, 3 * width], me
    )
    packed = dot_t(jnp.eye(8, 128, dtype=jnp.bfloat16), packed)
    gain_one, shift_one, gain_two, shift_two, gain_three, shift_three, drop_bias = [
        packed[j : j + 1] for j in range(7)
    ]

    def cut_tokens(value):
        return [value[cuts[p] : cuts[p + 1]] for p in range(3)]

    def token_pairs(kept, got):
        pairs = []
        for p in range(3):
            first, last = near_count * cuts[p], near_count * cuts[p + 1]
            middle = (first + last) // 2
            pairs.append(
                [
                    narrow(widen(kept[rows]) + widen(got[rows]))
                    for rows in (slice(first, middle), slice(middle, last))
                ]
            )
        return pairs

    inputs = frames.reshape(token_count, width)
    query, pairs, normed_one, inverse_one, hidden_one = project(
        inputs, gain_one, shift_one, triple_low, turn_tables, scale
    )
    query, normed_one = traffic.turn(
        (query, normed_one),
        lambda done: {"pairs": double_list(pairs, seq_masks)},
        step=[],
    )
    for _ in seq_masks:
        (query,) = traffic.turn((query,), step=["pairs"])
    pairs = traffic.done["pairs"]
    self_mixed = attend(query, pairs, seen, row_count)

    def started(done):
        return {
            "last": once((twos[1],) + done["two"][:2], [core] * 3),
            "up": double_each(cut_tokens(upstream_tokens), near_orders),
        }

    self_mixed, *feed_all = traffic.turn([self_mixed] + feed_parts + feed_got, started)
    got_two = traffic.done["two"]
    feed_all.append(traffic.done["feed"][0])
    far_count = len(masks_of(far))
    unit_count = far_count * units
    drop_low, value_low, gate_low = [
        jnp.concatenate([part[rows : rows + units] for part in feed_all[p::2]], 0)
        for p, rows in ((0, 0), (1, 0), (1, units))
    ]
    biases = [part[units : units + 2, :units] for part in feed_all[::2]]
    biases = jnp.concatenate(biases, 1)
    for mask in far[1:]:
        drop_low, value_low, gate_low = [
            jnp.concatenate([low, hop(low, mask)], 0) for low in (drop_low, value_low, gate_low)
        ]
        biases = jnp.concatenate([biases, hop(biases, mask)], 1)
    value_bias, gate_bias = widen(biases[:1]), widen(biases[1:])
    self_mixed, value_low, gate_low, drop_low, value_bias, gate_bias = traffic.turn(
        (self_mixed, value_low, gate_low, drop_low, value_bias, gate_bias),
        lambda done: {"mixed": double_list(self_mixed, seq_masks)},
    )
    got = traffic.done["last"]
    halves = add_core(
        pieces_of(twos, got_two[:2]), ((got_two[2], got[1]), (got[0], got[2]))
    )
    lows = settle(
        halves,
        [[(0, 0, 0, width), (width, 1, 0, width)], [(0, 2, 0, width), (width, 3, 0, width)]],
        [width] * 4,
        me,
    )
    self_low, ask_low, cross_low, memory_low, self_mixed = traffic.turn(
        (*lows, self_mixed), lambda done: {"hidden": double_list(hidden_one, seq_masks)}
    )
    after_self, normed_two, inverse_two, hidden_two, asking = ahead(
        self_mixed, self_low, inputs, gain_two, shift_two, ask_low, scale
    )
    asking, prompt_spread = lax.optimization_barrier((asking, prompt_spread))
    memory = multiply(prompt_spread, memory_low)
    cross_mixed = attend(asking, [memory], None, row_count)
    (cross_mixed,) = traffic.turn(
        (cross_mixed,), lambda done: {"asked": double_list(hidden_two, seq_masks)}
    )
    after_cross, normed_three, inverse_three, hidden_three = ahead(
        cross_mixed, cross_low, after_self, gain_three, shift_three
    )

    hidden_three, cross_mixed = traffic.turn(
        (hidden_three, cross_mixed),
        lambda done: {
            "rows": double_each(cut_tokens(hidden_three), near_orders),
            "crossed": double_list(cross_mixed, seq_masks),
        },
        step=["asked"],
    )
    traffic.turn((), step=["rows", "crossed"])
    up = jnp.concatenate(traffic.done["up"], 0)
    traffic.turn((), lambda done: {"ups": double_list(up, seq_masks)}, step=["rows"])
    for _ in seq_masks[1:]:
        traffic.turn((), step=["asked", "crossed", "hidden", "mixed", "ups"])
    hidden_all, mixed_all, asked_all, cross_all = [
        jnp.concatenate(traffic.done[name], 0) for name in ("hidden", "mixed", "asked", "crossed")
    ]
    def rows_there(done):
        if "rows" not in done:
            return {}
        done["rows"] = jnp.concatenate(done["rows"], 0)
        return {"all": double_list(done["rows"], seq_masks)}

    hidden_all, mixed_all, asked_all, cross_all = traffic.turn(
        (hidden_all, mixed_all, asked_all, cross_all), rows_there
    )
    while "rows" in traffic.flows:
        traffic.turn((), rows_there)
    ups = traffic.done["ups"]
    lows = (value_low, gate_low, drop_low, value_bias, gate_bias)
    results = [feed_block(traffic.done["rows"], ups[0], *lows)]
    results[0] = traffic.turn(results[0])
    for _ in seq_masks[1:]:
        traffic.turn((), step=["all"])
    feed_rows = traffic.done["all"]
    for rows, up in zip(feed_rows[1:], ups[1:]):
        results.append(feed_block(rows, up, *lows))
    middles, value_grads, gate_grads, back_sums = [list(item) for item in zip(*results)]

    def back_flow():
        blocks = back_sums
        for mask in reversed(seq_masks):
            half = len(blocks) // 2
            sent = yield tuple(blocks[half:])
            got = yield hops(sent, (mask,) * half)
            if half > 1:
                blocks = [narrow(widen(a) + widen(b)) for a, b in zip(blocks[:half], got)]
        return (yield from halve_pairs(token_pairs(blocks[0], got[0]), near_orders))

    blocks = len(feed_rows)
    tied = traffic.turn(middles + value_grads + gate_grads, lambda done: {"back": back_flow()})
    middles, value_grads, gate_grads = tied[:blocks], tied[blocks : 2 * blocks], tied[2 * blocks :]
    drop_grad = unit_grad(middles, ups, False)[0]
    tied = traffic.turn((drop_grad, hidden_all, *value_grads, *gate_grads))
    for _ in seq_masks[1:]:
        tied = traffic.turn(tied)
    drop_grad, hidden_all, tied = tied[0], tied[1], tied[2:]
    value_grads, gate_grads = tied[:blocks], tied[blocks:]
    turned_triple = [turn_rows(hidden_all, matrix) for matrix in matrices]
    value_grad, value_bias_grad = unit_grad(value_grads, feed_rows, True)
    gate_grad, gate_bias_grad = unit_grad(gate_grads, feed_rows, True)

    def unit_blocks(grad):
        return [grad[k * units : (k + 1) * units] for k in range(far_count)]

    bias_grads = [
        narrow(
            jnp.pad(
                jnp.concatenate(
                    [bias[:, k * units : (k + 1) * units] for bias in (value_bias_grad, gate_bias_grad)], 0
                ),
                ((0, 14), (0, width - units)),
            )
        )
        for k in range(far_count)
    ]

    def unit_flow(p):
        blocks = unit_blocks((drop_grad, drop_grad, value_grad, value_grad, gate_grad)[p])
        if p == 4:
            blocks = [jnp.concatenate(pair, 0) for pair in zip(blocks, bias_grads)]
            return halve_rows(blocks, 0, units + 16, far)
        half = units // 2
        return halve_rows(blocks, p % 2 * half, (p % 2 + 1) * half, far)

    value_grad, gate_grad, drop_grad, mixed_all, *turned_triple = traffic.turn(
        [value_grad, gate_grad, drop_grad, mixed_all] + turned_triple,
        lambda done: {"unit0": unit_flow(0)},
    )
    turned_self = [turn_rows(mixed_all, matrix) for matrix in matrices]

    term_sums = [multiply(middle, drop_low) for middle in middles]

    def term_flow():
        blocks = term_sums
        for mask in reversed(seq_masks):
            half = len(blocks) // 2
            sent = yield tuple(blocks[half:])
            got = yield hops(sent, (mask,) * half)
            if half > 1:
                blocks = [narrow(widen(a) + widen(b)) for a, b in zip(blocks[:half], got)]
        return blocks[0], got[0]

    cross_all, asked_all, *turned_self = traffic.turn(
        [cross_all, asked_all] + turned_self, lambda done: {"term": term_flow()}
    )
    turned_cross = turn_rows(cross_all, matrices[0])
    turned_ask = turn_rows(asked_all, matrices[1])
    for _ in seq_masks[1:]:
        traffic.turn((), step=["term"])
    while "back" in traffic.flows:
        turned_cross, turned_ask = traffic.turn((turned_cross, turned_ask), step=["back", "term"])

    while "back" in traffic.flows:
        unit_sums = list(traffic.turn(unit_sums, step=["back", "term"]))
    feed_back = jnp.concatenate(traffic.done["back"], 0)
    (feed_back,) = traffic.turn(
        (feed_back,),
        lambda done: {
            "term_near": halve_pairs(token_pairs(*done["term"]), near_orders),
        },
    )
    cross_out_grad, grad_gain_three, grad_shift_three, cross_branch, cross_mixed_grad = back(
        feed_back, None, upstream_tokens, normed_three, inverse_three, gain_three, cross_low
    )

    def weight_pair(turned, *grads):
        half = turned.shape[1] // 2
        pair = []
        for columns in (turned[:, :half], turned[:, half:]):
            sums = [narrow(tdot(columns, grad)) for grad in grads]
            if len(grads) > 1:
                rows = cross_memory.shape[0]
                sums = [
                    jnp.pad(part.reshape(-1, rows, width), ((0, 0), (0, share // 2 - rows), (0, 0)))
                    for part in sums
                ]
                sums = [jnp.concatenate(sums, 1).reshape(-1, width)]
            pair.append(sums[0])
        return tuple(pair)

    (cross_mixed_grad,) = traffic.turn(
        (cross_mixed_grad,),
        lambda done: {"dc": double_list(cross_branch, seq_masks), "unit1": unit_flow(1)},
    )
    asked_grad = attend_back(
        asking, [memory], None, cross_mixed_grad, None, row_count, scale
    )
    (asked_grad,) = traffic.turn(
        (asked_grad,),
        lambda done: {"dq": double_list(asked_grad, seq_masks), "unit2": unit_flow(2)},
    )
    for _ in seq_masks[1:]:
        traffic.turn((), step=["dc"])
    self_out_grad, grad_gain_two, grad_shift_two, self_branch, self_mixed_grad = back(
        asked_grad,
        ask_low,
        cross_out_grad,
        normed_two,
        inverse_two,
        gain_two,
        self_low,
        memory.shape[0] // token_count,
    )
    (self_mixed_grad,) = traffic.turn(
        (self_mixed_grad,),
        lambda done: {"da": double_list(self_branch, seq_masks)},
    )
    for _ in seq_masks[1:]:
        traffic.turn((), step=["dq", "da"])
    cross_pair = weight_pair(turned_cross, jnp.concatenate(traffic.done["dc"], 0))
    layer_output = narrow(
        after_cross + jnp.concatenate(traffic.done["term_near"], 0) + drop_bias
    )
    memory_all = traffic.done["dq"]
    half = memory.shape[0] // 2
    ask_pair = weight_pair(turned_ask, jnp.concatenate([part[2 * half :] for part in memory_all], 0))
    memory_pair = weight_pair(
        turned_memory,
        jnp.concatenate([part[:half] for part in memory_all], 0),
        jnp.concatenate([part[half : 2 * half] for part in memory_all], 0),
    )
    self_mixed_grad, layer_output = traffic.turn(
        (self_mixed_grad, layer_output),
        lambda done: {
            "first": halve_pairs([cross_pair, ask_pair, memory_pair], tail_orders),
        },
    )
    pair_grad = attend_back(
        query, pairs, seen, self_mixed_grad, back_tables, row_count, scale
    )

    def shed_frames(value):
        query_grad = value[-token_count:]
        count = value.shape[0] - token_count
        for mask in reversed(seq_masks):
            half = count // 2
            (sent,) = yield (value[half:count],)
            (got,) = yield hops((sent,), (mask,))
            if mask > seq_masks[0]:
                value = narrow(widen(value[:half]) + widen(got))
                count = half
        if len(seq_masks) > 1:
            value = jnp.concatenate([value, query_grad], 0)
        return value, got

    (pair_grad,) = traffic.turn((pair_grad,), lambda done: {"pair": shed_frames(pair_grad)}, step=[])
    for _ in seq_masks:
        traffic.turn((), step=["pair"])
    triple_back = spin_backward(*traffic.done["pair"], *back_tables)
    (triple_back,) = traffic.turn(
        (triple_back,),
        lambda done: {"dt": double_list(triple_back, seq_masks), "unit3": unit_flow(3)},
    )
    frame_grad, grad_gain_one, grad_shift_one = back(
        triple_back, triple_low, self_out_grad, normed_one, inverse_one, gain_one
    )
    branch_all = jnp.concatenate(traffic.done["da"], 0)
    shares = [0, width // 6, width // 3, width]
    sums = [
        grad_gain_one,
        grad_shift_one,
        grad_gain_two,
        grad_shift_two,
        grad_gain_three,
        grad_shift_three,
        grad_drop_bias,
    ]
    sums = jnp.pad(jnp.concatenate(sums, 0), ((0, 1), (0, 0)))
    frame_grad, sums = traffic.turn((frame_grad, sums), lambda done: {"sums": double_list(sums, seq_masks)})
    for _ in seq_masks:
        traffic.turn((), step=["dt", "sums"])
    triple_all = jnp.concatenate(traffic.done["dt"], 0)
    sums = sum(traffic.done["sums"])
    sums_turned = tdot(matrices[1], narrow(jnp.transpose(sums)))
    sums_turned = narrow(jnp.pad(sums_turned, ((0, 0), (0, 120))))

    def triple_pair(p, beside=None):
        grads = [
            triple_all[:, p * width : (p + 1) * width],
            branch_all[:, shares[p] : shares[p + 1]],
        ]
        return list(weight_sums([turned_triple[p], turned_self[p]], grads, beside))

    triple_pairs = [triple_pair(0), None, triple_pair(2)]
    while traffic.count["first"] < len(batch_masks) - 1:
        traffic.turn(())

    def tail_first(*which):
        return once([triple_pairs[p][1] for p in which], [tail_orders[p][-1] for p in which])

    (sums_turned,) = traffic.turn((sums_turned,), lambda done: {"early": tail_first(0, 2)})
    triple_pairs[1] = triple_pair(1, sums_turned)
    (triple_pairs[1][1],) = traffic.turn(
        (triple_pairs[1][1],),
        lambda done: {"unit4": unit_flow(4)},
        step=["first"],
    )
    traffic.turn((), lambda done: {"late": tail_first(1)}, step=[])

    def tail_rest(done):
        got = (done["early"][0], done["late"][0], done["early"][1])
        pairs = []
        for (kept, _), part in zip(triple_pairs, got):
            half = kept.shape[0] // 2
            pairs.append(
                [
                    narrow(widen(kept[rows]) + widen(part[rows]))
                    for rows in (slice(half), slice(half, None))
                ]
            )
        orders = [order[:-1] for order in tail_orders]
        return {"tail": halve_pairs(pairs, orders)}

    traffic.turn((), tail_rest)
    while traffic.flows:
        traffic.turn(())
    parts = traffic.done["tail"]
    grad_cross, grad_ask, grad_memory = traffic.done["first"]
    grad_self = jnp.concatenate(
        [part[:, width : width + shares[p + 1] - shares[p]] for p, part in enumerate(parts)], 1
    )
    drop_sums = jnp.concatenate([traffic.done[name] for name in UNITS[:2]], 0)
    value_sums = jnp.concatenate([traffic.done[name] for name in UNITS[2:4]], 0)
    gate_sums = traffic.done[UNITS[4]]
    grad_triple = jnp.concatenate([part[:, :width] for part in parts], 1)
    sums = width + shares[2] - shares[1]
    sums = jnp.transpose(parts[1][:, sums : sums + 7])
    grad_memory = grad_memory.reshape(2, share // 2, width)[:, : cross_memory.shape[0]]
    grad_memory = jnp.concatenate([grad_memory[0], grad_memory[1]], 1)
    grad_lift = jnp.stack([value_sums, gate_sums[:units]], 0)
    grad_drop = drop_sums
    grad_lift_bias = gate_sums[units : units + 2, :units]
    shape = frames.shape
    return (
        layer_output.reshape(shape),
        frame_grad.reshape(shape),
        sums[0],
        sums[1],
        grad_triple,
        grad_self,
        sums[2],
        sums[3],
        grad_ask,
        grad_memory,
        grad_cross,
        sums[4],
        sums[5],
        grad_lift,
        grad_lift_bias,
        grad_drop,
        sums[6],
    )


def solution(mesh):
    both = P(AX)
    wide = P(AX, None)
    rows = P(B, S, None)
    units = P(None, AX, None)
    in_specs = (
        rows,
        P(B, None, None),
        P(B, None),
        rows,
        both,
        both,
        wide,
        wide,
        both,
        both,
        wide,
        wide,
        wide,
        both,
        both,
        units,
        P(None, AX),
        wide,
        both,
    )
    out_specs = (
        rows,
        rows,
        both,
        both,
        wide,
        wide,
        both,
        both,
        wide,
        wide,
        wide,
        both,
        both,
        units,
        P(None, AX),
        wide,
        both,
    )
    return jax.shard_map(local, mesh=mesh, in_specs=in_specs, out_specs=out_specs, check_vma=False)
```
